128 devices in a mesh: dp: 16 (over z, x_lo, core), fsdp: 8 (over y, x_hi).
Axes of the slice: x: 4 (x_hi: 2, x_lo: 2; x = x_hi * 2 + x_lo), y: 4, z: 4, core: 2. Of those that a mesh axis runs over, the one named last changes fastest.
Arguments:
- states_in: bfloat16 [16, 1024, 768], P('dp', 'fsdp'), may hold values from -6 to 6
- attn_weight: bfloat16 [2, 768, 2304], P(None, 'dp', 'fsdp'), may hold values from -0.21875 to 0.21875
- out_weight: bfloat16 [2, 768, 768], P(None, 'dp', 'fsdp'), may hold values from -0.875 to 0.875
- fc_weight: bfloat16 [2, 768, 3072], P(None, 'dp', 'fsdp'), may hold values from -0.21875 to 0.21875
- proj_weight: bfloat16 [2, 3072, 768], P(None, 'dp', 'fsdp'), may hold values from -0.109375 to 0.109375
- norm_gain: float32 [2, 2, 768], replicated, may hold values from 0.1 to 1.9
- norm_shift: float32 [2, 2, 768], replicated, may hold values from -1 to 1
- prefix_table: float32 [10, 768], replicated, may hold values from -6 to 6
- reparam_in: float32 [768, 512], replicated, may hold values from -0.21875 to 0.21875
- reparam_in_bias: float32 [512], replicated, may hold values from -3 to 3
- reparam_out: float32 [512, 3072], replicated, may hold values from -1 to 1
- reparam_out_bias: float32 [3072], replicated, may hold values from -3 to 3
- doc_lengths: int32 [16, 8], P('dp'), may hold values from 1 to 1017, as said below
- pad_counts: int32 [16], P('dp'), may hold values from 0 to 63
- states_grad: bfloat16 [16, 1024, 768], P('dp', 'fsdp'), may hold values from -6 to 6
Outputs:
- final_states: float32 [16, 1024, 768], P('dp', 'fsdp')
- grad_states: float32 [16, 1024, 768], P('dp', 'fsdp')
- grad_table: float32 [10, 768], replicated
- grad_reparam_in: float32 [768, 512], replicated
- grad_reparam_in_bias: float32 [512], replicated
- grad_reparam_out: float32 [512, 3072], replicated
- grad_reparam_out_bias: float32 [3072], replicated
The draws below stay inside these ranges and needn't reach their ends.
Inputs may be any that keep to these rules, and one draw needn't show every extreme that they name: `doc_lengths`: the lengths of a sequence sum to 1024 minus its padding count.
All inputs are finite; a program needn't handle non-finite values.
Results may differ from the reference program's by a relative error of at most 0.02.
The reference program's roundings to bfloat16 on the way count: a program that leaves them out, or rounds other values in their place, can miss the bound.
Values may be sent and summed in bfloat16 or wider, within the bound.
No kernel may reach another device: no remote copies, remote signals or barrier semaphores. Data moves between devices by JAX's collectives and lax.ppermute only.
A program may use at most 192 MiB of HBM per device.

```python
from functools import partial
import jax
import jax.numpy as jnp
from jax import lax

D = 768
H = 12
HD = 64
FF = 3072
LENGTH = 1024
PREFIX = 10
RHID = 512
LAYERS = 2
MAXSEG = 8
TOK_DEV = 128
SEQS = 16


def pack_layout(key):
    base = jax.random.fold_in(key, 101)
    key_list = jax.random.split(base, 4)
    most_pad = TOK_DEV // 2 - 1
    padding = jax.random.randint(key_list[0], (SEQS,), 0, most_pad + 1)
    chosen = jax.random.randint(key_list[1], (), 0, SEQS)
    order = jnp.arange(SEQS)
    padding = jnp.where(order == chosen, most_pad, padding)
    unpadded = order == (chosen + 1) % SEQS
    padding = jnp.where(unpadded, 0, padding)
    short_most = TOK_DEV // (2 * MAXSEG)
    shorts = jax.random.randint(key_list[2], (SEQS, MAXSEG), 1, short_most + 1)
    shorts = jnp.where(unpadded[:, None], 1, shorts)
    longest = jax.random.randint(key_list[3], (SEQS,), 0, MAXSEG)
    slots = jnp.arange(MAXSEG)
    is_long = slots[None, :] == longest[:, None]
    short_total = jnp.sum(jnp.where(is_long, 0, shorts), axis=1)
    long_length = LENGTH - padding - short_total
    lengths = jnp.where(is_long, long_length[:, None], shorts)
    return (lengths.astype(jnp.int32), padding.astype(jnp.int32))


def draw_doc_lengths(key, part):
    return pack_layout(key)[0]


def draw_pad_counts(key, part):
    return pack_layout(key)[1]


def shard_levels(own_key, extent, shards, least, largest):
    def one(dim, blocks):
        steps = jax.random.uniform(jax.random.fold_in(jax.random.fold_in(own_key, 6), dim), (blocks,), jnp.float32, least / len(shards), largest / len(shards))
        return jnp.repeat(jnp.exp(steps), extent[dim] // blocks).reshape((-1,) + (1,) * (len(extent) - dim - 1))

    level = one(*shards[0])
    for cut in shards[1:]:
        level = level * one(*cut)
    return level


def noise(stream_key, shape, scale, bound, cuts=(), kind=jnp.bfloat16):
    entries = jax.random.normal(stream_key, shape, jnp.float32) * scale
    if len(cuts) > 0:
        entries = shard_levels(stream_key, shape, cuts, -0.22, 0.18) * entries
    return jnp.clip(entries, min=-bound, max=bound).astype(kind)


def setup_inputs(seed: int = 0) -> dict:
    keys = jax.random.split(jax.random.key(seed), 16)
    states_in = noise(keys[0], (SEQS, LENGTH, D), 1.0, 6.0, ((0, 16), (1, 8)))
    attn_weight = noise(keys[1], (LAYERS, D, 3 * D), D ** -0.5, 0.21875, ((1, 16), (2, 8)))
    out_weight = noise(keys[2], (LAYERS, D, D), (D // 16) ** -0.5, 0.875, ((1, 16), (2, 8)))
    fc_weight = noise(keys[3], (LAYERS, D, FF), D ** -0.5, 0.21875, ((1, 16), (2, 8)))
    proj_weight = noise(keys[4], (LAYERS, FF, D), FF ** -0.5, 0.109375, ((1, 16), (2, 8)))
    norm_gain = jnp.clip(1.0 + 0.18 * jax.random.normal(keys[5], (LAYERS, 2, D), jnp.float32), 0.1, 1.9)
    norm_shift = noise(keys[6], (LAYERS, 2, D), 0.2, 1.0, (), jnp.float32)
    prefix_table = noise(keys[7], (PREFIX, D), 1.0, 6.0, (), jnp.float32)
    reparam_in = noise(keys[8], (D, RHID), D ** -0.5, 0.21875, (), jnp.float32)
    reparam_in_bias = noise(keys[9], (RHID,), 0.5, 3.0, (), jnp.float32)
    reparam_out = noise(keys[10], (RHID, 2 * LAYERS * D), (RHID // 16) ** -0.5, 1.0, (), jnp.float32)
    reparam_out_bias = noise(keys[11], (2 * LAYERS * D,), 0.5, 3.0, (), jnp.float32)
    doc_lengths = draw_doc_lengths(jax.random.fold_in(keys[15], 71), 0)
    pad_counts = draw_pad_counts(jax.random.fold_in(keys[15], 71), 0)
    states_grad = noise(keys[14], (SEQS, LENGTH, D), 1.0, 6.0, ((0, 16), (1, 8)))
    return dict(states_in=states_in, attn_weight=attn_weight, out_weight=out_weight, fc_weight=fc_weight, proj_weight=proj_weight, norm_gain=norm_gain, norm_shift=norm_shift, prefix_table=prefix_table, reparam_in=reparam_in, reparam_in_bias=reparam_in_bias, reparam_out=reparam_out, reparam_out_bias=reparam_out_bias, doc_lengths=doc_lengths, pad_counts=pad_counts, states_grad=states_grad)


@jax.custom_vjp
def low(v):
    return lax.optimization_barrier(v.astype(jnp.bfloat16)).astype(jnp.float32)

@jax.custom_vjp
def low_back(v):
    return v

def low_keep(v):
    return (low(v), None)

def low_pass(kept, grad):
    return (grad,)

def back_keep(v):
    return (v, None)

def back_low(kept, grad):
    return (low(grad),)
low.defvjp(low_keep, low_pass)
low_back.defvjp(back_keep, back_low)
epsilon = 1e-05
highest = lax.Precision.HIGHEST
big_negative = -1e+30

def layer_norm(stream, gain, shift):
    centre = lax.optimization_barrier(jnp.mean(stream, axis=-1, keepdims=True))
    centred = stream - centre
    spread = lax.optimization_barrier(jnp.mean(centred * centred, axis=-1, keepdims=True))
    return centred * lax.rsqrt(spread + epsilon) * gain + shift

def reparam_forward(prefix_table, reparam_in, reparam_in_bias, reparam_out, reparam_out_bias):
    hidden = jnp.tanh(jnp.dot(prefix_table, reparam_in, precision=highest) + reparam_in_bias)
    return jnp.dot(hidden, reparam_out, precision=highest) + reparam_out_bias

def attend_block(query_block, start, key_rows, values, segment, living):
    block_size = query_block.shape[0]
    row_places = start + jnp.arange(block_size, dtype=jnp.int32)
    col_places = jnp.arange(segment.shape[0], dtype=jnp.int32)
    row_segment = lax.dynamic_slice_in_dim(segment, start, block_size)
    row_living = lax.dynamic_slice_in_dim(living, start, block_size)
    visible = (col_places[None, :] <= row_places[:, None]) & (segment[None, :] == row_segment[:, None])
    visible = visible & living[None, :] & row_living[:, None]
    prefix_open = jnp.zeros((block_size, PREFIX), jnp.int32) == 0
    allowed = jnp.concatenate([prefix_open, visible], axis=1)
    scores = jnp.einsum('qhd,khd->hqk', query_block, key_rows, precision=highest) * HD ** (-0.5)
    scores = low_back(jnp.where(allowed[None], scores, big_negative))
    attn_probs = low(jax.nn.softmax(scores, axis=-1))
    return jnp.einsum('hqk,khd->qhd', attn_probs, values, precision=highest)

def run_sequence(stream, lengths, padding, frozen, norm_gain, norm_shift, prefix, block_rows):
    attn_weight, out_weight, fc_weight, proj_weight = frozen
    ends = jnp.cumsum(lengths)
    places = jnp.arange(LENGTH, dtype=jnp.int32)
    segment = lax.optimization_barrier(jnp.sum((places[:, None] >= ends[None, :]).astype(jnp.int32), axis=1))
    living = places < LENGTH - padding
    blocks = LENGTH // block_rows
    starts = jnp.arange(blocks, dtype=jnp.int32) * block_rows
    for layer_index in range(LAYERS):
        normed = low(layer_norm(stream, norm_gain[layer_index, 0], norm_shift[layer_index, 0]))
        packed = low(low_back(jnp.dot(normed, attn_weight[layer_index], precision=highest)))
        queries, key_part, value_part = jnp.split(packed, 3, axis=1)
        key_rows = jnp.concatenate([prefix[:, layer_index, 0], key_part.reshape(LENGTH, H, HD)], axis=0)
        values = jnp.concatenate([prefix[:, layer_index, 1], value_part.reshape(LENGTH, H, HD)], axis=0)
        query_blocks = queries.reshape(blocks, block_rows, H, HD)
        block_fn = jax.checkpoint(partial(attend_block, key_rows=key_rows, values=values, segment=segment, living=living))
        mixed = lax.map(lambda block_pair: block_fn(block_pair[0], block_pair[1]), (query_blocks, starts))
        mixed = low(low_back(mixed.reshape(LENGTH, H * HD)))
        stream = stream + low_back(jnp.dot(mixed, out_weight[layer_index], precision=highest))
        normed = low(layer_norm(stream, norm_gain[layer_index, 1], norm_shift[layer_index, 1]))
        before = low_back(jnp.dot(normed, fc_weight[layer_index], precision=highest))
        activated = low(jax.nn.gelu(before, approximate=True))
        stream = stream + low_back(jnp.dot(activated, proj_weight[layer_index], precision=highest))
    return stream

def reference(states_in, attn_weight, out_weight, fc_weight, proj_weight, norm_gain, norm_shift, prefix_table, reparam_in, reparam_in_bias, reparam_out, reparam_out_bias, doc_lengths, pad_counts, states_grad):
    frozen = (attn_weight.astype(jnp.float32), out_weight.astype(jnp.float32), fc_weight.astype(jnp.float32), proj_weight.astype(jnp.float32))
    block_rows = min(512, LENGTH)

    def forward(stream_all, table, in_weight, in_bias, out_matrix, out_bias):
        prefix = low(reparam_forward(table, in_weight, in_bias, out_matrix, out_bias))
        prefix = prefix.reshape(PREFIX, LAYERS, 2, H, HD)

        def run_packed(packed_row):
            return run_sequence(packed_row[0], packed_row[1], packed_row[2], frozen, norm_gain, norm_shift, prefix, block_rows)
        return lax.map(jax.checkpoint(run_packed), (stream_all, doc_lengths, pad_counts))
    stream_all = states_in.astype(jnp.float32)
    final_states, pull_back = jax.vjp(forward, stream_all, prefix_table, reparam_in, reparam_in_bias, reparam_out, reparam_out_bias)
    grad_list = pull_back(states_grad.astype(jnp.float32))
    return (final_states, grad_list[0], grad_list[1], grad_list[2], grad_list[3], grad_list[4], grad_list[5])
```

```python
import jax
import jax.numpy as jnp
from jax import lax
from jax.experimental import pallas as pl
from jax.experimental.pallas import tpu as pltpu
from jax.sharding import Mesh
from jax.sharding import PartitionSpec as P

D = 768
H = 12
HD = 64
FF = 3072
LENGTH = 1024
PREFIX = 10
LAYERS = 2
TOK = 128
PAD = 16
GROUP = 3
ROWS = 32
SIDE = 4
AXES = ("z", "xl", "core", "y", "xh")
GRID = (4, 2, 2, 4, 2)

epsilon = 1e-05
highest = lax.Precision.HIGHEST
big_negative = -1e30
bf16 = jnp.bfloat16
f32 = jnp.float32
VMEM_LIMIT = 56 * 2**20


def index_of(z, x, core, y):
    return (((z * 2 + x % 2) * 2 + core) * 4 + y) * 2 + x // 2


def everywhere():
    return [(z, x, c, y) for z in range(4) for x in range(4) for c in range(2) for y in range(4)]


def ring(axis, ahead):
    pairs = []
    for spot in everywhere():
        source = list(spot)
        source[axis] = (source[axis] + ahead) % 4
        pairs.append((index_of(*source), index_of(*spot)))
    return pairs


def two_rings(axis_zero, axis_one, ahead):
    pairs = []
    for spot in everywhere():
        source = list(spot)
        axis = axis_one if spot[CORE] else axis_zero
        source[axis] = (source[axis] + ahead) % 4
        pairs.append((index_of(*source), index_of(*spot)))
    return pairs


def core_pairs():
    return [(index_of(z, x, 1 - c, y), index_of(z, x, c, y)) for z, x, c, y in everywhere()]


def seat_pairs():
    return [(index_of(z, c * 2 + x % 2, x // 2, y), index_of(z, x, c, y)) for z, x, c, y in everywhere()]


Z, X, CORE, Y = 0, 1, 2, 3


def move(value, pairs):
    return lax.ppermute(value, AXES, pairs)


def around(value, axis):
    return [value] + [move(value, ring(axis, k)) for k in (1, 2, 3)]


def around_two(value, axis_zero, axis_one):
    return [value] + [move(value, two_rings(axis_zero, axis_one, k)) for k in (1, 2, 3)]


def to_places(blocks, axis):
    got = [None, *[move(blocks[k], ring(axis, -k)) for k in (1, 2, 3)]]
    return [blocks[0], got[3], got[2], got[1]]


def wrap(value):
    return lax.rem(value, SIDE)


def params(limit=VMEM_LIMIT):
    return pltpu.CompilerParams(vmem_limit_bytes=limit)


def anywhere(count):
    return [pl.BlockSpec(memory_space=pl.ANY)] * count


def in_vmem(count):
    return [pl.BlockSpec(memory_space=pltpu.VMEM)] * count


SCALARS = pl.BlockSpec(memory_space=pltpu.SMEM)


def shape(*dims, dtype=bf16):
    return jax.ShapeDtypeStruct(dims, dtype)


def lanes(start, size):
    return pl.ds(pl.multiple_of(start, 128), size)


def block_of(layer, dims):
    if layer is None:
        return pl.BlockSpec(dims, lambda i: (0,) * len(dims))
    return pl.BlockSpec((None, *dims[1:]), lambda i: (layer,) + (0,) * (len(dims) - 1))


def assemble(here, blocks, layer, out, put, waits=()):
    def kernel(here, *refs):
        for k in range(4):
            put(here, k, refs[k], refs[-1])

    return pl.pallas_call(
        kernel,
        grid=(1,),
        out_shape=out,
        in_specs=[SCALARS, *[block_of(layer, b.shape) for b in blocks], *anywhere(len(waits))],
        out_specs=pl.BlockSpec(out.shape, lambda i: (0,) * len(out.shape)),
        compiler_params=params(),
        name="assemble",
    )(here, *blocks, *waits)


def pick(here, zero, one):
    return jnp.where(here[CORE] == 0, zero, one)


def put_pair_one(here, k, block, result):
    place = wrap(pick(here, here[X], here[Y]) + k)
    low, high = lax.rem(place, 2), lax.div(place, 2)
    for c in range(2):
        row, col = pick(here, 2 * low + c, 2 * c + high), pick(here, high, low)
        result[:, row, :, lanes(384 * col, 384)] = block[:, c]


def put_pair_two(here, k, block, result):
    place = wrap(pick(here, here[Y], here[Z]) + k)
    for i in range(4):
        result[pick(here, i, place), :, lanes(768 * pick(here, place, i), 768)] = block[i]


def put_proj_one(here, k, block, result):
    result[:, :, lanes(384 * wrap(here[Z] + k), 384)] = block[...]


def put_proj_two(here, k, block, result):
    place = wrap(here[X] + k)
    result[lax.div(place, 2), :, lanes(1536 * lax.rem(place, 2), 1536)] = block[...]


AO_HELD = pltpu.VMEM((4, 4, 48, 3072), bf16)
FC_HELD = pltpu.VMEM((2, 4, 2, 2, 48, 1536), bf16)
PJ_HELD = pltpu.VMEM((4, 2, 2, 48, 3072), bf16)


class Chosen:
    def __init__(self, here, zero, one, target, sem):
        self.here = here
        self.copies = [pltpu.make_async_copy(source, target, sem) for source in (zero, one)]

    def start(self):
        for core in range(2):
            pl.when(self.here[CORE] == core)(self.copies[core].start)

    def wait(self):
        self.copies[0].wait()


def fetch_ao(here, refs, held, sems):
    return [Chosen(here, refs[k], refs[4 + k], held.at[wrap(here[Z] + k)], sems.at[k]) for k in range(4)]


def fetch_fc(here, refs, held, sems):
    copies = []
    for k in range(4):
        there = wrap(here[X] + k)
        for c in range(2):
            target = held.at[lax.div(there, 2), :, lax.rem(there, 2), c]
            cols = slice(1536 * c, 1536 * c + 1536)
            copies.append(Chosen(here, refs[4 + k].at[:, :, cols], refs[k].at[:, :, cols], target, sems.at[2 * k + c]))
    return copies


def fetch_pj(here, refs, held, sems):
    return [
        pltpu.make_async_copy(refs[4 * n + k], held.at[wrap(here[Y] + k), :, core], sems.at[4 * n + k])
        for n, core in enumerate((here[CORE], 1 - here[CORE]))
        for k in range(4)
    ]


def begin(copies):
    for one in copies:
        one.start()


def finish(copies):
    for one in copies:
        one.wait()


def flipped(value):
    return value.astype(f32).T


def norm_stats(stream):
    centre = jnp.mean(stream, axis=0, keepdims=True)
    centred = stream - centre
    spread = jnp.mean(centred * centred, axis=0, keepdims=True)
    return centred, lax.rsqrt(spread + epsilon)


def norm(stream, gain, shift):
    centred, rate = norm_stats(stream)
    return centred * rate * gain + shift


def norm_back(stream, gain, grad):
    centred, rate = norm_stats(stream)
    unit = centred * rate
    scaled = grad * gain
    inner = jnp.mean(scaled * unit, axis=0, keepdims=True)
    return rate * (scaled - jnp.mean(scaled, axis=0, keepdims=True) - unit * inner)


root = 0.7978845608028654


def gate(u):
    return 0.5 * u * (1.0 + jnp.tanh(root * (u + 0.044715 * (u * u * u))))


def gate_slope(u):
    squared = u * u
    t = jnp.tanh(root * (u + 0.044715 * (squared * u)))
    return 0.5 * (1.0 + t) + (0.5 * root) * u * (1.0 - t * t) * (1.0 + (3.0 * 0.044715) * squared)


def column(gains, layer, which, part):
    at = layer * 4 + which * 2 + part
    return gains[:, at : at + 1]


def rows_of_place(place):
    pieces = []
    for t in range(3):
        for u in range(2):
            piece = 8 * t + 2 * place + u
            pieces.append((384 * (piece // 3) + 96 * (piece % 3), t * 192 + u * 96))
    return pieces


def send_qkv(here, stream, gains, layer, held, wide, sends):
    normed = norm(stream, column(gains, layer, 0, 0), column(gains, layer, 0, 1)).T.astype(bf16)

    for j in range(4):
        cols = slice(768 * j, 768 * j + 768)
        packed = jnp.dot(normed, held[:, :, :, cols].reshape(D, 768), preferred_element_type=f32)
        wide[cols, :] = packed.T.astype(bf16)
    for y in range(4):

        @pl.when(here[Y] == y)
        def _():
            for k in range(4):
                for row, at in rows_of_place((y + k) % 4):
                    sends[k][at : at + 96, :] = wide[row : row + 96, :]


def first_kernel(here, x_ref, gains, *refs):
    ao, (stream, *sends), (held, wide, sems) = refs[0:8], refs[8:13], refs[13:]
    copies = fetch_ao(here, ao, held, sems)
    begin(copies)
    stream[...] = flipped(x_ref[...])
    finish(copies)
    send_qkv(here, stream[...], gains, 0, held, wide, sends)


def first(here, x, gains, ao):
    return pl.pallas_call(
        first_kernel,
        out_shape=(shape(D, TOK, dtype=f32), *[shape(576, TOK)] * 4),
        in_specs=[SCALARS, *in_vmem(2), *anywhere(8)],
        out_specs=tuple(in_vmem(5)),
        scratch_shapes=[AO_HELD, pltpu.VMEM((FF, TOK), bf16), pltpu.SemaphoreType.DMA((8,))],
        compiler_params=params(),
        name="first",
    )(here, x, gains, *ao)


def after_attention(here, stream, mixed, gains, layer, ao_held, fc_held, pj_held, waits, joined, act, before, middle, result):
    for y in range(4):

        @pl.when(here[Y] == y)
        def _():
            for k in range(4):
                row = 192 * ((y + k) % 4)
                joined[row : row + 192, :] = mixed[k][...]

    rows = flipped(joined[...]).astype(bf16)
    finish(waits[0])

    weight = jnp.concatenate([ao_held[:, :, :, 384 * j + 256 : 384 * j + 384].reshape(D, 128) for j in range(8)], axis=1)
    part = jnp.dot(rows, weight, preferred_element_type=f32).T
    for j in range(8):
        at = slice(96 * j, 96 * j + 96)
        middle[at, :] = stream[at, :] + part[128 * j + 32 : 128 * j + 128, :]
    normed = norm(middle[...], column(gains, layer, 1, 0), column(gains, layer, 1, 1)).T.astype(bf16)
    finish(waits[1])

    for n in range(4):
        low = 768 * (n % 2)
        weight = fc_held[n // 2, :, :, :, :, low : low + 768].reshape(D, 768)
        inputs = jnp.dot(normed, weight, preferred_element_type=f32)
        before[n] = inputs
        act[768 * n : 768 * n + 768, :] = gate(inputs).T.astype(bf16)
    finish(waits[2])
    for n in range(2):
        at = slice(384 * n, 384 * n + 384)
        weight = pj_held[2 * n : 2 * n + 2].reshape(384, FF)
        result[at, :] = middle[at, :] + jnp.dot(weight, act[...], preferred_element_type=f32)


def middle_kernel(here, stream, gains, *refs):
    mixed, pair, pj, pair_next = refs[0:4], refs[4:12], refs[12:20], refs[20:28]
    middle, before, result, *sends = refs[28:35]
    ao_held, fc_held, pj_held, next_held, joined, act, sems = refs[35:]
    waits = [
        fetch_ao(here, pair, ao_held, sems.at[0]),
        fetch_fc(here, pair, fc_held, sems.at[1]),
        fetch_pj(here, pj, pj_held, sems.at[2]),
        fetch_ao(here, pair_next, next_held, sems.at[3]),
    ]
    for copies in waits:
        begin(copies)
    after_attention(here, stream, mixed, gains, 0, ao_held, fc_held, pj_held, waits, joined, act, before, middle, result)
    finish(waits[3])
    send_qkv(here, result[...], gains, 1, next_held, act, sends)


def middle_part(here, stream, gains, mixed, pair, pj, pair_next):
    return pl.pallas_call(
        middle_kernel,
        out_shape=(shape(D, TOK, dtype=f32), shape(4, TOK, 768, dtype=f32), shape(D, TOK, dtype=f32), *[shape(576, TOK)] * 4),
        in_specs=[SCALARS, *in_vmem(6), *anywhere(24)],
        out_specs=tuple(in_vmem(7)),
        scratch_shapes=[
            AO_HELD,
            FC_HELD,
            PJ_HELD,
            AO_HELD,
            pltpu.VMEM((D, TOK), bf16),
            pltpu.VMEM((FF, TOK), bf16),
            pltpu.SemaphoreType.DMA((4, 8)),
        ],
        compiler_params=params(),
        name="middle_part",
    )(here, stream, gains, *mixed, *pair, *pj, *pair_next)


def back_feed(here, grad, before, middle, gains, layer, ao_held, fc_held, pj_held, waits, act, joined, spread, grad_middle, sends):
    rows = grad[...].T.astype(bf16)
    finish(waits[2])

    for n in range(4):
        cols = slice(768 * n, 768 * n + 768)
        grad_act = jnp.dot(rows, pj_held[:, :, :, :, cols].reshape(D, 768), preferred_element_type=f32)
        act[cols, :] = (gate_slope(before[n]) * grad_act).T.astype(bf16)
    finish(waits[1])
    for n in range(2):
        low = jnp.dot(fc_held[0, 2 * n : 2 * n + 2].reshape(384, 1536), act[:1536, :], preferred_element_type=f32)
        high = jnp.dot(fc_held[1, 2 * n : 2 * n + 2].reshape(384, 1536), act[1536:, :], preferred_element_type=f32)
        grad_middle[384 * n : 384 * n + 384, :] = low + high
    total = grad[...] + norm_back(middle[...], column(gains, layer, 1, 0), grad_middle[...])
    grad_middle[...] = total
    rounded = total.astype(bf16)
    for j in range(8):
        spread[128 * j : 128 * j + 32, :] = jnp.zeros((32, TOK), bf16)
        spread[128 * j + 32 : 128 * j + 128, :] = rounded[96 * j : 96 * j + 96, :]
    finish(waits[0])

    weight = jnp.concatenate([ao_held[:, :, :, 384 * j + 256 : 384 * j + 384].reshape(D, 128) for j in range(8)], axis=1)
    joined[...] = jnp.dot(weight, spread[...], preferred_element_type=f32).astype(bf16)
    for y in range(4):

        @pl.when(here[Y] == y)
        def _():
            for k in range(4):
                row = 192 * ((y + k) % 4)
                sends[k][...] = joined[row : row + 192, :]


def last_kernel(here, stream, gains, *refs):
    mixed, grad_in, pair, pj = refs[0:4], refs[4], refs[5:13], refs[13:21]
    final, grad_middle, *sends = refs[21:27]
    ao_held, fc_held, pj_held, joined, act, spread, before, middle, result, sems = refs[27:]
    waits = [
        fetch_ao(here, pair, ao_held, sems.at[0]),
        fetch_fc(here, pair, fc_held, sems.at[1]),
        fetch_pj(here, pj, pj_held, sems.at[2]),
    ]
    for copies in waits:
        begin(copies)
    after_attention(here, stream, mixed, gains, 1, ao_held, fc_held, pj_held, waits, joined, act, before, middle, result)
    final[...] = result[...].T
    result[...] = flipped(grad_in[...])
    back_feed(here, result, before, middle, gains, 1, ao_held, fc_held, pj_held, [[], [], []], act, joined, spread, grad_middle, sends)


def last_part(here, stream, gains, mixed, grad_in, pair, pj):
    return pl.pallas_call(
        last_kernel,
        out_shape=(shape(TOK, D, dtype=f32), shape(D, TOK, dtype=f32), *[shape(192, TOK)] * 4),
        in_specs=[SCALARS, *in_vmem(7), *anywhere(16)],
        out_specs=tuple(in_vmem(6)),
        scratch_shapes=[
            AO_HELD,
            FC_HELD,
            PJ_HELD,
            pltpu.VMEM((D, TOK), bf16),
            pltpu.VMEM((FF, TOK), bf16),
            pltpu.VMEM((1024, TOK), bf16),
            pltpu.VMEM((4, TOK, 768), f32),
            pltpu.VMEM((D, TOK), f32),
            pltpu.VMEM((D, TOK), f32),
            pltpu.SemaphoreType.DMA((3, 8)),
        ],
        compiler_params=params(),
        name="last_part",
    )(here, stream, gains, *mixed, grad_in, *pair, *pj)


def back_qkv(here, blocks, held, wait, wide, stream, gains, layer, grad_middle, result):
    for j in range(8):
        wide[384 * j + 288 : 384 * j + 384, :] = jnp.zeros((96, TOK), bf16)
    for y in range(4):

        @pl.when(here[Y] == y)
        def _():
            for k in range(4):
                for row, at in rows_of_place((y + k) % 4):
                    wide[row : row + 96, :] = blocks[k][at : at + 96, :]

    finish(wait)

    for n in range(2):
        weight = held[2 * n : 2 * n + 2].reshape(384, 3072)
        result[384 * n : 384 * n + 384, :] = jnp.dot(weight, wide[...], preferred_element_type=f32)
    result[...] = grad_middle[...] + norm_back(stream[...], column(gains, layer, 0, 0), result[...])


def turn_kernel(here, stream, gains, grad_above, before, middle, *refs):
    blocks, pair_above, pair, pj = refs[0:4], refs[4:12], refs[12:20], refs[20:28]
    grad_middle, *sends = refs[28:33]
    above_held, ao_held, fc_held, pj_held, joined, act, spread, grad, sems = refs[33:]
    waits = [
        fetch_ao(here, pair_above, above_held, sems.at[0]),
        fetch_pj(here, pj, pj_held, sems.at[3]),
        fetch_fc(here, pair, fc_held, sems.at[2]),
        fetch_ao(here, pair, ao_held, sems.at[1]),
    ]
    for copies in waits:
        begin(copies)
    back_qkv(here, blocks, above_held, waits[0], act, stream, gains, 1, grad_above, grad)
    back_feed(here, grad, before, middle, gains, 0, ao_held, fc_held, pj_held, [waits[3], waits[2], waits[1]], act, joined, spread, grad_middle, sends)


def turn_part(here, stream, gains, grad_above, before, middle, blocks, pair_above, pair, pj):
    return pl.pallas_call(
        turn_kernel,
        out_shape=(shape(D, TOK, dtype=f32), *[shape(192, TOK)] * 4),
        in_specs=[SCALARS, *in_vmem(9), *anywhere(24)],
        out_specs=tuple(in_vmem(5)),
        scratch_shapes=[
            AO_HELD,
            AO_HELD,
            FC_HELD,
            PJ_HELD,
            pltpu.VMEM((D, TOK), bf16),
            pltpu.VMEM((FF, TOK), bf16),
            pltpu.VMEM((1024, TOK), bf16),
            pltpu.VMEM((D, TOK), f32),
            pltpu.SemaphoreType.DMA((4, 8)),
        ],
        compiler_params=params(),
        name="turn_part",
    )(here, stream, gains, grad_above, before, middle, *blocks, *pair_above, *pair, *pj)


def end_kernel(here, stream, gains, grad_middle, *refs):
    blocks, ao, out, (held, wide, grad, sems) = refs[0:4], refs[4:12], refs[12], refs[13:]
    wait = fetch_ao(here, ao, held, sems)
    begin(wait)
    back_qkv(here, blocks, held, wait, wide, stream, gains, 0, grad_middle, grad)
    out[...] = grad[...].T


def end_part(here, stream, gains, grad_middle, blocks, ao):
    return pl.pallas_call(
        end_kernel,
        out_shape=shape(TOK, D, dtype=f32),
        in_specs=[SCALARS, *in_vmem(7), *anywhere(8)],
        out_specs=pl.BlockSpec(memory_space=pltpu.VMEM),
        scratch_shapes=[AO_HELD, pltpu.VMEM((FF, TOK), bf16), pltpu.VMEM((D, TOK), f32), pltpu.SemaphoreType.DMA((8,))],
        compiler_params=params(),
        name="end_part",
    )(here, stream, gains, grad_middle, *blocks, *ao)


HALF = 256
every = slice(None)
EVERY_PIECE = [slice(TOK * n, TOK * n + TOK) for n in range(8)] + [slice(LENGTH, LENGTH + PAD)]
SEEN = ((0, 1, 4, 5, 8), (0, 1, 2, 3, 4, 5, 6, 7, 8))


def in_order(here, lists):
    for y in range(4):

        @pl.when(here[Y] == y)
        def _():
            for blocks, held, at in lists:
                for k in range(4):
                    held[at + (y + k) % 4] = blocks[k][...]


def hide(here, spans, hidden):
    inside = lax.broadcasted_iota(jnp.int32, (TOK, HALF), 0)
    for part in range(2):
        cols = slice(part * HALF, part * HALF + HALF)
        low, high = spans[0:1, cols], spans[1:2, cols]
        for n in SEEN[part][:-1]:
            start = TOK * (2 * (n % 4) + (here[CORE] if n < 4 else 1 - here[CORE]))
            seen = (inside >= low - start) & (inside <= high - start)
            hidden[EVERY_PIECE[n], cols] = jnp.where(seen, 0.0, big_negative)
    real = lax.broadcasted_iota(jnp.int32, (PAD, 2 * HALF), 0) < PREFIX
    hidden[LENGTH:, :] = jnp.where(real, 0.0, big_negative)


def head_rows(held, n, t, h):
    return held[n, 192 * t + 64 * h : 192 * t + 64 * h + 64, :]


def keys_and_values(held, table, h):
    tall = []
    for n in range(8):
        both = jnp.concatenate([head_rows(held, n, 1, h), head_rows(held, n, 2, h)], axis=0)
        tall.append(both.astype(f32).T.astype(bf16))
    return [*tall, table[h]]


def side_by_side(held, pieces, t, h):
    return jnp.concatenate([head_rows(held, n, t, h) for n in pieces], axis=1)


def stacked_rows(ref, pieces, cols):
    return jnp.concatenate([ref[EVERY_PIECE[n], cols] for n in pieces], axis=0)


def attend_kernel(here, spans, *refs):
    own, other, (table, table_t), mixed, logs = refs[0:4], refs[4:8], refs[8:10], refs[10:14], refs[14]
    held, hidden, scores, probs, out = refs[15:]
    in_order(here, [(own, held, 0), (other, held, 4)])
    hide(here, spans, hidden)
    for h in range(GROUP):
        tall = keys_and_values(held, table, h)
        for part in range(2):
            cols = slice(part * HALF, part * HALF + HALF)
            pieces = SEEN[part]
            query = side_by_side(held, (2 * part, 2 * part + 1), 0, h) * bf16(0.125)
            right = jnp.concatenate([query, jnp.zeros_like(query)], axis=0)
            top = jnp.full((8, HALF), big_negative, f32)
            for n in pieces:
                block = jnp.dot(tall[n], right, preferred_element_type=f32) + hidden[EVERY_PIECE[n], cols]
                scores[EVERY_PIECE[n], :] = block
                top = jnp.maximum(top, jnp.max(block.reshape(-1, 8, HALF), axis=0))
            top = jnp.max(top, axis=0, keepdims=True)
            total = jnp.zeros((8, HALF), f32)
            for n in pieces:
                block = jnp.exp(scores[EVERY_PIECE[n], :] - top)
                scores[EVERY_PIECE[n], :] = block
                total = total + jnp.sum(block.reshape(-1, 8, HALF), axis=0)
            total = jnp.sum(total, axis=0, keepdims=True)
            share = 1.0 / total
            for n in pieces:
                probs[EVERY_PIECE[n], :] = (scores[EVERY_PIECE[n], :] * share).astype(bf16)
            result = jnp.dot(
                side_by_side(held, pieces[:-1], 2, h), stacked_rows(probs, pieces[:-1], every), preferred_element_type=f32
            )
            result = result + jnp.dot(table_t[h, 64:, :], probs[LENGTH:, :], preferred_element_type=f32)
            for n in range(2):
                out[2 * part + n, 64 * h : 64 * h + 64, :] = result[:, TOK * n : TOK * n + TOK].astype(bf16)
            logs[h : h + 1, cols] = top + jnp.log(total)
    for y in range(4):

        @pl.when(here[Y] == y)
        def _():
            for k in range(4):
                mixed[k][...] = out[(y + k) % 4]


def attend(here, spans, own, other, table, table_t):
    return pl.pallas_call(
        attend_kernel,
        out_shape=(*[shape(192, TOK)] * 4, shape(8, 512, dtype=f32)),
        in_specs=[SCALARS, *in_vmem(11)],
        out_specs=tuple(in_vmem(5)),
        scratch_shapes=[
            pltpu.VMEM((8, 576, TOK), bf16),
            pltpu.VMEM((LENGTH + PAD, 2 * HALF), f32),
            pltpu.VMEM((LENGTH + PAD, HALF), f32),
            pltpu.VMEM((LENGTH + PAD, HALF), bf16),
            pltpu.VMEM((4, 192, TOK), bf16),
        ],
        compiler_params=params(),
        name="attend",
    )(here, spans, *own, *other, table, table_t)


def attend_back_kernel(here, spans, logs, *refs):
    own, other, grads, (table, table_t) = refs[0:4], refs[4:8], refs[8:12], refs[12:14]
    grad_query, mine, others, grad_table = refs[14:18]
    held, grads_held, hidden, probs, slopes, packed, sums = refs[18:]
    in_order(here, [(own, held, 0), (other, held, 4), (grads, grads_held, 0)])
    hide(here, spans, hidden)
    for h in range(GROUP):
        tall = keys_and_values(held, table, h)
        for part in (1, 0):
            cols = slice(part * HALF, part * HALF + HALF)
            pieces = SEEN[part]
            query = side_by_side(held, (2 * part, 2 * part + 1), 0, h) * bf16(0.125)
            grad = jnp.concatenate([grads_held[2 * part + n, 64 * h : 64 * h + 64, :] for n in range(2)], axis=1)
            nothing = jnp.zeros_like(query)
            right = jnp.concatenate(
                [jnp.concatenate([query, nothing], axis=1), jnp.concatenate([nothing, grad], axis=1)], axis=0
            )
            right_t = right.astype(f32).T.astype(bf16)
            log_total = logs[h : h + 1, cols]
            inner = jnp.zeros((8, HALF), f32)
            for n in pieces:
                piece = EVERY_PIECE[n]
                both = jnp.dot(tall[n], right, preferred_element_type=f32)
                prob = jnp.exp(both[:, :HALF] + hidden[piece, cols] - log_total)
                slope = both[:, HALF:]
                probs[piece, :] = prob
                slopes[piece, :] = slope
                packed[piece, HALF:] = prob.astype(bf16)
                inner = inner + jnp.sum((prob * slope).reshape(-1, 8, HALF), axis=0)
            inner = jnp.sum(inner, axis=0, keepdims=True)
            for n in pieces:
                piece = EVERY_PIECE[n]
                packed[piece, :HALF] = (probs[piece, :] * (slopes[piece, :] - inner)).astype(bf16)
            result = jnp.dot(
                side_by_side(held, pieces[:-1], 1, h),
                stacked_rows(packed, pieces[:-1], slice(0, HALF)),
                preferred_element_type=f32,
            )
            result = result + jnp.dot(table_t[h, :64, :], packed[LENGTH:, :HALF], preferred_element_type=f32)
            grad_query[64 * h : 64 * h + 64, cols] = (result * 0.125).astype(bf16)
            for n in pieces:
                new = jnp.dot(packed[EVERY_PIECE[n], :], right_t, preferred_element_type=f32)
                sums[EVERY_PIECE[n], :] = new if part == 1 else sums[EVERY_PIECE[n], :] + new
        for n in range(4):
            mine[h, :, TOK * n : TOK * n + TOK] = sums[EVERY_PIECE[n], :].T
            others[h, :, TOK * n : TOK * n + TOK] = sums[EVERY_PIECE[4 + n], :].T.astype(bf16)
        grad_table[PREFIX * h : PREFIX * h + PREFIX, :] = sums[LENGTH : LENGTH + PREFIX, :]
    grad_table[GROUP * PREFIX :, :] = jnp.zeros((ROWS - GROUP * PREFIX, 128), f32)


def attend_back(here, spans, logs, own, other, grads, table, table_t):
    return pl.pallas_call(
        attend_back_kernel,
        out_shape=(
            shape(192, 512),
            shape(GROUP, 128, 512, dtype=f32),
            shape(GROUP, 128, 512),
            shape(ROWS, 128, dtype=f32),
        ),
        in_specs=[SCALARS, *in_vmem(16)],
        out_specs=tuple(in_vmem(4)),
        scratch_shapes=[
            pltpu.VMEM((8, 576, TOK), bf16),
            pltpu.VMEM((4, 192, TOK), bf16),
            pltpu.VMEM((LENGTH + PAD, 2 * HALF), f32),
            pltpu.VMEM((LENGTH + PAD, HALF), f32),
            pltpu.VMEM((LENGTH + PAD, HALF), f32),
            pltpu.VMEM((LENGTH + PAD, 2 * HALF), bf16),
            pltpu.VMEM((LENGTH + PAD, 128), f32),
        ],
        compiler_params=params(),
        name="attend_back",
    )(here, spans, logs, *own, *other, *grads, table, table_t)


def pack_back_kernel(here, grad_query, mine, got, *outs):
    for y in range(4):

        @pl.when(here[Y] == y)
        def _():
            for k in range(4):
                start = TOK * ((y + k) % 4)
                cols = slice(start, start + TOK)
                outs[k][0:192, :] = grad_query[:, cols]
                for h in range(GROUP):
                    both = (mine[h, :, cols] + got[h, :, cols].astype(f32)).astype(bf16)
                    outs[k][192 + 64 * h : 256 + 64 * h, :] = both[:64, :]
                    outs[k][384 + 64 * h : 448 + 64 * h, :] = both[64:, :]


def pack_back(here, grad_query, mine, got):
    return pl.pallas_call(
        pack_back_kernel,
        out_shape=tuple([shape(576, TOK)] * 4),
        in_specs=[SCALARS, *in_vmem(3)],
        out_specs=tuple(in_vmem(4)),
        compiler_params=params(),
        name="pack_back",
    )(here, grad_query, mine, got)


def split(value):
    high = value.astype(bf16)
    return high, (value - high.astype(f32)).astype(bf16)


def products(left, right, dims):
    total = None
    for a, b in ((1, 0), (0, 1), (0, 0)):
        term = lax.dot_general(left[a], right[b], (dims, ((), ())), preferred_element_type=f32)
        total = term if total is None else total + term
    return total


PLAIN, TURNED = ((1,), (0,)), ((1,), (1,))


def chain_kernel(hidden, hidden_t, table_t, matrix_in, matrix_out, parts, g_table, g_in, g_in_bias, g_out, g_out_bias, *scratch):
    grads, held_out, new_out, held_in, sems = scratch
    chunks = [slice(512 * n, 512 * n + 512) for n in range(6)]
    reads = [pltpu.make_async_copy(matrix_out.at[:, c], held_out.at[:, c], sems.at[n]) for n, c in enumerate(chunks)]
    reads.append(pltpu.make_async_copy(matrix_in, held_in, sems.at[6]))
    writes = [pltpu.make_async_copy(new_out.at[:, c], g_out.at[:, c], sems.at[7 + n]) for n, c in enumerate(chunks)]
    begin(reads)
    grads[...] = jnp.zeros_like(grads)
    for y in range(SIDE):
        total = jnp.zeros((LAYERS * ROWS, 128), f32)
        for z in range(4):
            for xl in range(2):
                for xh in range(2):
                    total = total + parts[((z * 2 + xl) * 4 + y) * 2 + xh]
        for layer in range(LAYERS):
            for h in range(GROUP):
                first_row = ROWS * layer + PREFIX * h
                rows = total[first_row : first_row + PREFIX, :]
                at = layer * 2 * D + (GROUP * y + h) * HD
                grads[:PREFIX, at : at + HD] = rows[:, :HD]
                grads[:PREFIX, at + D : at + D + HD] = rows[:, HD:]
    g_out_bias[...] = jnp.sum(grads[...], axis=0, keepdims=True)
    hidden_parts = split(hidden_t[...])
    some = [split(grads[:, cols]) for cols in chunks]
    for n, cols in enumerate(chunks):
        new_out[:, cols] = products(hidden_parts, some[n], PLAIN)
        writes[n].start()
    slope = jnp.zeros((PAD, 512), f32)
    for n, cols in enumerate(chunks):
        reads[n].wait()
        slope = slope + products(some[n], split(held_out[:, cols]), TURNED)
    slope = slope * (1.0 - hidden[...] * hidden[...])
    g_in_bias[...] = jnp.sum(slope, axis=0, keepdims=True)
    parts_of_slope = split(slope)
    g_in[...] = products(split(table_t[...]), parts_of_slope, PLAIN)
    reads[6].wait()
    g_table[...] = products(parts_of_slope, split(held_in[...]), TURNED)[:PREFIX, :]
    finish(writes)


def chain(hidden, table, matrix_in, matrix_out, parts):
    g_table, g_in, g_in_bias, g_out, g_out_bias = pl.pallas_call(
        chain_kernel,
        out_shape=(
            shape(PREFIX, D, dtype=f32),
            shape(D, 512, dtype=f32),
            shape(1, 512, dtype=f32),
            shape(512, 2 * LAYERS * D, dtype=f32),
            shape(1, 2 * LAYERS * D, dtype=f32),
        ),
        in_specs=[*in_vmem(3), *anywhere(2), *in_vmem(1)],
        out_specs=(*in_vmem(3), *anywhere(1), *in_vmem(1)),
        scratch_shapes=[
            pltpu.VMEM((PAD, 2 * LAYERS * D), f32),
            pltpu.VMEM((512, 2 * LAYERS * D), f32),
            pltpu.VMEM((512, 2 * LAYERS * D), f32),
            pltpu.VMEM((D, 512), f32),
            pltpu.SemaphoreType.DMA((13,)),
        ],
        compiler_params=params(),
        name="chain",
    )(hidden, hidden.T, table.T, matrix_in, matrix_out, parts)
    return g_table, g_in, g_in_bias[0], g_out, g_out_bias[0]


def start_weights(here, attn_weight, out_weight, fc_weight, proj_weight):
    core = here[CORE]
    turned = jnp.swapaxes(proj_weight, 1, 2)
    mine = lax.dynamic_slice_in_dim(turned, 48 * core, 48, axis=1)
    theirs = lax.dynamic_slice_in_dim(turned, 48 * (1 - core), 48, axis=1)
    ao = jnp.concatenate([attn_weight, out_weight], axis=2)
    kept, given = jnp.where(core == 0, ao, fc_weight), jnp.where(core == 0, fc_weight, ao)
    got = move(given, core_pairs())
    pair = jnp.where(core == 0, jnp.stack([kept, got], axis=1), jnp.stack([got, kept], axis=1))
    got = move(theirs, core_pairs())
    pj = jnp.where(core == 0, jnp.concatenate([mine, got], axis=2), jnp.concatenate([got, mine], axis=2))
    pair = assemble(here, around_two(pair, X, Y), None, shape(2, 4, 48, 768), put_pair_one)
    pj = assemble(here, around(pj, Z), None, shape(2, 48, 1536), put_proj_one)
    return around_two(pair, Y, Z), around(pj, X)


def both_cores(blocks):
    return [*blocks, *[move(b, core_pairs()) for b in blocks]]


def rest_of_pair(here, blocks, layer, waits=()):
    whole = assemble(here, blocks, layer, shape(4, 48, 3072), put_pair_two, waits)
    return both_cores(around_two(whole, Z, X))


def rest_of_proj(here, blocks, layer, waits=()):
    whole = assemble(here, blocks, layer, shape(2, 48, 3072), put_proj_two, waits)
    return both_cores(around(whole, Y))


def share_tables(parts):
    both = jnp.concatenate(parts, axis=0)
    spread = jnp.broadcast_to(both[None], (64, LAYERS * ROWS, 128))
    return lax.all_to_all(spread, ("z", "xl", "y", "xh"), 0, 0, tiled=True)


def on_device(
    states_in,
    attn_weight,
    out_weight,
    fc_weight,
    proj_weight,
    norm_gain,
    norm_shift,
    prefix_table,
    reparam_in,
    reparam_in_bias,
    reparam_out,
    reparam_out_bias,
    doc_lengths,
    pad_counts,
    states_grad,
):
    z, xl, core, y, xh = (lax.axis_index(name) for name in AXES)
    here = jnp.stack([z, 2 * xh + xl, core, y]).astype(jnp.int32)
    pair, proj = start_weights(here, attn_weight, out_weight, fc_weight, proj_weight)
    weights = [[rest_of_pair(here, pair, 0), rest_of_proj(here, proj, 0)], None]
    x = move(states_in[0], seat_pairs())
    grad_in = move(states_grad[0], seat_pairs())

    layout = jnp.concatenate([doc_lengths[0], pad_counts])
    layout = jnp.where(xh == core, layout, move(layout, core_pairs()))
    ends = jnp.cumsum(layout[:-1])
    blocks = 2 * jnp.arange(4) + core
    places = (TOK * blocks[:, None] + jnp.arange(TOK)[None, :]).reshape(-1)
    starts = jnp.max(jnp.where(ends[:, None] <= places[None, :], ends[:, None], 0), axis=0)
    starts = jnp.where(places < LENGTH - layout[-1], starts, 4 * LENGTH)
    spans = jnp.stack([starts, places]).astype(jnp.int32)

    table = jnp.pad(prefix_table, ((0, PAD - PREFIX), (0, 0)))
    hidden = jnp.tanh(jnp.dot(prefix_table, reparam_in, precision=highest) + reparam_in_bias)
    prefix_flat = jnp.dot(hidden, reparam_out, precision=highest) + reparam_out_bias
    hidden = jnp.pad(hidden, ((0, PAD - PREFIX), (0, 0)))
    tables = prefix_flat.astype(bf16).reshape(PREFIX, LAYERS, 2, SIDE, GROUP, HD)
    tables = lax.dynamic_index_in_dim(tables, y, axis=3, keepdims=False)
    tables = tables.transpose(1, 3, 0, 2, 4).reshape(LAYERS, GROUP, PREFIX, 2 * HD)
    tables = jnp.pad(tables, ((0, 0), (0, 0), (0, PAD - PREFIX), (0, 0)))
    tables_t = jnp.swapaxes(tables, 2, 3)
    gains = jnp.stack([norm_gain, norm_shift], axis=2).reshape(8, D).T

    stream, *sends = first(here, x, gains, weights[0][0])
    streams = [stream]
    later = (sends[0],)
    weights[1] = [rest_of_pair(here, pair, 1, later), rest_of_proj(here, proj, 1, later)]
    kept = []
    for layer in range(LAYERS):
        own = to_places(sends, Y)
        other = [move(b, core_pairs()) for b in own]
        *mixed, logs = attend(here, spans, own, other, tables[layer], tables_t[layer])
        mixed = to_places(mixed, Y)
        kept.append((own, other, logs))
        if layer == 0:
            middle, before, stream, *sends = middle_part(here, stream, gains, mixed, *weights[0], weights[1][0])
            streams.append(stream)
        else:
            final, grad_middle, *sends = last_part(here, stream, gains, mixed, grad_in, *weights[1])
    final = move(final, seat_pairs())

    totals = [None] * LAYERS
    for layer in reversed(range(LAYERS)):
        own, other, logs = kept[layer]
        grads = to_places(sends, Y)
        grad_query, mine, theirs, grad_table = attend_back(here, spans, logs, own, other, grads, tables[layer], tables_t[layer])
        sends = pack_back(here, grad_query, mine, move(theirs, core_pairs()))
        totals[layer] = grad_table + move(grad_table, core_pairs())
        back = to_places(sends, Y)
        if layer == 1:
            grad_middle, *sends = turn_part(
                here, streams[1], gains, grad_middle, before, middle, back, weights[1][0], *weights[0]
            )
        else:
            grad_states = end_part(here, streams[0], gains, grad_middle, back, weights[0][0])
    grad_states = move(grad_states, seat_pairs())

    return (final[None], grad_states[None], *chain(hidden, table, reparam_in, reparam_out, share_tables(totals)))


def solution(mesh):
    grid = Mesh(mesh.devices.reshape(GRID), AXES)
    rows, cols = ("z", "xl", "core"), ("y", "xh")
    return jax.shard_map(
        on_device,
        mesh=grid,
        in_specs=(
            P(rows, cols, None),
            P(None, rows, cols),
            P(None, rows, cols),
            P(None, rows, cols),
            P(None, rows, cols),
            P(),
            P(),
            P(),
            P(),
            P(),
            P(),
            P(),
            P(rows, None),
            P(rows),
            P(rows, cols, None),
        ),
        out_specs=(P(rows, cols, None), P(rows, cols, None), P(), P(), P(), P(), P()),
        check_vma=False,
    )
```

```python
import jax
import jax.numpy as jnp
from jax import lax
from jax.experimental import pallas as pl
from jax.experimental.pallas import tpu as pltpu
from jax.sharding import Mesh
from jax.sharding import PartitionSpec as P

D = 768
H = 12
HD = 64
FF = 3072
LENGTH = 1024
PREFIX = 10
LAYERS = 2
TOK = 128
PAD = 16
GROUP = 3
ROWS = 32
SIDE = 4
AXES = ("z", "xl", "core", "y", "xh")
GRID = (4, 2, 2, 4, 2)

epsilon = 1e-05
highest = lax.Precision.HIGHEST
big_negative = -1e30
bf16 = jnp.bfloat16
f32 = jnp.float32
VMEM_LIMIT = 56 * 2**20


def index_of(z, x, core, y):
    return (((z * 2 + x % 2) * 2 + core) * 4 + y) * 2 + x // 2


def everywhere():
    return [(z, x, c, y) for z in range(4) for x in range(4) for c in range(2) for y in range(4)]


def ring(axis, ahead):
    pairs = []
    for spot in everywhere():
        source = list(spot)
        source[axis] = (source[axis] + ahead) % 4
        pairs.append((index_of(*source), index_of(*spot)))
    return pairs


def two_rings(axis_zero, axis_one, ahead):
    pairs = []
    for spot in everywhere():
        source = list(spot)
        axis = axis_one if spot[CORE] else axis_zero
        source[axis] = (source[axis] + ahead) % 4
        pairs.append((index_of(*source), index_of(*spot)))
    return pairs


def core_pairs():
    return [(index_of(z, x, 1 - c, y), index_of(z, x, c, y)) for z, x, c, y in everywhere()]


def seat_pairs():
    return [(index_of(z, c * 2 + x % 2, x // 2, y), index_of(z, x, c, y)) for z, x, c, y in everywhere()]


Z, X, CORE, Y = 0, 1, 2, 3


def move(value, pairs):
    return lax.ppermute(value, AXES, pairs)


def around(value, axis):
    return [value] + [move(value, ring(axis, k)) for k in (1, 2, 3)]


def around_two(value, axis_zero, axis_one):
    return [value] + [move(value, two_rings(axis_zero, axis_one, k)) for k in (1, 2, 3)]


def to_places(blocks):
    got = [None, *[move(blocks[k], ring(Y, -k)) for k in (1, 2, 3)]]
    return [blocks[0], got[3], got[2], got[1]]


def swap_on_ring(blocks):
    return lax.all_to_all(blocks, "y", 0, 0, tiled=True)


def wrap(value):
    return lax.rem(value, SIDE)


def params(limit=VMEM_LIMIT):
    return pltpu.CompilerParams(vmem_limit_bytes=limit)


def anywhere(count):
    return [pl.BlockSpec(memory_space=pl.ANY)] * count


def in_vmem(count):
    return [pl.BlockSpec(memory_space=pltpu.VMEM)] * count


SCALARS = pl.BlockSpec(memory_space=pltpu.SMEM)


def shape(*dims, dtype=bf16):
    return jax.ShapeDtypeStruct(dims, dtype)


def lanes(start, size):
    return pl.ds(pl.multiple_of(start, 128), size)


def block_of(layer, dims):
    if layer is None:
        return pl.BlockSpec(dims, lambda i: (0,) * len(dims))
    return pl.BlockSpec((None, *dims[1:]), lambda i: (layer,) + (0,) * (len(dims) - 1))


def assemble(here, layer, groups, waits=()):
    count = len(groups)

    def kernel(here, *refs):
        for n, (_, _, put) in enumerate(groups):
            for k in range(4):
                put(here, k, refs[4 * n + k], refs[n - count])

    blocks = [b for group in groups for b in group[0]]
    outs = [group[1] for group in groups]
    return pl.pallas_call(
        kernel,
        grid=(1,),
        out_shape=outs,
        in_specs=[SCALARS, *[block_of(layer, b.shape) for b in blocks], *anywhere(len(waits))],
        out_specs=[block_of(None, out.shape) for out in outs],
        compiler_params=params(),
        name="assemble",
    )(here, *blocks, *waits)


def pick(here, zero, one):
    return jnp.where(here[CORE] == 0, zero, one)


def put_pair_one(here, k, block, result):
    place = wrap(pick(here, here[X], here[Y]) + k)
    low, high = lax.rem(place, 2), lax.div(place, 2)
    for c in range(2):
        row, col = pick(here, 2 * low + c, 2 * c + high), pick(here, high, low)
        result[:, row, :, lanes(384 * col, 384)] = block[c]


def put_pair_two(here, k, block, result):
    place = wrap(pick(here, here[Y], here[Z]) + k)
    for i in range(4):
        result[pick(here, i, place), :, lanes(768 * pick(here, place, i), 768)] = block[i]


def put_proj_one(here, k, block, result):
    result[:, :, lanes(384 * wrap(here[Z] + k), 384)] = block[...]


def put_proj_two(here, k, block, result):
    place = wrap(here[X] + k)
    result[lax.div(place, 2), :, lanes(1536 * lax.rem(place, 2), 1536)] = block[...]


AO_HELD = pltpu.VMEM((4, 4, 48, 3072), bf16)
FC_HELD = pltpu.VMEM((2, 4, 2, 2, 48, 1536), bf16)
PJ_HELD = pltpu.VMEM((4, 2, 2, 48, 3072), bf16)


class Chosen:
    def __init__(self, here, zero, one, target, sem):
        self.here = here
        self.copies = [pltpu.make_async_copy(source, target, sem) for source in (zero, one)]

    def start(self):
        for core in range(2):
            pl.when(self.here[CORE] == core)(self.copies[core].start)

    def wait(self):
        self.copies[0].wait()


def fetch_ao(here, refs, held, sems):
    return [Chosen(here, refs[k], refs[4 + k], held.at[wrap(here[Z] + k)], sems.at[k]) for k in range(4)]


def fetch_fc(here, refs, held, sems):
    copies = []
    for k in range(4):
        there = wrap(here[X] + k)
        for c in range(2):
            target = held.at[lax.div(there, 2), :, lax.rem(there, 2), c]
            cols = slice(1536 * c, 1536 * c + 1536)
            copies.append(Chosen(here, refs[4 + k].at[:, :, cols], refs[k].at[:, :, cols], target, sems.at[2 * k + c]))
    return copies


def fetch_pj(here, refs, held, sems):
    return [
        pltpu.make_async_copy(refs[4 * n + k], held.at[wrap(here[Y] + k), :, core], sems.at[4 * n + k])
        for n, core in enumerate((here[CORE], 1 - here[CORE]))
        for k in range(4)
    ]


def begin(copies):
    for one in copies:
        one.start()


def finish(copies):
    for one in copies:
        one.wait()


def flipped(value):
    return value.astype(f32).T


def norm_stats(stream):
    centre = jnp.mean(stream, axis=0, keepdims=True)
    centred = stream - centre
    spread = jnp.mean(centred * centred, axis=0, keepdims=True)
    return centred, lax.rsqrt(spread + epsilon)


def norm(stream, gain, shift):
    centred, rate = norm_stats(stream)
    return centred * rate * gain + shift


def norm_back(stream, gain, grad):
    centred, rate = norm_stats(stream)
    unit = centred * rate
    scaled = grad * gain
    inner = jnp.mean(scaled * unit, axis=0, keepdims=True)
    return rate * (scaled - jnp.mean(scaled, axis=0, keepdims=True) - unit * inner)


root = 0.7978845608028654


def gate(u):
    return 0.5 * u * (1.0 + jnp.tanh(root * (u + 0.044715 * (u * u * u))))


def gate_slope(u):
    squared = u * u
    t = jnp.tanh(root * (u + 0.044715 * (squared * u)))
    return 0.5 * (1.0 + t) + (0.5 * root) * u * (1.0 - t * t) * (1.0 + (3.0 * 0.044715) * squared)


def column(gains, layer, which, part):
    at = layer * 4 + which * 2 + part
    return gains[:, at : at + 1]


def rows_of_place(place):
    pieces = []
    for t in range(3):
        for u in range(2):
            piece = 8 * t + 2 * place + u
            pieces.append((384 * (piece // 3) + 96 * (piece % 3), t * 192 + u * 96))
    return pieces


def send_qkv(here, stream, gains, layer, held, wide, sends):
    normed = norm(stream, column(gains, layer, 0, 0), column(gains, layer, 0, 1)).T.astype(bf16)
    for j in range(4):
        cols = slice(768 * j, 768 * j + 768)
        packed = jnp.dot(normed, held[:, :, :, cols].reshape(D, 768), preferred_element_type=f32)
        wide[cols, :] = packed.T.astype(bf16)
    for place in range(4):
        for row, at in rows_of_place(place):
            sends[place, at : at + 96, :] = wide[row : row + 96, :]


def first_kernel(here, x_ref, gains, *refs):
    ao, (stream, sends), (held, wide, sems) = refs[0:8], refs[8:10], refs[10:]
    copies = fetch_ao(here, ao, held, sems)
    begin(copies)
    stream[...] = flipped(x_ref[...])
    finish(copies)
    send_qkv(here, stream[...], gains, 0, held, wide, sends)


def first(here, x, gains, ao, waits):
    def kernel(*refs):
        first_kernel(*refs[:11], *refs[11 + len(waits) :])

    return pl.pallas_call(
        kernel,
        out_shape=(shape(D, TOK, dtype=f32), shape(4, 576, TOK)),
        in_specs=[SCALARS, *in_vmem(2), *anywhere(8 + len(waits))],
        out_specs=tuple(in_vmem(2)),
        scratch_shapes=[AO_HELD, pltpu.VMEM((FF, TOK), bf16), pltpu.SemaphoreType.DMA((8,))],
        compiler_params=params(),
        name="first",
    )(here, x, gains, *ao, *waits)


def after_attention(here, stream, mixed, gains, layer, ao_held, fc_held, pj_held, waits, act, before, middle, result):
    rows = flipped(mixed[...].reshape(D, TOK)).astype(bf16)
    finish(waits[0])

    weight = jnp.concatenate([ao_held[:, :, :, 384 * j + 256 : 384 * j + 384].reshape(D, 128) for j in range(8)], axis=1)
    part = jnp.dot(rows, weight, preferred_element_type=f32).T
    for j in range(8):
        at = slice(96 * j, 96 * j + 96)
        middle[at, :] = stream[at, :] + part[128 * j + 32 : 128 * j + 128, :]
    normed = norm(middle[...], column(gains, layer, 1, 0), column(gains, layer, 1, 1)).T.astype(bf16)
    finish(waits[1])

    for n in range(4):
        low = 768 * (n % 2)
        weight = fc_held[n // 2, :, :, :, :, low : low + 768].reshape(D, 768)
        inputs = jnp.dot(normed, weight, preferred_element_type=f32)
        before[n] = inputs
        act[768 * n : 768 * n + 768, :] = gate(inputs).T.astype(bf16)
    finish(waits[2])
    for n in range(2):
        at = slice(384 * n, 384 * n + 384)
        weight = pj_held[2 * n : 2 * n + 2].reshape(384, FF)
        result[at, :] = middle[at, :] + jnp.dot(weight, act[...], preferred_element_type=f32)


def middle_kernel(here, stream, gains, *refs):
    mixed, pair, pj, pair_next = refs[0], refs[1:9], refs[9:17], refs[17:25]
    middle, before, result, sends = refs[25:29]
    ao_held, fc_held, pj_held, next_held, act, sems = refs[29:]
    waits = [
        fetch_ao(here, pair, ao_held, sems.at[0]),
        fetch_fc(here, pair, fc_held, sems.at[1]),
        fetch_pj(here, pj, pj_held, sems.at[2]),
        fetch_ao(here, pair_next, next_held, sems.at[3]),
    ]
    for copies in waits:
        begin(copies)
    after_attention(here, stream, mixed, gains, 0, ao_held, fc_held, pj_held, waits, act, before, middle, result)
    finish(waits[3])
    send_qkv(here, result[...], gains, 1, next_held, act, sends)


def middle_part(here, stream, gains, mixed, pair, pj, pair_next, waits):
    def kernel(*refs):
        middle_kernel(*refs[:28], *refs[28 + len(waits) :])

    return pl.pallas_call(
        kernel,
        out_shape=(shape(D, TOK, dtype=f32), shape(4, TOK, 768, dtype=f32), shape(D, TOK, dtype=f32), shape(4, 576, TOK)),
        in_specs=[SCALARS, *in_vmem(3), *anywhere(24 + len(waits))],
        out_specs=tuple(in_vmem(4)),
        scratch_shapes=[
            AO_HELD,
            FC_HELD,
            PJ_HELD,
            AO_HELD,
            pltpu.VMEM((FF, TOK), bf16),
            pltpu.SemaphoreType.DMA((4, 8)),
        ],
        compiler_params=params(),
        name="middle_part",
    )(here, stream, gains, mixed, *pair, *pj, *pair_next, *waits)


def back_feed(here, grad, before, middle, gains, layer, ao_held, fc_held, pj_held, waits, act, spread, grad_middle, sends):
    rows = grad[...].T.astype(bf16)
    finish(waits[2])

    for n in range(4):
        cols = slice(768 * n, 768 * n + 768)
        grad_act = jnp.dot(rows, pj_held[:, :, :, :, cols].reshape(D, 768), preferred_element_type=f32)
        act[cols, :] = (gate_slope(before[n]) * grad_act).T.astype(bf16)
    finish(waits[1])
    for n in range(2):
        low = jnp.dot(fc_held[0, 2 * n : 2 * n + 2].reshape(384, 1536), act[:1536, :], preferred_element_type=f32)
        high = jnp.dot(fc_held[1, 2 * n : 2 * n + 2].reshape(384, 1536), act[1536:, :], preferred_element_type=f32)
        grad_middle[384 * n : 384 * n + 384, :] = low + high
    total = grad[...] + norm_back(middle[...], column(gains, layer, 1, 0), grad_middle[...])
    grad_middle[...] = total
    rounded = total.astype(bf16)
    for j in range(8):
        spread[128 * j : 128 * j + 32, :] = jnp.zeros((32, TOK), bf16)
        spread[128 * j + 32 : 128 * j + 128, :] = rounded[96 * j : 96 * j + 96, :]
    finish(waits[0])

    weight = jnp.concatenate([ao_held[:, :, :, 384 * j + 256 : 384 * j + 384].reshape(D, 128) for j in range(8)], axis=1)
    whole = jnp.dot(weight, spread[...], preferred_element_type=f32).astype(bf16)
    for y in range(4):

        @pl.when(here[Y] == y)
        def _():
            for k in range(4):
                row = 192 * ((y + k) % 4)
                sends[k][...] = whole[row : row + 192, :]


def last_kernel(here, stream, gains, *refs):
    mixed, grad_in, pair, pj = refs[0], refs[1], refs[2:10], refs[10:18]
    final, grad_middle, *sends = refs[18:24]
    ao_held, fc_held, pj_held, act, spread, before, middle, result, sems = refs[24:]
    waits = [
        fetch_ao(here, pair, ao_held, sems.at[0]),
        fetch_fc(here, pair, fc_held, sems.at[1]),
        fetch_pj(here, pj, pj_held, sems.at[2]),
    ]
    for copies in waits:
        begin(copies)
    after_attention(here, stream, mixed, gains, 1, ao_held, fc_held, pj_held, waits, act, before, middle, result)
    final[...] = result[...].T
    result[...] = flipped(grad_in[...])
    back_feed(here, result, before, middle, gains, 1, ao_held, fc_held, pj_held, [[], [], []], act, spread, grad_middle, sends)


def last_part(here, stream, gains, mixed, grad_in, pair, pj):
    return pl.pallas_call(
        last_kernel,
        out_shape=(shape(TOK, D, dtype=f32), shape(D, TOK, dtype=f32), *[shape(192, TOK)] * 4),
        in_specs=[SCALARS, *in_vmem(4), *anywhere(16)],
        out_specs=tuple(in_vmem(6)),
        scratch_shapes=[
            AO_HELD,
            FC_HELD,
            PJ_HELD,
            pltpu.VMEM((FF, TOK), bf16),
            pltpu.VMEM((1024, TOK), bf16),
            pltpu.VMEM((4, TOK, 768), f32),
            pltpu.VMEM((D, TOK), f32),
            pltpu.VMEM((D, TOK), f32),
            pltpu.SemaphoreType.DMA((3, 8)),
        ],
        compiler_params=params(),
        name="last_part",
    )(here, stream, gains, mixed, grad_in, *pair, *pj)


def back_qkv(here, blocks, held, wait, wide, stream, gains, layer, grad_middle, result):
    for j in range(8):
        wide[384 * j + 288 : 384 * j + 384, :] = jnp.zeros((96, TOK), bf16)
    for y in range(4):

        @pl.when(here[Y] == y)
        def _():
            for k in range(4):
                for row, at in rows_of_place((y + k) % 4):
                    wide[row : row + 96, :] = blocks[k][at : at + 96, :]

    finish(wait)

    for n in range(2):
        weight = held[2 * n : 2 * n + 2].reshape(384, 3072)
        result[384 * n : 384 * n + 384, :] = jnp.dot(weight, wide[...], preferred_element_type=f32)
    result[...] = grad_middle[...] + norm_back(stream[...], column(gains, layer, 0, 0), result[...])


def turn_kernel(here, stream, gains, grad_above, before, middle, *refs):
    blocks, pair_above, pair, pj = refs[0:4], refs[4:12], refs[12:20], refs[20:28]
    grad_middle, *sends = refs[28:33]
    above_held, ao_held, fc_held, pj_held, act, spread, grad, sems = refs[33:]
    waits = [
        fetch_ao(here, pair_above, above_held, sems.at[0]),
        fetch_pj(here, pj, pj_held, sems.at[3]),
        fetch_fc(here, pair, fc_held, sems.at[2]),
        fetch_ao(here, pair, ao_held, sems.at[1]),
    ]
    for copies in waits:
        begin(copies)
    back_qkv(here, blocks, above_held, waits[0], act, stream, gains, 1, grad_above, grad)
    back_feed(here, grad, before, middle, gains, 0, ao_held, fc_held, pj_held, [waits[3], waits[2], waits[1]], act, spread, grad_middle, sends)


def turn_part(here, stream, gains, grad_above, before, middle, blocks, pair_above, pair, pj):
    return pl.pallas_call(
        turn_kernel,
        out_shape=(shape(D, TOK, dtype=f32), *[shape(192, TOK)] * 4),
        in_specs=[SCALARS, *in_vmem(9), *anywhere(24)],
        out_specs=tuple(in_vmem(5)),
        scratch_shapes=[
            AO_HELD,
            AO_HELD,
            FC_HELD,
            PJ_HELD,
            pltpu.VMEM((FF, TOK), bf16),
            pltpu.VMEM((1024, TOK), bf16),
            pltpu.VMEM((D, TOK), f32),
            pltpu.SemaphoreType.DMA((4, 8)),
        ],
        compiler_params=params(),
        name="turn_part",
    )(here, stream, gains, grad_above, before, middle, *blocks, *pair_above, *pair, *pj)


def end_kernel(here, stream, gains, grad_middle, *refs):
    blocks, ao, out, (held, wide, grad, sems) = refs[0:4], refs[4:12], refs[12], refs[13:]
    wait = fetch_ao(here, ao, held, sems)
    begin(wait)
    back_qkv(here, blocks, held, wait, wide, stream, gains, 0, grad_middle, grad)
    out[...] = grad[...].T


def end_part(here, stream, gains, grad_middle, blocks, ao):
    return pl.pallas_call(
        end_kernel,
        out_shape=shape(TOK, D, dtype=f32),
        in_specs=[SCALARS, *in_vmem(7), *anywhere(8)],
        out_specs=pl.BlockSpec(memory_space=pltpu.VMEM),
        scratch_shapes=[AO_HELD, pltpu.VMEM((FF, TOK), bf16), pltpu.VMEM((D, TOK), f32), pltpu.SemaphoreType.DMA((8,))],
        compiler_params=params(),
        name="end_part",
    )(here, stream, gains, grad_middle, *blocks, *ao)


HALF = 256
every = slice(None)
EVERY_PIECE = [slice(TOK * n, TOK * n + TOK) for n in range(8)] + [slice(LENGTH, LENGTH + PAD)]
SEEN = ((0, 1, 4, 5, 8), (0, 1, 2, 3, 4, 5, 6, 7, 8))


def hide(here, spans, hidden):
    inside = lax.broadcasted_iota(jnp.int32, (TOK, HALF), 0)
    for part in range(2):
        cols = slice(part * HALF, part * HALF + HALF)
        low, high = spans[0:1, cols], spans[1:2, cols]
        for n in SEEN[part][:-1]:
            start = TOK * (2 * (n % 4) + (here[CORE] if n < 4 else 1 - here[CORE]))
            seen = (inside >= low - start) & (inside <= high - start)
            hidden[EVERY_PIECE[n], cols] = jnp.where(seen, 0.0, big_negative)
    real = lax.broadcasted_iota(jnp.int32, (PAD, 2 * HALF), 0) < PREFIX
    hidden[LENGTH:, :] = jnp.where(real, 0.0, big_negative)


def head_rows(held, n, t, h):
    return held[n // 4][n % 4, 192 * t + 64 * h : 192 * t + 64 * h + 64, :]


def keys_and_values(held, table, h):
    tall = []
    for n in range(8):
        both = jnp.concatenate([head_rows(held, n, 1, h), head_rows(held, n, 2, h)], axis=0)
        tall.append(both.astype(f32).T.astype(bf16))
    return [*tall, table[h]]


def turned_table(table):
    return [table[h].astype(f32).T.astype(bf16) for h in range(GROUP)]


def side_by_side(held, pieces, t, h):
    return jnp.concatenate([head_rows(held, n, t, h) for n in pieces], axis=1)


def stacked_rows(ref, pieces, cols):
    return jnp.concatenate([ref[EVERY_PIECE[n], cols] for n in pieces], axis=0)


def attend_kernel(here, spans, *refs):
    held, table, out, logs = refs[0:2], refs[2], refs[3], refs[4]
    hidden, scores, probs = refs[5:]
    table_t = turned_table(table)
    hide(here, spans, hidden)
    for h in range(GROUP):
        tall = keys_and_values(held, table, h)
        for part in range(2):
            cols = slice(part * HALF, part * HALF + HALF)
            pieces = SEEN[part]
            query = side_by_side(held, (2 * part, 2 * part + 1), 0, h) * bf16(0.125)
            right = jnp.concatenate([query, jnp.zeros_like(query)], axis=0)
            top = jnp.full((8, HALF), big_negative, f32)
            for n in pieces:
                block = jnp.dot(tall[n], right, preferred_element_type=f32) + hidden[EVERY_PIECE[n], cols]
                scores[EVERY_PIECE[n], :] = block
                top = jnp.maximum(top, jnp.max(block.reshape(-1, 8, HALF), axis=0))
            top = jnp.max(top, axis=0, keepdims=True)
            total = jnp.zeros((8, HALF), f32)
            for n in pieces:
                block = jnp.exp(scores[EVERY_PIECE[n], :] - top)
                scores[EVERY_PIECE[n], :] = block
                total = total + jnp.sum(block.reshape(-1, 8, HALF), axis=0)
            total = jnp.sum(total, axis=0, keepdims=True)
            share = 1.0 / total
            for n in pieces:
                probs[EVERY_PIECE[n], :] = (scores[EVERY_PIECE[n], :] * share).astype(bf16)
            result = jnp.dot(
                side_by_side(held, pieces[:-1], 2, h), stacked_rows(probs, pieces[:-1], every), preferred_element_type=f32
            )
            result = result + jnp.dot(table_t[h][64:, :], probs[LENGTH:, :], preferred_element_type=f32)
            for n in range(2):
                out[2 * part + n, 64 * h : 64 * h + 64, :] = result[:, TOK * n : TOK * n + TOK].astype(bf16)
            logs[h : h + 1, cols] = top + jnp.log(total)


def attend(here, spans, own, other, tables, layer, waits=()):
    def kernel(*refs):
        attend_kernel(*refs[:4], refs[4].at[layer], *refs[5 + len(waits) :])

    return pl.pallas_call(
        kernel,
        out_shape=(shape(4, 192, TOK), shape(8, 512, dtype=f32)),
        in_specs=[SCALARS, *in_vmem(4), *anywhere(len(waits))],
        out_specs=tuple(in_vmem(2)),
        scratch_shapes=[
            pltpu.VMEM((LENGTH + PAD, 2 * HALF), f32),
            pltpu.VMEM((LENGTH + PAD, HALF), f32),
            pltpu.VMEM((LENGTH + PAD, HALF), bf16),
        ],
        compiler_params=params(),
        name="attend",
    )(here, spans, own, other, tables, *waits)


def attend_back_kernel(here, spans, logs, *refs):
    held, blocks, table = refs[0:2], refs[2:6], refs[6]
    grad_query, mine, others, grad_table = refs[7:11]
    hidden, probs, slopes, packed, sums, grads = refs[11:]
    table_t = turned_table(table)
    for y in range(4):

        @pl.when(here[Y] == y)
        def _():
            for k in range(4):
                grads[(y + k) % 4] = blocks[k][...]

    hide(here, spans, hidden)
    for h in range(GROUP):
        tall = keys_and_values(held, table, h)
        for part in (1, 0):
            cols = slice(part * HALF, part * HALF + HALF)
            pieces = SEEN[part]
            query = side_by_side(held, (2 * part, 2 * part + 1), 0, h) * bf16(0.125)
            grad = jnp.concatenate([grads[2 * part + n, 64 * h : 64 * h + 64, :] for n in range(2)], axis=1)
            nothing = jnp.zeros_like(query)
            right = jnp.concatenate(
                [jnp.concatenate([query, nothing], axis=1), jnp.concatenate([nothing, grad], axis=1)], axis=0
            )
            right_t = right.astype(f32).T.astype(bf16)
            log_total = logs[h : h + 1, cols]
            inner = jnp.zeros((8, HALF), f32)
            for n in pieces:
                piece = EVERY_PIECE[n]
                both = jnp.dot(tall[n], right, preferred_element_type=f32)
                prob = jnp.exp(both[:, :HALF] + hidden[piece, cols] - log_total)
                slope = both[:, HALF:]
                probs[piece, :] = prob
                slopes[piece, :] = slope
                packed[piece, HALF:] = prob.astype(bf16)
                inner = inner + jnp.sum((prob * slope).reshape(-1, 8, HALF), axis=0)
            inner = jnp.sum(inner, axis=0, keepdims=True)
            for n in pieces:
                piece = EVERY_PIECE[n]
                packed[piece, :HALF] = (probs[piece, :] * (slopes[piece, :] - inner)).astype(bf16)
            result = jnp.dot(
                side_by_side(held, pieces[:-1], 1, h),
                stacked_rows(packed, pieces[:-1], slice(0, HALF)),
                preferred_element_type=f32,
            )
            result = result + jnp.dot(table_t[h][:64, :], packed[LENGTH:, :HALF], preferred_element_type=f32)
            grad_query[64 * h : 64 * h + 64, cols] = (result * 0.125).astype(bf16)
            for n in pieces:
                new = jnp.dot(packed[EVERY_PIECE[n], :], right_t, preferred_element_type=f32)
                sums[EVERY_PIECE[n], :] = new if part == 1 else sums[EVERY_PIECE[n], :] + new
        for n in range(4):
            mine[h, :, TOK * n : TOK * n + TOK] = sums[EVERY_PIECE[n], :].T
            others[h, :, TOK * n : TOK * n + TOK] = sums[EVERY_PIECE[4 + n], :].T.astype(bf16)
        grad_table[PREFIX * h : PREFIX * h + PREFIX, :] = sums[LENGTH : LENGTH + PREFIX, :]
    grad_table[GROUP * PREFIX :, :] = jnp.zeros((ROWS - GROUP * PREFIX, 128), f32)


def attend_back(here, spans, logs, own, other, grads, tables, layer):
    def kernel(*refs):
        attend_back_kernel(*refs[:9], refs[9].at[layer], *refs[10:])

    return pl.pallas_call(
        kernel,
        out_shape=(
            shape(192, 512),
            shape(GROUP, 128, 512, dtype=f32),
            shape(GROUP, 128, 512),
            shape(ROWS, 128, dtype=f32),
        ),
        in_specs=[SCALARS, *in_vmem(9)],
        out_specs=tuple(in_vmem(4)),
        scratch_shapes=[
            pltpu.VMEM((LENGTH + PAD, 2 * HALF), f32),
            pltpu.VMEM((LENGTH + PAD, HALF), f32),
            pltpu.VMEM((LENGTH + PAD, HALF), f32),
            pltpu.VMEM((LENGTH + PAD, 2 * HALF), bf16),
            pltpu.VMEM((LENGTH + PAD, 128), f32),
            pltpu.VMEM((4, 192, TOK), bf16),
        ],
        compiler_params=params(),
        name="attend_back",
    )(here, spans, logs, own, other, *grads, tables)


def pack_back_kernel(here, grad_query, mine, got, *refs):
    outs = refs[-4:]
    for y in range(4):

        @pl.when(here[Y] == y)
        def _():
            for k in range(4):
                start = TOK * ((y + k) % 4)
                cols = slice(start, start + TOK)
                outs[k][0:192, :] = grad_query[:, cols]
                for h in range(GROUP):
                    both = (mine[h, :, cols] + got[h, :, cols].astype(f32)).astype(bf16)
                    outs[k][192 + 64 * h : 256 + 64 * h, :] = both[:64, :]
                    outs[k][384 + 64 * h : 448 + 64 * h, :] = both[64:, :]


def pack_tables_kernel(here, grad_query, mine, got, *refs):
    tables, spread = refs[: 2 * LAYERS], refs[2 * LAYERS]
    pack_back_kernel(here, grad_query, mine, got, *refs[2 * LAYERS + 1 :])
    whole = jnp.concatenate([tables[2 * n][...] + tables[2 * n + 1][...] for n in range(LAYERS)], axis=0).astype(bf16)
    for n in range(64):
        spread[n] = whole


def pack_back(here, grad_query, mine, got, tables=()):
    spread = [shape(64, LAYERS * ROWS, 128)] if tables else []
    return pl.pallas_call(
        pack_tables_kernel if tables else pack_back_kernel,
        out_shape=(*spread, *[shape(576, TOK)] * 4),
        in_specs=[SCALARS, *in_vmem(3 + len(tables))],
        out_specs=tuple(in_vmem(4 + len(spread))),
        compiler_params=params(),
        name="pack_back",
    )(here, grad_query, mine, got, *tables)


def split(value):
    high = value.astype(bf16)
    return high, (value - high.astype(f32)).astype(bf16)


def products(left, right, dims):
    total = None
    for a, b in ((1, 0), (0, 1), (0, 0)):
        term = lax.dot_general(left[a], right[b], (dims, ((), ())), preferred_element_type=f32)
        total = term if total is None else total + term
    return total


PLAIN, TURNED = ((1,), (0,)), ((1,), (1,))


def prepare_kernel(
    here, layout_own, layout_other, table, matrix_in, bias_in, matrix_out, bias_out, gain, offset, tables, hidden, spans, gains, flat
):
    flat[:PREFIX, :D] = table[...]
    flat[PREFIX:, :D] = jnp.zeros((PAD - PREFIX, D), f32)
    inner = products(split(flat[:, :D]), split(matrix_in[...]), PLAIN) + bias_in[...]
    real = lax.broadcasted_iota(jnp.int32, (PAD, 512), 0) < PREFIX
    hidden[...] = jnp.where(real, jnp.tanh(inner), 0.0)
    parts = split(hidden[...])
    for n in range(6):
        cols = slice(512 * n, 512 * n + 512)
        flat[:, cols] = products(parts, split(matrix_out[:, cols]), PLAIN) + bias_out[:, cols]
    real = lax.broadcasted_iota(jnp.int32, (PAD, 2 * HD), 0) < PREFIX
    for y in range(SIDE):

        @pl.when(here[Y] == y)
        def _():
            for layer in range(LAYERS):
                for h in range(GROUP):
                    at = layer * 2 * D + (GROUP * y + h) * HD
                    both = jnp.concatenate([flat[:, at : at + HD], flat[:, at + D : at + D + HD]], axis=1)
                    tables[layer, h] = jnp.where(real, both, 0.0).astype(bf16)

    lane = lax.broadcasted_iota(jnp.int32, (8, 4 * TOK), 1)
    places = lane + TOK * (lax.div(lane, TOK) + here[CORE])
    own = here[4] == here[CORE]
    end = jnp.int32(0)
    starts = jnp.zeros((8, 4 * TOK), jnp.int32)
    for n in range(8):
        end = end + jnp.where(own, layout_own[n], layout_other[n])
        starts = jnp.where(places >= end, end, starts)
    living = LENGTH - jnp.where(own, layout_own[8], layout_other[8])
    starts = jnp.where(places < living, starts, 4 * LENGTH)
    spans[0:1, :] = starts[0:1, :]
    spans[1:2, :] = places[0:1, :]
    rows = [ref[layer, which : which + 1, :] for layer in range(LAYERS) for which in range(2) for ref in (gain, offset)]
    gains[...] = jnp.concatenate(rows, axis=0).T


def prepare(here, layout_own, layout_other, table, matrix_in, bias_in, matrix_out, bias_out, gain, offset):
    return pl.pallas_call(
        prepare_kernel,
        out_shape=(
            shape(LAYERS, GROUP, PAD, 2 * HD),
            shape(PAD, 512, dtype=f32),
            shape(2, 4 * TOK, dtype=jnp.int32),
            shape(D, 8, dtype=f32),
        ),
        in_specs=[SCALARS] * 3 + in_vmem(7),
        out_specs=tuple(in_vmem(4)),
        scratch_shapes=[pltpu.VMEM((PAD, 2 * LAYERS * D), f32)],
        compiler_params=params(),
        name="prepare",
    )(here, layout_own, layout_other, table, matrix_in, bias_in[None], matrix_out, bias_out[None], gain, offset)


def chain_kernel(hidden, hidden_t, table_t, matrix_in, matrix_out, parts, g_table, g_in, g_in_bias, g_out, g_out_bias, *scratch):
    grads, held_out, new_out, held_in, sems = scratch
    chunks = [slice(512 * n, 512 * n + 512) for n in range(6)]
    reads = [pltpu.make_async_copy(matrix_out.at[:, c], held_out.at[:, c], sems.at[n]) for n, c in enumerate(chunks)]
    reads.append(pltpu.make_async_copy(matrix_in, held_in, sems.at[6]))
    writes = [pltpu.make_async_copy(new_out.at[:, c], g_out.at[:, c], sems.at[7 + n]) for n, c in enumerate(chunks)]
    begin(reads)
    grads[...] = jnp.zeros_like(grads)
    for y in range(SIDE):
        total = jnp.zeros((LAYERS * ROWS, 128), f32)
        for z in range(4):
            for xl in range(2):
                for xh in range(2):
                    total = total + parts[((z * 2 + xl) * 4 + y) * 2 + xh].astype(f32)
        for layer in range(LAYERS):
            for h in range(GROUP):
                first_row = ROWS * layer + PREFIX * h
                rows = total[first_row : first_row + PREFIX, :]
                at = layer * 2 * D + (GROUP * y + h) * HD
                grads[:PREFIX, at : at + HD] = rows[:, :HD]
                grads[:PREFIX, at + D : at + D + HD] = rows[:, HD:]
    g_out_bias[...] = jnp.sum(grads[...], axis=0, keepdims=True)
    hidden_parts = split(hidden_t[...])
    some = [split(grads[:, cols]) for cols in chunks]
    for n, cols in enumerate(chunks):
        new_out[:, cols] = products(hidden_parts, some[n], PLAIN)
        writes[n].start()
    slope = jnp.zeros((PAD, 512), f32)
    for n, cols in enumerate(chunks):
        reads[n].wait()
        slope = slope + products(some[n], split(held_out[:, cols]), TURNED)
    slope = slope * (1.0 - hidden[...] * hidden[...])
    g_in_bias[...] = jnp.sum(slope, axis=0, keepdims=True)
    parts_of_slope = split(slope)
    g_in[...] = products(split(table_t[...]), parts_of_slope, PLAIN)
    reads[6].wait()
    g_table[...] = products(parts_of_slope, split(held_in[...]), TURNED)[:PREFIX, :]
    finish(writes)


def chain(hidden, table, matrix_in, matrix_out, parts):
    g_table, g_in, g_in_bias, g_out, g_out_bias = pl.pallas_call(
        chain_kernel,
        out_shape=(
            shape(PREFIX, D, dtype=f32),
            shape(D, 512, dtype=f32),
            shape(1, 512, dtype=f32),
            shape(512, 2 * LAYERS * D, dtype=f32),
            shape(1, 2 * LAYERS * D, dtype=f32),
        ),
        in_specs=[*in_vmem(3), *anywhere(2), *in_vmem(1)],
        out_specs=(*in_vmem(3), *anywhere(1), *in_vmem(1)),
        scratch_shapes=[
            pltpu.VMEM((PAD, 2 * LAYERS * D), f32),
            pltpu.VMEM((512, 2 * LAYERS * D), f32),
            pltpu.VMEM((512, 2 * LAYERS * D), f32),
            pltpu.VMEM((D, 512), f32),
            pltpu.SemaphoreType.DMA((13,)),
        ],
        compiler_params=params(),
        name="chain",
    )(hidden, hidden.T, table.T, matrix_in, matrix_out, parts)
    return g_table, g_in, g_in_bias[0], g_out, g_out_bias[0]


def start_weights(here, attn_weight, out_weight, fc_weight, proj_weight, waits):
    core = here[CORE]
    turned = jnp.swapaxes(proj_weight, 1, 2)
    mine = lax.dynamic_slice_in_dim(turned, 48 * core, 48, axis=1)
    theirs = lax.dynamic_slice_in_dim(turned, 48 * (1 - core), 48, axis=1)
    ao = jnp.concatenate([attn_weight, out_weight], axis=2)
    kept, given = jnp.where(core == 0, ao, fc_weight), jnp.where(core == 0, fc_weight, ao)
    got = move(given, core_pairs())
    pair = jnp.where(core == 0, jnp.stack([kept, got]), jnp.stack([got, kept]))
    got = move(theirs, core_pairs())
    pj = jnp.where(core == 0, jnp.concatenate([mine, got], axis=2), jnp.concatenate([got, mine], axis=2))
    pair, pj = assemble(
        here,
        None,
        [
            (around_two(pair, X, Y), shape(2, 4, 48, 768), put_pair_one),
            (around(pj, Z), shape(2, 48, 1536), put_proj_one),
        ],
        waits,
    )
    return around_two(pair, Y, Z), around(pj, X)


def both_cores(blocks):
    return [*blocks, *[move(b, core_pairs()) for b in blocks]]


def rest_of_weights(here, pair, proj, others):
    pair_whole, proj_whole = shape(4, 48, 3072), shape(2, 48, 3072)
    (whole,) = assemble(here, 0, [(pair, pair_whole, put_pair_two)], (*proj[1:], *others))
    pair_zero = around_two(whole, Z, X)
    (whole,) = assemble(here, 0, [(proj, proj_whole, put_proj_two)], (whole,))
    proj_zero = around(whole, Y)
    whole, whole_proj = assemble(
        here, 1, [(pair, pair_whole, put_pair_two), (proj, proj_whole, put_proj_two)], (*pair_zero[1:], *proj_zero[1:])
    )
    near = [whole_proj, move(whole_proj, ring(Y, 1)), move(whole_proj, ring(Y, 3))]
    return both_cores(pair_zero), both_cores(proj_zero), both_cores(around_two(whole, Z, X)), near


def last_of_weights(here, proj, near, waits):
    (whole,) = assemble(here, 1, [(proj, shape(2, 48, 3072), put_proj_two)], waits)
    own, ahead, behind = near
    return both_cores([own, ahead, move(whole, ring(Y, 2)), behind])


def on_device(
    states_in,
    attn_weight,
    out_weight,
    fc_weight,
    proj_weight,
    norm_gain,
    norm_shift,
    prefix_table,
    reparam_in,
    reparam_in_bias,
    reparam_out,
    reparam_out_bias,
    doc_lengths,
    pad_counts,
    states_grad,
):
    z, xl, core, y, xh = (lax.axis_index(name) for name in AXES)
    here = jnp.stack([z, 2 * xh + xl, core, y, xh]).astype(jnp.int32)
    x = move(states_in[0], seat_pairs())
    grad_in = move(states_grad[0], seat_pairs())
    layout = jnp.concatenate([doc_lengths[0], pad_counts])
    pair, proj = start_weights(here, attn_weight, out_weight, fc_weight, proj_weight, ())
    tables, hidden, spans, gains = prepare(
        here,
        layout,
        move(layout, core_pairs()),
        prefix_table,
        reparam_in,
        reparam_in_bias,
        reparam_out,
        reparam_out_bias,
        norm_gain,
        norm_shift,
    )
    table = jnp.pad(prefix_table, ((0, PAD - PREFIX), (0, 0)))
    pair_zero, proj_zero, pair_one, near = rest_of_weights(here, pair, proj, (tables, spans, gains, x, grad_in))
    stream, sends = first(here, x, gains, pair_zero, (spans, tables))
    arrived = [(*pair_one[1:4], *near[1:]), ()]
    streams = [stream]
    kept = []
    for layer in range(LAYERS):
        own = swap_on_ring(sends)
        other = move(own, core_pairs())
        if layer == 0:
            proj_one = last_of_weights(here, proj, near, (own,))
        mixed, logs = attend(here, spans, own, other, tables, layer, arrived[layer])
        mixed = swap_on_ring(mixed)
        kept.append((own, other, logs))
        if layer == 0:
            middle, before, stream, sends = middle_part(here, stream, gains, mixed, pair_zero, proj_zero, pair_one, (proj_one[2],))
            streams.append(stream)
        else:
            final, grad_middle, *sends = last_part(here, stream, gains, mixed, grad_in, pair_one, proj_one)
    final = move(final, seat_pairs())

    tables_back = ()
    for layer in reversed(range(LAYERS)):
        own, other, logs = kept[layer]
        grads = to_places(sends)
        grad_query, mine, theirs, grad_table = attend_back(here, spans, logs, own, other, grads, tables, layer)
        tables_back = (grad_table, move(grad_table, core_pairs()), *tables_back)
        theirs = move(theirs, core_pairs())
        *spread, b0, b1, b2, b3 = pack_back(here, grad_query, mine, theirs, () if layer else tables_back)
        back = to_places([b0, b1, b2, b3])
        if layer == 1:
            grad_middle, *sends = turn_part(
                here, streams[1], gains, grad_middle, before, middle, back, pair_one, pair_zero, proj_zero
            )
        else:
            grad_states = end_part(here, streams[0], gains, grad_middle, back, pair_zero)
    grad_states = move(grad_states, seat_pairs())
    shared = lax.all_to_all(spread[0], ("z", "xl", "y", "xh"), 0, 0, tiled=True)

    return (final[None], grad_states[None], *chain(hidden, table, reparam_in, reparam_out, shared))


def solution(mesh):
    grid = Mesh(mesh.devices.reshape(GRID), AXES)
    rows, cols = ("z", "xl", "core"), ("y", "xh")
    return jax.shard_map(
        on_device,
        mesh=grid,
        in_specs=(
            P(rows, cols, None),
            P(None, rows, cols),
            P(None, rows, cols),
            P(None, rows, cols),
            P(None, rows, cols),
            P(),
            P(),
            P(),
            P(),
            P(),
            P(),
            P(),
            P(rows, None),
            P(rows),
            P(rows, cols, None),
        ),
        out_specs=(P(rows, cols, None), P(rows, cols, None), P(), P(), P(), P(), P()),
        check_vma=False,
    )
```

```python
import jax
import jax.numpy as jnp
from jax import lax
from jax.experimental import pallas as pl
from jax.experimental.pallas import tpu as pltpu
from jax.sharding import Mesh
from jax.sharding import PartitionSpec as P

D = 768
H = 12
HD = 64
FF = 3072
LENGTH = 1024
PREFIX = 10
LAYERS = 2
TOK = 128
PAD = 16
GROUP = 3
ROWS = 32
SIDE = 4
AXES = ("z", "xl", "core", "y", "xh")
GRID = (4, 2, 2, 4, 2)

epsilon = 1e-05
highest = lax.Precision.HIGHEST
big_negative = -1e30
bf16 = jnp.bfloat16
f32 = jnp.float32


def index_of(z, x, core, y):
    return (((z * 2 + x % 2) * 2 + core) * 4 + y) * 2 + x // 2


def everywhere():
    return [(z, x, c, y) for z in range(4) for x in range(4) for c in range(2) for y in range(4)]


def ring(axis, ahead):
    pairs = []
    for spot in everywhere():
        source = list(spot)
        source[axis] = (source[axis] + ahead) % 4
        pairs.append((index_of(*source), index_of(*spot)))
    return pairs


def two_rings(axis_zero, axis_one, ahead):
    pairs = []
    for spot in everywhere():
        source = list(spot)
        axis = axis_one if spot[CORE] else axis_zero
        source[axis] = (source[axis] + ahead) % 4
        pairs.append((index_of(*source), index_of(*spot)))
    return pairs


def core_pairs():
    return [(index_of(z, x, 1 - c, y), index_of(z, x, c, y)) for z, x, c, y in everywhere()]


def seat_pairs():
    return [(index_of(z, c * 2 + x % 2, x // 2, y), index_of(z, x, c, y)) for z, x, c, y in everywhere()]


Z, X, CORE, Y = 0, 1, 2, 3


def move(value, pairs):
    return lax.ppermute(value, AXES, pairs)


def around(value, axis):
    return [value] + [move(value, ring(axis, k)) for k in (1, 2, 3)]


def around_two(value, axis_zero, axis_one):
    return [value] + [move(value, two_rings(axis_zero, axis_one, k)) for k in (1, 2, 3)]


def to_places(blocks):
    got = [None, *[move(blocks[k], ring(Y, -k)) for k in (1, 2, 3)]]
    return [blocks[0], got[3], got[2], got[1]]


def swap_on_ring(blocks):
    return lax.all_to_all(blocks, "y", 0, 0, tiled=True)


def wrap(value):
    return lax.rem(value, SIDE)


def params(limit):
    return pltpu.CompilerParams(vmem_limit_bytes=limit * 2**20)


def anywhere(count):
    return [pl.BlockSpec(memory_space=pl.ANY)] * count


def in_vmem(count):
    return [pl.BlockSpec(memory_space=pltpu.VMEM)] * count


SCALARS = pl.BlockSpec(memory_space=pltpu.SMEM)


def shape(*dims, dtype=bf16):
    return jax.ShapeDtypeStruct(dims, dtype)


def lanes(start, size):
    return pl.ds(pl.multiple_of(start, 128), size)


def block_of(layer, dims):
    if layer is None:
        return pl.BlockSpec(dims, lambda i: (0,) * len(dims))
    return pl.BlockSpec((None, *dims[1:]), lambda i: (layer,) + (0,) * (len(dims) - 1))


def assemble(here, layer, groups, waits=()):
    count = len(groups)

    def kernel(here, *refs):
        for n, (_, _, put) in enumerate(groups):
            for k in range(4):
                put(here, k, refs[4 * n + k], refs[n - count])

    blocks = [b for group in groups for b in group[0]]
    outs = [group[1] for group in groups]
    return pl.pallas_call(
        kernel,
        grid=(1,),
        out_shape=outs,
        in_specs=[SCALARS, *[block_of(layer, b.shape) for b in blocks], *anywhere(len(waits))],
        out_specs=[block_of(None, out.shape) for out in outs],
        compiler_params=params(16),
        name="assemble",
    )(here, *blocks, *waits)


def pick(here, zero, one):
    return jnp.where(here[CORE] == 0, zero, one)


def put_pair_one(here, k, block, result):
    place = wrap(pick(here, here[X], here[Y]) + k)
    low, high = lax.rem(place, 2), lax.div(place, 2)
    for c in range(2):
        row, col = pick(here, 2 * low + c, 2 * c + high), pick(here, high, low)
        result[:, row, :, lanes(384 * col, 384)] = block[c]


def put_pair_two(here, k, block, result):
    place = wrap(pick(here, here[Y], here[Z]) + k)
    for i in range(4):
        result[pick(here, i, place), :, lanes(768 * pick(here, place, i), 768)] = block[i]


def put_proj_one(here, k, block, result):
    result[:, :, lanes(384 * wrap(here[Z] + k), 384)] = block[...]


def put_proj_two(here, k, block, result):
    place = wrap(here[X] + k)
    result[lax.div(place, 2), :, lanes(1536 * lax.rem(place, 2), 1536)] = block[...]


AO_HELD = pltpu.VMEM((4, 4, 48, 3072), bf16)
FC_HELD = pltpu.VMEM((2, 4, 2, 2, 48, 1536), bf16)
PJ_HELD = pltpu.VMEM((4, 2, 2, 48, 3072), bf16)


class Chosen:
    def __init__(self, here, zero, one, target, sem):
        self.here = here
        self.copies = [pltpu.make_async_copy(source, target, sem) for source in (zero, one)]

    def start(self):
        for core in range(2):
            pl.when(self.here[CORE] == core)(self.copies[core].start)

    def wait(self):
        self.copies[0].wait()


def fetch_ao(here, refs, held, sems):
    return [Chosen(here, refs[k], refs[4 + k], held.at[wrap(here[Z] + k)], sems.at[k]) for k in range(4)]


def fetch_fc(here, refs, held, sems):
    copies = []
    for k in range(4):
        there = wrap(here[X] + k)
        for c in range(2):
            target = held.at[lax.div(there, 2), :, lax.rem(there, 2), c]
            cols = slice(1536 * c, 1536 * c + 1536)
            copies.append(Chosen(here, refs[4 + k].at[:, :, cols], refs[k].at[:, :, cols], target, sems.at[2 * k + c]))
    return copies


def fetch_pj(here, refs, held, sems):
    cores = (here[CORE], 1 - here[CORE])
    return [pltpu.make_async_copy(refs[n], held.at[:, :, core], sems.at[n]) for n, core in enumerate(cores)]


def begin(copies):
    for one in copies:
        one.start()


def finish(copies):
    for one in copies:
        one.wait()


def flipped(value):
    return value.astype(f32).T


def norm_stats(stream):
    centre = jnp.mean(stream, axis=0, keepdims=True)
    centred = stream - centre
    spread = jnp.mean(centred * centred, axis=0, keepdims=True)
    return centred, lax.rsqrt(spread + epsilon)


def norm(stream, gain, shift):
    centred, rate = norm_stats(stream)
    return centred * rate * gain + shift


def norm_back(stream, gain, grad):
    centred, rate = norm_stats(stream)
    unit = centred * rate
    scaled = grad * gain
    inner = jnp.mean(scaled * unit, axis=0, keepdims=True)
    return rate * (scaled - jnp.mean(scaled, axis=0, keepdims=True) - unit * inner)


root = 0.7978845608028654


def gate(u):
    return 0.5 * u * (1.0 + jnp.tanh(root * (u + 0.044715 * (u * u * u))))


def gate_slope(u):
    squared = u * u
    t = jnp.tanh(root * (u + 0.044715 * (squared * u)))
    return 0.5 * (1.0 + t) + (0.5 * root) * u * (1.0 - t * t) * (1.0 + (3.0 * 0.044715) * squared)


def column(gains, layer, which, part):
    at = layer * 4 + which * 2 + part
    return gains[:, at : at + 1]


def rows_of_place(place):
    pieces = []
    for t in range(3):
        for u in range(2):
            piece = 8 * t + 2 * place + u
            pieces.append((384 * (piece // 3) + 96 * (piece % 3), t * 192 + u * 96))
    return pieces


def send_qkv(here, stream, gains, layer, held, wide, sends):
    normed = norm(stream, column(gains, layer, 0, 0), column(gains, layer, 0, 1)).T.astype(bf16)
    for j in range(4):
        cols = slice(768 * j, 768 * j + 768)
        packed = jnp.dot(normed, held[:, :, :, cols].reshape(D, 768), preferred_element_type=f32)
        wide[cols, :] = packed.T.astype(bf16)
    for place in range(4):
        for row, at in rows_of_place(place):
            sends[place, at : at + 96, :] = wide[row : row + 96, :]


def first_kernel(here, x_ref, gains, *refs):
    ao, (stream, sends), (held, wide, sems) = refs[0:8], refs[8:10], refs[10:]
    copies = fetch_ao(here, ao, held, sems)
    begin(copies)
    stream[...] = flipped(x_ref[...])
    finish(copies)
    send_qkv(here, stream[...], gains, 0, held, wide, sends)


def first(here, x, gains, ao, waits):
    def kernel(*refs):
        first_kernel(*refs[:11], *refs[11 + len(waits) :])

    return pl.pallas_call(
        kernel,
        out_shape=(shape(D, TOK, dtype=f32), shape(4, 576, TOK)),
        in_specs=[SCALARS, *in_vmem(2), *anywhere(8 + len(waits))],
        out_specs=tuple(in_vmem(2)),
        scratch_shapes=[AO_HELD, pltpu.VMEM((FF, TOK), bf16), pltpu.SemaphoreType.DMA((8,))],
        compiler_params=params(24),
        name="first",
    )(here, x, gains, *ao, *waits)


def after_attention(here, stream, mixed, gains, layer, ao_held, fc_held, pj_held, waits, act, before, middle, result):
    rows = flipped(mixed[...].reshape(D, TOK)).astype(bf16)
    finish(waits[0])

    weight = jnp.concatenate([ao_held[:, :, :, 384 * j + 256 : 384 * j + 384].reshape(D, 128) for j in range(8)], axis=1)
    part = jnp.dot(rows, weight, preferred_element_type=f32).T
    for j in range(8):
        at = slice(96 * j, 96 * j + 96)
        middle[at, :] = stream[at, :] + part[128 * j + 32 : 128 * j + 128, :]
    normed = norm(middle[...], column(gains, layer, 1, 0), column(gains, layer, 1, 1)).T.astype(bf16)
    finish(waits[1])

    for n in range(4):
        low = 768 * (n % 2)
        weight = fc_held[n // 2, :, :, :, :, low : low + 768].reshape(D, 768)
        inputs = jnp.dot(normed, weight, preferred_element_type=f32)
        before[n] = inputs
        act[768 * n : 768 * n + 768, :] = gate(inputs).T.astype(bf16)
    finish(waits[2])
    for n in range(2):
        at = slice(384 * n, 384 * n + 384)
        weight = pj_held[2 * n : 2 * n + 2].reshape(384, FF)
        result[at, :] = middle[at, :] + jnp.dot(weight, act[...], preferred_element_type=f32)


def middle_kernel(here, stream, gains, *refs):
    mixed, pair, pj, pair_next = refs[0], refs[1:9], refs[9:11], refs[11:19]
    middle, before, result, sends = refs[19:23]
    ao_held, fc_held, pj_held, next_held, act, sems = refs[23:]
    waits = [
        fetch_ao(here, pair, ao_held, sems.at[0]),
        fetch_fc(here, pair, fc_held, sems.at[1]),
        fetch_pj(here, pj, pj_held, sems.at[2]),
        fetch_ao(here, pair_next, next_held, sems.at[3]),
    ]
    for copies in waits:
        begin(copies)
    after_attention(here, stream, mixed, gains, 0, ao_held, fc_held, pj_held, waits, act, before, middle, result)
    finish(waits[3])
    send_qkv(here, result[...], gains, 1, next_held, act, sends)


def middle_part(here, stream, gains, mixed, pair, pj, pair_next, waits):
    def kernel(*refs):
        middle_kernel(*refs[:22], *refs[22 + len(waits) :])

    return pl.pallas_call(
        kernel,
        out_shape=(shape(D, TOK, dtype=f32), shape(4, TOK, 768, dtype=f32), shape(D, TOK, dtype=f32), shape(4, 576, TOK)),
        in_specs=[SCALARS, *in_vmem(3), *anywhere(18 + len(waits))],
        out_specs=tuple(in_vmem(4)),
        scratch_shapes=[
            AO_HELD,
            FC_HELD,
            PJ_HELD,
            AO_HELD,
            pltpu.VMEM((FF, TOK), bf16),
            pltpu.SemaphoreType.DMA((4, 8)),
        ],
        compiler_params=params(56),
        name="middle_part",
    )(here, stream, gains, mixed, *pair, *pj, *pair_next, *waits)


def back_feed(here, grad, before, middle, gains, layer, ao_held, fc_held, pj_held, waits, act, spread, grad_middle, sends):
    rows = grad[...].T.astype(bf16)
    finish(waits[2])

    for n in range(4):
        cols = slice(768 * n, 768 * n + 768)
        grad_act = jnp.dot(rows, pj_held[:, :, :, :, cols].reshape(D, 768), preferred_element_type=f32)
        act[cols, :] = (gate_slope(before[n]) * grad_act).T.astype(bf16)
    finish(waits[1])
    for n in range(2):
        low = jnp.dot(fc_held[0, 2 * n : 2 * n + 2].reshape(384, 1536), act[:1536, :], preferred_element_type=f32)
        high = jnp.dot(fc_held[1, 2 * n : 2 * n + 2].reshape(384, 1536), act[1536:, :], preferred_element_type=f32)
        grad_middle[384 * n : 384 * n + 384, :] = low + high
    total = grad[...] + norm_back(middle[...], column(gains, layer, 1, 0), grad_middle[...])
    grad_middle[...] = total
    rounded = total.astype(bf16)
    for j in range(8):
        spread[128 * j : 128 * j + 32, :] = jnp.zeros((32, TOK), bf16)
        spread[128 * j + 32 : 128 * j + 128, :] = rounded[96 * j : 96 * j + 96, :]
    finish(waits[0])

    weight = jnp.concatenate([ao_held[:, :, :, 384 * j + 256 : 384 * j + 384].reshape(D, 128) for j in range(8)], axis=1)
    whole = jnp.dot(weight, spread[...], preferred_element_type=f32).astype(bf16)
    for y in range(4):

        @pl.when(here[Y] == y)
        def _():
            for k in range(4):
                row = 192 * ((y + k) % 4)
                sends[k][...] = whole[row : row + 192, :]


def last_kernel(here, stream, gains, *refs):
    mixed, grad_in, pair, pj = refs[0], refs[1], refs[2:10], refs[10:12]
    final, grad_middle, *sends = refs[12:18]
    ao_held, fc_held, pj_held, act, spread, before, middle, result, sems = refs[18:]
    waits = [
        fetch_ao(here, pair, ao_held, sems.at[0]),
        fetch_fc(here, pair, fc_held, sems.at[1]),
        fetch_pj(here, pj, pj_held, sems.at[2]),
    ]
    for copies in waits:
        begin(copies)
    after_attention(here, stream, mixed, gains, 1, ao_held, fc_held, pj_held, waits, act, before, middle, result)
    final[...] = result[...].T
    result[...] = flipped(grad_in[...])
    back_feed(here, result, before, middle, gains, 1, ao_held, fc_held, pj_held, [[], [], []], act, spread, grad_middle, sends)


def last_part(here, stream, gains, mixed, grad_in, pair, pj):
    return pl.pallas_call(
        last_kernel,
        out_shape=(shape(TOK, D, dtype=f32), shape(D, TOK, dtype=f32), *[shape(192, TOK)] * 4),
        in_specs=[SCALARS, *in_vmem(4), *anywhere(10)],
        out_specs=tuple(in_vmem(6)),
        scratch_shapes=[
            AO_HELD,
            FC_HELD,
            PJ_HELD,
            pltpu.VMEM((FF, TOK), bf16),
            pltpu.VMEM((1024, TOK), bf16),
            pltpu.VMEM((4, TOK, 768), f32),
            pltpu.VMEM((D, TOK), f32),
            pltpu.VMEM((D, TOK), f32),
            pltpu.SemaphoreType.DMA((3, 8)),
        ],
        compiler_params=params(40),
        name="last_part",
    )(here, stream, gains, mixed, grad_in, *pair, *pj)


def back_qkv(here, blocks, held, wait, wide, stream, gains, layer, grad_middle, result):
    for j in range(8):
        wide[384 * j + 288 : 384 * j + 384, :] = jnp.zeros((96, TOK), bf16)
    for y in range(4):

        @pl.when(here[Y] == y)
        def _():
            for k in range(4):
                for row, at in rows_of_place((y + k) % 4):
                    wide[row : row + 96, :] = blocks[k][at : at + 96, :]

    finish(wait)

    for n in range(2):
        weight = held[2 * n : 2 * n + 2].reshape(384, 3072)
        result[384 * n : 384 * n + 384, :] = jnp.dot(weight, wide[...], preferred_element_type=f32)
    result[...] = grad_middle[...] + norm_back(stream[...], column(gains, layer, 0, 0), result[...])


def turn_kernel(here, stream, gains, grad_above, before, middle, *refs):
    blocks, pair_above, pair, pj = refs[0:4], refs[4:12], refs[12:20], refs[20:22]
    grad_middle, *sends = refs[22:27]
    above_held, ao_held, fc_held, pj_held, act, spread, grad, sems = refs[27:]
    waits = [
        fetch_ao(here, pair_above, above_held, sems.at[0]),
        fetch_pj(here, pj, pj_held, sems.at[3]),
        fetch_fc(here, pair, fc_held, sems.at[2]),
        fetch_ao(here, pair, ao_held, sems.at[1]),
    ]
    for copies in waits:
        begin(copies)
    back_qkv(here, blocks, above_held, waits[0], act, stream, gains, 1, grad_above, grad)
    back_feed(here, grad, before, middle, gains, 0, ao_held, fc_held, pj_held, [waits[3], waits[2], waits[1]], act, spread, grad_middle, sends)


def turn_part(here, stream, gains, grad_above, before, middle, blocks, pair_above, pair, pj, waits):
    def kernel(*refs):
        turn_kernel(*refs[:28], *refs[28 + len(waits) :])

    return pl.pallas_call(
        kernel,
        out_shape=(shape(D, TOK, dtype=f32), *[shape(192, TOK)] * 4),
        in_specs=[SCALARS, *in_vmem(9), *anywhere(18 + len(waits))],
        out_specs=tuple(in_vmem(5)),
        scratch_shapes=[
            AO_HELD,
            AO_HELD,
            FC_HELD,
            PJ_HELD,
            pltpu.VMEM((FF, TOK), bf16),
            pltpu.VMEM((1024, TOK), bf16),
            pltpu.VMEM((D, TOK), f32),
            pltpu.SemaphoreType.DMA((4, 8)),
        ],
        compiler_params=params(44),
        name="turn_part",
    )(here, stream, gains, grad_above, before, middle, *blocks, *pair_above, *pair, *pj, *waits)


def end_kernel(here, stream, gains, grad_middle, *refs):
    blocks, ao, out, (held, wide, grad, sems) = refs[0:4], refs[4:12], refs[12], refs[13:]
    wait = fetch_ao(here, ao, held, sems)
    begin(wait)
    back_qkv(here, blocks, held, wait, wide, stream, gains, 0, grad_middle, grad)
    out[...] = grad[...].T


def end_part(here, stream, gains, grad_middle, blocks, ao, waits):
    def kernel(*refs):
        end_kernel(*refs[:16], *refs[16 + len(waits) :])

    return pl.pallas_call(
        kernel,
        out_shape=shape(TOK, D, dtype=f32),
        in_specs=[SCALARS, *in_vmem(7), *anywhere(8 + len(waits))],
        out_specs=pl.BlockSpec(memory_space=pltpu.VMEM),
        scratch_shapes=[AO_HELD, pltpu.VMEM((FF, TOK), bf16), pltpu.VMEM((D, TOK), f32), pltpu.SemaphoreType.DMA((8,))],
        compiler_params=params(56),
        name="end_part",
    )(here, stream, gains, grad_middle, *blocks, *ao, *waits)


HALF = 256
every = slice(None)
EVERY_PIECE = [slice(TOK * n, TOK * n + TOK) for n in range(8)] + [slice(LENGTH, LENGTH + PAD)]
SEEN = ((0, 1, 4, 5, 8), (0, 1, 2, 3, 4, 5, 6, 7, 8))


def hide(here, spans, hidden):
    inside = lax.broadcasted_iota(jnp.int32, (TOK, HALF), 0)
    for part in range(2):
        cols = slice(part * HALF, part * HALF + HALF)
        low, high = spans[0:1, cols], spans[1:2, cols]
        for n in SEEN[part][:-1]:
            start = TOK * (2 * (n % 4) + (here[CORE] if n < 4 else 1 - here[CORE]))
            seen = (inside >= low - start) & (inside <= high - start)
            hidden[EVERY_PIECE[n], cols] = jnp.where(seen, 0.0, big_negative)
    real = lax.broadcasted_iota(jnp.int32, (PAD, 2 * HALF), 0) < PREFIX
    hidden[LENGTH:, :] = jnp.where(real, 0.0, big_negative)


def head_rows(held, n, t, h):
    return held[n // 4][n % 4, 192 * t + 64 * h : 192 * t + 64 * h + 64, :]


def keys_and_values(held, table, h):
    tall = []
    for n in range(8):
        both = jnp.concatenate([head_rows(held, n, 1, h), head_rows(held, n, 2, h)], axis=0)
        tall.append(both.astype(f32).T.astype(bf16))
    return [*tall, table[h]]


def turned_table(table):
    return [table[h].astype(f32).T.astype(bf16) for h in range(GROUP)]


def side_by_side(held, pieces, t, h):
    return jnp.concatenate([head_rows(held, n, t, h) for n in pieces], axis=1)


def stacked_rows(ref, pieces, cols):
    return jnp.concatenate([ref[EVERY_PIECE[n], cols] for n in pieces], axis=0)


def attend_kernel(here, spans, *refs):
    held, table, out, logs = refs[0:2], refs[2], refs[3], refs[4]
    hidden, scores, probs = refs[5:]
    table_t = turned_table(table)
    hide(here, spans, hidden)
    for h in range(GROUP):
        tall = keys_and_values(held, table, h)
        for part in range(2):
            cols = slice(part * HALF, part * HALF + HALF)
            pieces = SEEN[part]
            query = side_by_side(held, (2 * part, 2 * part + 1), 0, h) * bf16(0.125)
            right = jnp.concatenate([query, jnp.zeros_like(query)], axis=0)
            top = jnp.full((8, HALF), big_negative, f32)
            for n in pieces:
                block = jnp.dot(tall[n], right, preferred_element_type=f32) + hidden[EVERY_PIECE[n], cols]
                scores[EVERY_PIECE[n], :] = block
                top = jnp.maximum(top, jnp.max(block.reshape(-1, 8, HALF), axis=0))
            top = jnp.max(top, axis=0, keepdims=True)
            total = jnp.zeros((8, HALF), f32)
            for n in pieces:
                block = jnp.exp(scores[EVERY_PIECE[n], :] - top)
                scores[EVERY_PIECE[n], :] = block
                total = total + jnp.sum(block.reshape(-1, 8, HALF), axis=0)
            total = jnp.sum(total, axis=0, keepdims=True)
            share = 1.0 / total
            for n in pieces:
                probs[EVERY_PIECE[n], :] = (scores[EVERY_PIECE[n], :] * share).astype(bf16)
            result = jnp.dot(
                side_by_side(held, pieces[:-1], 2, h), stacked_rows(probs, pieces[:-1], every), preferred_element_type=f32
            )
            result = result + jnp.dot(table_t[h][64:, :], probs[LENGTH:, :], preferred_element_type=f32)
            for n in range(2):
                out[2 * part + n, 64 * h : 64 * h + 64, :] = result[:, TOK * n : TOK * n + TOK].astype(bf16)
            logs[h : h + 1, cols] = top + jnp.log(total)


def attend(here, spans, own, other, tables, layer, waits=()):
    def kernel(*refs):
        attend_kernel(*refs[:4], refs[4].at[layer], *refs[5 + len(waits) :])

    return pl.pallas_call(
        kernel,
        out_shape=(shape(4, 192, TOK), shape(8, 512, dtype=f32)),
        in_specs=[SCALARS, *in_vmem(4), *anywhere(len(waits))],
        out_specs=tuple(in_vmem(2)),
        scratch_shapes=[
            pltpu.VMEM((LENGTH + PAD, 2 * HALF), f32),
            pltpu.VMEM((LENGTH + PAD, HALF), f32),
            pltpu.VMEM((LENGTH + PAD, HALF), bf16),
        ],
        compiler_params=params(20),
        name="attend",
    )(here, spans, own, other, tables, *waits)


def attend_back_kernel(here, spans, logs, *refs):
    held, blocks, table = refs[0:2], refs[2:6], refs[6]
    grad_query, mine, others, grad_table = refs[7:11]
    hidden, probs, slopes, packed, sums, grads = refs[11:]
    table_t = turned_table(table)
    for y in range(4):

        @pl.when(here[Y] == y)
        def _():
            for k in range(4):
                grads[(y + k) % 4] = blocks[k][...]

    hide(here, spans, hidden)
    for h in range(GROUP):
        tall = keys_and_values(held, table, h)
        for part in (1, 0):
            cols = slice(part * HALF, part * HALF + HALF)
            pieces = SEEN[part]
            query = side_by_side(held, (2 * part, 2 * part + 1), 0, h) * bf16(0.125)
            grad = jnp.concatenate([grads[2 * part + n, 64 * h : 64 * h + 64, :] for n in range(2)], axis=1)
            nothing = jnp.zeros_like(query)
            right = jnp.concatenate(
                [jnp.concatenate([query, nothing], axis=1), jnp.concatenate([nothing, grad], axis=1)], axis=0
            )
            right_t = right.astype(f32).T.astype(bf16)
            log_total = logs[h : h + 1, cols]
            inner = jnp.zeros((8, HALF), f32)
            for n in pieces:
                piece = EVERY_PIECE[n]
                both = jnp.dot(tall[n], right, preferred_element_type=f32)
                prob = jnp.exp(both[:, :HALF] + hidden[piece, cols] - log_total)
                slope = both[:, HALF:]
                probs[piece, :] = prob
                slopes[piece, :] = slope
                packed[piece, HALF:] = prob.astype(bf16)
                inner = inner + jnp.sum((prob * slope).reshape(-1, 8, HALF), axis=0)
            inner = jnp.sum(inner, axis=0, keepdims=True)
            for n in pieces:
                piece = EVERY_PIECE[n]
                packed[piece, :HALF] = (probs[piece, :] * (slopes[piece, :] - inner)).astype(bf16)
            result = jnp.dot(
                side_by_side(held, pieces[:-1], 1, h),
                stacked_rows(packed, pieces[:-1], slice(0, HALF)),
                preferred_element_type=f32,
            )
            result = result + jnp.dot(table_t[h][:64, :], packed[LENGTH:, :HALF], preferred_element_type=f32)
            grad_query[64 * h : 64 * h + 64, cols] = (result * 0.125).astype(bf16)
            for n in pieces:
                new = jnp.dot(packed[EVERY_PIECE[n], :], right_t, preferred_element_type=f32)
                sums[EVERY_PIECE[n], :] = new if part == 1 else sums[EVERY_PIECE[n], :] + new
        for n in range(4):
            mine[h, :, TOK * n : TOK * n + TOK] = sums[EVERY_PIECE[n], :].T
            others[h, :, TOK * n : TOK * n + TOK] = sums[EVERY_PIECE[4 + n], :].T.astype(bf16)
        grad_table[PREFIX * h : PREFIX * h + PREFIX, :] = sums[LENGTH : LENGTH + PREFIX, :]
    grad_table[GROUP * PREFIX :, :] = jnp.zeros((ROWS - GROUP * PREFIX, 128), f32)


def attend_back(here, spans, logs, own, other, grads, tables, layer):
    def kernel(*refs):
        attend_back_kernel(*refs[:9], refs[9].at[layer], *refs[10:])

    return pl.pallas_call(
        kernel,
        out_shape=(
            shape(192, 512),
            shape(GROUP, 128, 512, dtype=f32),
            shape(GROUP, 128, 512),
            shape(ROWS, 128, dtype=f32),
        ),
        in_specs=[SCALARS, *in_vmem(9)],
        out_specs=tuple(in_vmem(4)),
        scratch_shapes=[
            pltpu.VMEM((LENGTH + PAD, 2 * HALF), f32),
            pltpu.VMEM((LENGTH + PAD, HALF), f32),
            pltpu.VMEM((LENGTH + PAD, HALF), f32),
            pltpu.VMEM((LENGTH + PAD, 2 * HALF), bf16),
            pltpu.VMEM((LENGTH + PAD, 128), f32),
            pltpu.VMEM((4, 192, TOK), bf16),
        ],
        compiler_params=params(24),
        name="attend_back",
    )(here, spans, logs, own, other, *grads, tables)


def pack_back_kernel(here, grad_query, mine, got, *refs):
    outs = refs[-4:]
    for y in range(4):

        @pl.when(here[Y] == y)
        def _():
            for k in range(4):
                start = TOK * ((y + k) % 4)
                cols = slice(start, start + TOK)
                outs[k][0:192, :] = grad_query[:, cols]
                for h in range(GROUP):
                    both = (mine[h, :, cols] + got[h, :, cols].astype(f32)).astype(bf16)
                    outs[k][192 + 64 * h : 256 + 64 * h, :] = both[:64, :]
                    outs[k][384 + 64 * h : 448 + 64 * h, :] = both[64:, :]


def pack_back(here, grad_query, mine, got, waits):
    def kernel(*refs):
        pack_back_kernel(*refs[:4], *refs[-4:])

    return pl.pallas_call(
        kernel,
        out_shape=tuple([shape(576, TOK)] * 4),
        in_specs=[SCALARS, *in_vmem(3), *anywhere(len(waits))],
        out_specs=tuple(in_vmem(4)),
        compiler_params=params(16),
        name="pack_back",
    )(here, grad_query, mine, got, *waits)


def spread_kernel(*refs):
    tables, spread = refs[: 2 * LAYERS], refs[-1]
    whole = jnp.concatenate([tables[2 * n][...] + tables[2 * n + 1][...] for n in range(LAYERS)], axis=0).astype(bf16)
    for n in range(64):
        spread[n] = whole


def spread_tables(tables):
    return pl.pallas_call(
        spread_kernel,
        out_shape=shape(64, LAYERS * ROWS, 128),
        in_specs=in_vmem(2 * LAYERS),
        out_specs=pl.BlockSpec(memory_space=pltpu.VMEM),
        compiler_params=params(8),
        name="spread_tables",
    )(*tables)


def split(value):
    high = value.astype(bf16)
    return high, (value - high.astype(f32)).astype(bf16)


def products(left, right, dims):
    total = None
    for a, b in ((1, 0), (0, 1), (0, 0)):
        term = lax.dot_general(left[a], right[b], (dims, ((), ())), preferred_element_type=f32)
        total = term if total is None else total + term
    return total


PLAIN, TURNED = ((1,), (0,)), ((1,), (1,))


def prepare_kernel(
    here, layout_own, layout_other, table, matrix_in, bias_in, matrix_out, bias_out, gain, offset, tables, hidden, spans, gains, flat
):
    flat[:PREFIX, :D] = table[...]
    flat[PREFIX:, :D] = jnp.zeros((PAD - PREFIX, D), f32)
    inner = products(split(flat[:, :D]), split(matrix_in[...]), PLAIN) + bias_in[...]
    real = lax.broadcasted_iota(jnp.int32, (PAD, 512), 0) < PREFIX
    hidden[...] = jnp.where(real, jnp.tanh(inner), 0.0)
    parts = split(hidden[...])
    for n in range(6):
        cols = slice(512 * n, 512 * n + 512)
        flat[:, cols] = products(parts, split(matrix_out[:, cols]), PLAIN) + bias_out[:, cols]
    real = lax.broadcasted_iota(jnp.int32, (PAD, 2 * HD), 0) < PREFIX
    for y in range(SIDE):

        @pl.when(here[Y] == y)
        def _():
            for layer in range(LAYERS):
                for h in range(GROUP):
                    at = layer * 2 * D + (GROUP * y + h) * HD
                    both = jnp.concatenate([flat[:, at : at + HD], flat[:, at + D : at + D + HD]], axis=1)
                    tables[layer, h] = jnp.where(real, both, 0.0).astype(bf16)

    lane = lax.broadcasted_iota(jnp.int32, (8, 4 * TOK), 1)
    places = lane + TOK * (lax.div(lane, TOK) + here[CORE])
    own = here[4] == here[CORE]
    end = jnp.int32(0)
    starts = jnp.zeros((8, 4 * TOK), jnp.int32)
    for n in range(8):
        end = end + jnp.where(own, layout_own[n], layout_other[n])
        starts = jnp.where(places >= end, end, starts)
    living = LENGTH - jnp.where(own, layout_own[8], layout_other[8])
    starts = jnp.where(places < living, starts, 4 * LENGTH)
    spans[0:1, :] = starts[0:1, :]
    spans[1:2, :] = places[0:1, :]
    rows = [ref[layer, which : which + 1, :] for layer in range(LAYERS) for which in range(2) for ref in (gain, offset)]
    gains[...] = jnp.concatenate(rows, axis=0).T


def prepare(here, layout_own, layout_other, table, matrix_in, bias_in, matrix_out, bias_out, gain, offset):
    return pl.pallas_call(
        prepare_kernel,
        out_shape=(
            shape(LAYERS, GROUP, PAD, 2 * HD),
            shape(PAD, 512, dtype=f32),
            shape(2, 4 * TOK, dtype=jnp.int32),
            shape(D, 8, dtype=f32),
        ),
        in_specs=[SCALARS] * 3 + in_vmem(7),
        out_specs=tuple(in_vmem(4)),
        scratch_shapes=[pltpu.VMEM((PAD, 2 * LAYERS * D), f32)],
        compiler_params=params(20),
        name="prepare",
    )(here, layout_own, layout_other, table, matrix_in, bias_in[None], matrix_out, bias_out[None], gain, offset)


def chain_kernel(hidden, hidden_t, table_t, matrix_in, matrix_out, parts, g_table, g_in, g_in_bias, g_out, g_out_bias, *scratch):
    grads, new_out, sems = scratch
    chunks = [slice(512 * n, 512 * n + 512) for n in range(6)]
    writes = [pltpu.make_async_copy(new_out.at[:, c], g_out.at[:, c], sems.at[n]) for n, c in enumerate(chunks)]
    grads[...] = jnp.zeros_like(grads)
    for y in range(SIDE):
        total = jnp.zeros((LAYERS * ROWS, 128), f32)
        for z in range(4):
            for xl in range(2):
                for xh in range(2):
                    total = total + parts[((z * 2 + xl) * 4 + y) * 2 + xh].astype(f32)
        for layer in range(LAYERS):
            for h in range(GROUP):
                first_row = ROWS * layer + PREFIX * h
                rows = total[first_row : first_row + PREFIX, :]
                at = layer * 2 * D + (GROUP * y + h) * HD
                grads[:PREFIX, at : at + HD] = rows[:, :HD]
                grads[:PREFIX, at + D : at + D + HD] = rows[:, HD:]
    g_out_bias[...] = jnp.sum(grads[...], axis=0, keepdims=True)
    hidden_parts = split(hidden_t[...])
    some = [split(grads[:, cols]) for cols in chunks]
    for n, cols in enumerate(chunks):
        new_out[:, cols] = products(hidden_parts, some[n], PLAIN)
        writes[n].start()
    slope = jnp.zeros((PAD, 512), f32)
    for n, cols in enumerate(chunks):
        slope = slope + products(some[n], split(matrix_out[:, cols]), TURNED)
    slope = slope * (1.0 - hidden[...] * hidden[...])
    g_in_bias[...] = jnp.sum(slope, axis=0, keepdims=True)
    parts_of_slope = split(slope)
    g_in[...] = products(split(table_t[...]), parts_of_slope, PLAIN)
    g_table[...] = products(parts_of_slope, split(matrix_in[...]), TURNED)[:PREFIX, :]
    finish(writes)


def chain(hidden, table, matrix_in, matrix_out, parts):
    g_table, g_in, g_in_bias, g_out, g_out_bias = pl.pallas_call(
        chain_kernel,
        out_shape=(
            shape(PREFIX, D, dtype=f32),
            shape(D, 512, dtype=f32),
            shape(1, 512, dtype=f32),
            shape(512, 2 * LAYERS * D, dtype=f32),
            shape(1, 2 * LAYERS * D, dtype=f32),
        ),
        in_specs=in_vmem(6),
        out_specs=(*in_vmem(3), *anywhere(1), *in_vmem(1)),
        scratch_shapes=[
            pltpu.VMEM((PAD, 2 * LAYERS * D), f32),
            pltpu.VMEM((512, 2 * LAYERS * D), f32),
            pltpu.SemaphoreType.DMA((6,)),
        ],
        compiler_params=params(32),
        name="chain",
    )(hidden, hidden.T, table.T, matrix_in, matrix_out, parts)
    return g_table, g_in, g_in_bias[0], g_out, g_out_bias[0]


def start_weights(here, attn_weight, out_weight, fc_weight, proj_weight, waits):
    core = here[CORE]
    turned = jnp.swapaxes(proj_weight, 1, 2)
    mine = lax.dynamic_slice_in_dim(turned, 48 * core, 48, axis=1)
    theirs = lax.dynamic_slice_in_dim(turned, 48 * (1 - core), 48, axis=1)
    ao = jnp.concatenate([attn_weight, out_weight], axis=2)
    kept, given = jnp.where(core == 0, ao, fc_weight), jnp.where(core == 0, fc_weight, ao)
    got = move(given, core_pairs())
    pair = jnp.where(core == 0, jnp.stack([kept, got]), jnp.stack([got, kept]))
    got = move(theirs, core_pairs())
    pj = jnp.where(core == 0, jnp.concatenate([mine, got], axis=2), jnp.concatenate([got, mine], axis=2))
    pair, pj = assemble(
        here,
        None,
        [
            (around_two(pair, X, Y), shape(2, 4, 48, 768), put_pair_one),
            (around(pj, Z), shape(2, 48, 1536), put_proj_one),
        ],
        waits,
    )
    return around_two(pair, Y, Z), around(pj, X)


def both_cores(blocks):
    return [*blocks, *[move(b, core_pairs()) for b in blocks]]


PROJ_WHOLE = shape(2, 48, 3072)


def rest_of_pairs(here, pair, proj, waits):
    pair_whole = shape(4, 48, 3072)
    whole, whole_proj = assemble(here, 0, [(pair, pair_whole, put_pair_two), (proj, PROJ_WHOLE, put_proj_two)], waits)
    zero = around_two(whole, Z, X)
    near = [whole_proj, move(whole_proj, ring(Y, 1)), move(whole_proj, ring(Y, 3))]
    (whole,) = assemble(here, 1, [(pair, pair_whole, put_pair_two)], tuple(zero[1:]))
    return both_cores(zero), both_cores(around_two(whole, Z, X)), near


def far_of_proj(here, proj, near, waits):
    (whole,) = assemble(here, 0, [(proj, PROJ_WHOLE, put_proj_two)], waits)
    own, ahead, behind = near
    return [own, ahead, move(whole, ring(Y, 2)), behind]


def rest_of_proj(here, proj, layer, waits):
    (whole,) = assemble(here, layer, [(proj, PROJ_WHOLE, put_proj_two)], waits)
    return around(whole, Y)


def put_stacked(here, k, block, result):
    result[wrap(here[Y] + k)] = block[...]


def proj_of_both(here, blocks, waits):
    (own,) = assemble(here, None, [(blocks, shape(4, 2, 48, 3072), put_stacked)], waits)
    return [own, move(own, core_pairs())]


def on_device(
    states_in,
    attn_weight,
    out_weight,
    fc_weight,
    proj_weight,
    norm_gain,
    norm_shift,
    prefix_table,
    reparam_in,
    reparam_in_bias,
    reparam_out,
    reparam_out_bias,
    doc_lengths,
    pad_counts,
    states_grad,
):
    z, xl, core, y, xh = (lax.axis_index(name) for name in AXES)
    here = jnp.stack([z, 2 * xh + xl, core, y, xh]).astype(jnp.int32)
    x = move(states_in[0], seat_pairs())
    grad_in = move(states_grad[0], seat_pairs())
    layout = jnp.concatenate([doc_lengths[0], pad_counts])
    pair, proj = start_weights(here, attn_weight, out_weight, fc_weight, proj_weight, ())
    layout_other = move(layout, core_pairs())

    prepared = prepare(
        here,
        layout,
        layout_other,
        prefix_table,
        reparam_in,
        reparam_in_bias,
        reparam_out,
        reparam_out_bias,
        norm_gain,
        norm_shift,
    )
    tables, hidden, spans, gains = prepared
    pair_zero, pair_one, near = rest_of_pairs(here, pair, proj, (*prepared, x, grad_in))
    table = jnp.pad(prefix_table, ((0, PAD - PREFIX), (0, 0)))
    stream, sends = first(here, x, gains, pair_zero, (spans, tables))
    proj_zero = far_of_proj(here, proj, near, (sends,))
    arrived = [(*pair_one[1:4], *near[1:]), ()]
    streams = [stream]
    kept = []
    for layer in range(LAYERS):
        own = swap_on_ring(sends)
        other = move(own, core_pairs())
        if layer == 0:
            proj_one = rest_of_proj(here, proj, 1, (own,))
        else:
            proj_one = proj_of_both(here, proj_one, (own,))
        mixed, logs = attend(here, spans, own, other, tables, layer, arrived[layer])
        if layer == 0:
            proj_zero = proj_of_both(here, proj_zero, (mixed,))
        mixed = swap_on_ring(mixed)
        kept.append((own, other, logs))
        if layer == 0:
            middle, before, stream, sends = middle_part(here, stream, gains, mixed, pair_zero, proj_zero, pair_one, ())
            streams.append(stream)
        else:
            final, grad_middle, *sends = last_part(here, stream, gains, mixed, grad_in, pair_one, proj_one)
    final = move(final, seat_pairs())

    tables_back = ()
    for layer in reversed(range(LAYERS)):
        own, other, logs = kept[layer]
        grads = to_places(sends)
        grad_query, mine, theirs, grad_table = attend_back(here, spans, logs, own, other, grads, tables, layer)
        tables_back = (grad_table, move(grad_table, core_pairs()), *tables_back)
        theirs = move(theirs, core_pairs())
        waits = () if layer else (spread_tables(tables_back),)
        back = to_places(pack_back(here, grad_query, mine, theirs, waits))
        if layer == 1:
            grad_middle, *sends = turn_part(
                here, streams[1], gains, grad_middle, before, middle, back, pair_one, pair_zero, proj_zero, (final,)
            )
        else:
            shared = lax.all_to_all(waits[0], ("z", "xl", "y", "xh"), 0, 0, tiled=True)
            prefix_grads = chain(hidden, table, reparam_in, reparam_out, shared)
            grad_states = end_part(here, streams[0], gains, grad_middle, back, pair_zero, (prefix_grads[0],))
    grad_states = move(grad_states, seat_pairs())

    return (final[None], grad_states[None], *prefix_grads)


def solution(mesh):
    grid = Mesh(mesh.devices.reshape(GRID), AXES)
    rows, cols = ("z", "xl", "core"), ("y", "xh")
    return jax.shard_map(
        on_device,
        mesh=grid,
        in_specs=(
            P(rows, cols, None),
            P(None, rows, cols),
            P(None, rows, cols),
            P(None, rows, cols),
            P(None, rows, cols),
            P(),
            P(),
            P(),
            P(),
            P(),
            P(),
            P(),
            P(rows, None),
            P(rows),
            P(rows, cols, None),
        ),
        out_specs=(P(rows, cols, None), P(rows, cols, None), P(), P(), P(), P(), P()),
        check_vma=False,
    )
```

```python
import jax
import jax.numpy as jnp
from jax import lax
from jax.experimental import pallas as pl
from jax.experimental.pallas import tpu as pltpu
from jax.sharding import Mesh
from jax.sharding import PartitionSpec as P

D = 768
H = 12
HD = 64
FF = 3072
LENGTH = 1024
PREFIX = 10
LAYERS = 2
TOK = 128
PAD = 16
GROUP = 3
ROWS = 32
SIDE = 4
AXES = ("z", "xl", "core", "y", "xh")
GRID = (4, 2, 2, 4, 2)

epsilon = 1e-05
highest = lax.Precision.HIGHEST
big_negative = -1e30
bf16 = jnp.bfloat16
f32 = jnp.float32


def index_of(z, x, core, y):
    return (((z * 2 + x % 2) * 2 + core) * 4 + y) * 2 + x // 2


def everywhere():
    return [(z, x, c, y) for z in range(4) for x in range(4) for c in range(2) for y in range(4)]


def ring(axis, ahead):
    pairs = []
    for spot in everywhere():
        source = list(spot)
        source[axis] = (source[axis] + ahead) % 4
        pairs.append((index_of(*source), index_of(*spot)))
    return pairs


def two_rings(axis_zero, axis_one, ahead):
    pairs = []
    for spot in everywhere():
        source = list(spot)
        axis = axis_one if spot[CORE] else axis_zero
        source[axis] = (source[axis] + ahead) % 4
        pairs.append((index_of(*source), index_of(*spot)))
    return pairs


def core_pairs():
    return [(index_of(z, x, 1 - c, y), index_of(z, x, c, y)) for z, x, c, y in everywhere()]


def seat_pairs():
    return [(index_of(z, c * 2 + x % 2, x // 2, y), index_of(z, x, c, y)) for z, x, c, y in everywhere()]


Z, X, CORE, Y = 0, 1, 2, 3


def move(value, pairs):
    return lax.ppermute(value, AXES, pairs)


def around(value, axis):
    return [value] + [move(value, ring(axis, k)) for k in (1, 2, 3)]


def around_two(value, axis_zero, axis_one):
    return [value] + [move(value, two_rings(axis_zero, axis_one, k)) for k in (1, 2, 3)]


def to_places(blocks):
    got = [None, *[move(blocks[k], ring(Y, -k)) for k in (1, 2, 3)]]
    return [blocks[0], got[3], got[2], got[1]]


def swap_on_ring(blocks):
    return lax.all_to_all(blocks, "y", 0, 0, tiled=True)


def wrap(value):
    return lax.rem(value, SIDE)


def params(limit):
    return pltpu.CompilerParams(vmem_limit_bytes=limit * 2**20)


def anywhere(count):
    return [pl.BlockSpec(memory_space=pl.ANY)] * count


def in_vmem(count):
    return [pl.BlockSpec(memory_space=pltpu.VMEM)] * count


SCALARS = pl.BlockSpec(memory_space=pltpu.SMEM)


def shape(*dims, dtype=bf16):
    return jax.ShapeDtypeStruct(dims, dtype)


def lanes(start, size):
    return pl.ds(pl.multiple_of(start, 128), size)


def block_of(layer, dims):
    if layer is None:
        return pl.BlockSpec(dims, lambda i: (0,) * len(dims))
    return pl.BlockSpec((None, *dims[1:]), lambda i: (layer,) + (0,) * (len(dims) - 1))


def assemble(here, layer, groups, waits=()):
    count = len(groups)

    def kernel(here, *refs):
        for n, (_, _, put, *_) in enumerate(groups):
            for k in range(4):
                put(here, k, refs[4 * n + k], refs[n - count])

    blocks = [b for group in groups for b in group[0]]
    outs = [group[1] for group in groups]
    specs = [block_of(None if len(group) > 3 else layer, b.shape) for group in groups for b in group[0]]
    return pl.pallas_call(
        kernel,
        grid=(1,),
        out_shape=outs,
        in_specs=[SCALARS, *specs, *anywhere(len(waits))],
        out_specs=[block_of(None, out.shape) for out in outs],
        compiler_params=params(16),
        name="assemble",
    )(here, *blocks, *waits)


def pick(here, zero, one):
    return jnp.where(here[CORE] == 0, zero, one)


def put_pair_one(here, k, block, result):
    place = wrap(pick(here, here[X], here[Y]) + k)
    low, high = lax.rem(place, 2), lax.div(place, 2)
    for c in range(2):
        row, col = pick(here, 2 * low + c, 2 * c + high), pick(here, high, low)
        result[:, row, :, lanes(384 * col, 384)] = block[c]


def put_pair_two(here, k, block, result):
    place = wrap(pick(here, here[Y], here[Z]) + k)
    for i in range(4):
        result[pick(here, i, place), :, lanes(768 * pick(here, place, i), 768)] = block[i]


def put_proj_one(layer):
    def put(here, k, block, result):
        result[:, lanes(384 * wrap(here[Z] + k), 384)] = block[layer]

    return put


def put_proj_two(here, k, block, result):
    place = wrap(here[X] + k)
    result[lax.div(place, 2), :, lanes(1536 * lax.rem(place, 2), 1536)] = block[...]


AO_HELD = pltpu.VMEM((4, 4, 48, 3072), bf16)
FC_HELD = pltpu.VMEM((2, 4, 2, 2, 48, 1536), bf16)
PJ_HELD = pltpu.VMEM((4, 2, 2, 48, 3072), bf16)


class Chosen:
    def __init__(self, here, zero, one, target, sem):
        self.here = here
        self.copies = [pltpu.make_async_copy(source, target, sem) for source in (zero, one)]

    def start(self):
        for core in range(2):
            pl.when(self.here[CORE] == core)(self.copies[core].start)

    def wait(self):
        self.copies[0].wait()


def fetch_ao(here, refs, held, sems):
    return [Chosen(here, refs[k], refs[4 + k], held.at[wrap(here[Z] + k)], sems.at[k]) for k in range(4)]


def fetch_fc(here, refs, held, sems):
    copies = []
    for k in range(4):
        there = wrap(here[X] + k)
        for c in range(2):
            target = held.at[lax.div(there, 2), :, lax.rem(there, 2), c]
            cols = slice(1536 * c, 1536 * c + 1536)
            copies.append(Chosen(here, refs[4 + k].at[:, :, cols], refs[k].at[:, :, cols], target, sems.at[2 * k + c]))
    return copies


def fetch_pj(here, refs, held, sems):
    cores = (here[CORE], 1 - here[CORE])
    return [pltpu.make_async_copy(refs[n], held.at[:, :, core], sems.at[n]) for n, core in enumerate(cores)]


def fetch_pj_one(here, refs, held, sems):
    copies = []
    for n, core in enumerate((here[CORE], 1 - here[CORE])):
        for x in range(4):
            cols = slice(1536 * (x % 2), 1536 * (x % 2) + 1536)
            copies.append(pltpu.make_async_copy(refs[n].at[x], held.at[:, x // 2, core, :, cols], sems.at[4 * n + x]))
    return copies


def begin(copies):
    for one in copies:
        one.start()


def finish(copies):
    for one in copies:
        one.wait()


def flipped(value):
    return value.astype(f32).T


def norm_stats(stream):
    centre = jnp.mean(stream, axis=0, keepdims=True)
    centred = stream - centre
    spread = jnp.mean(centred * centred, axis=0, keepdims=True)
    return centred, lax.rsqrt(spread + epsilon)


def norm(stream, gain, shift):
    centred, rate = norm_stats(stream)
    return centred * rate * gain + shift


def norm_back(stream, gain, grad):
    centred, rate = norm_stats(stream)
    unit = centred * rate
    scaled = grad * gain
    inner = jnp.mean(scaled * unit, axis=0, keepdims=True)
    return rate * (scaled - jnp.mean(scaled, axis=0, keepdims=True) - unit * inner)


root = 0.7978845608028654


def gate(u):
    return 0.5 * u * (1.0 + jnp.tanh(root * (u + 0.044715 * (u * u * u))))


def gate_slope(u):
    squared = u * u
    t = jnp.tanh(root * (u + 0.044715 * (squared * u)))
    return 0.5 * (1.0 + t) + (0.5 * root) * u * (1.0 - t * t) * (1.0 + (3.0 * 0.044715) * squared)


def column(gains, layer, which, part):
    at = layer * 4 + which * 2 + part
    return gains[:, at : at + 1]


def rows_of_place(place):
    pieces = []
    for t in range(3):
        for u in range(2):
            piece = 8 * t + 2 * place + u
            pieces.append((384 * (piece // 3) + 96 * (piece % 3), t * 192 + u * 96))
    return pieces


def send_qkv(here, stream, gains, layer, held, wide, sends):
    normed = norm(stream, column(gains, layer, 0, 0), column(gains, layer, 0, 1)).T.astype(bf16)
    for j in range(4):
        cols = slice(768 * j, 768 * j + 768)
        packed = jnp.dot(normed, held[:, :, :, cols].reshape(D, 768), preferred_element_type=f32)
        wide[cols, :] = packed.T.astype(bf16)
    for place in range(4):
        for row, at in rows_of_place(place):
            sends[place, at : at + 96, :] = wide[row : row + 96, :]


def first_kernel(here, x_ref, gains, *refs):
    ao, (stream, sends), (held, wide, sems) = refs[0:8], refs[8:10], refs[10:]
    copies = fetch_ao(here, ao, held, sems)
    begin(copies)
    stream[...] = flipped(x_ref[...])
    finish(copies)
    send_qkv(here, stream[...], gains, 0, held, wide, sends)


def first(here, x, gains, ao, waits):
    def kernel(*refs):
        first_kernel(*refs[:11], *refs[11 + len(waits) :])

    return pl.pallas_call(
        kernel,
        out_shape=(shape(D, TOK, dtype=f32), shape(4, 576, TOK)),
        in_specs=[SCALARS, *in_vmem(2), *anywhere(8 + len(waits))],
        out_specs=tuple(in_vmem(2)),
        scratch_shapes=[AO_HELD, pltpu.VMEM((FF, TOK), bf16), pltpu.SemaphoreType.DMA((8,))],
        compiler_params=params(24),
        name="first",
    )(here, x, gains, *ao, *waits)


def after_attention(here, stream, mixed, gains, layer, ao_held, fc_held, pj_held, waits, act, before, middle, result):
    rows = flipped(mixed[...].reshape(D, TOK)).astype(bf16)
    finish(waits[0])

    weight = jnp.concatenate([ao_held[:, :, :, 384 * j + 256 : 384 * j + 384].reshape(D, 128) for j in range(8)], axis=1)
    part = jnp.dot(rows, weight, preferred_element_type=f32).T
    for j in range(8):
        at = slice(96 * j, 96 * j + 96)
        middle[at, :] = stream[at, :] + part[128 * j + 32 : 128 * j + 128, :]
    normed = norm(middle[...], column(gains, layer, 1, 0), column(gains, layer, 1, 1)).T.astype(bf16)
    finish(waits[1])

    for n in range(4):
        low = 768 * (n % 2)
        weight = fc_held[n // 2, :, :, :, :, low : low + 768].reshape(D, 768)
        inputs = jnp.dot(normed, weight, preferred_element_type=f32)
        before[n] = inputs
        act[768 * n : 768 * n + 768, :] = gate(inputs).T.astype(bf16)
    finish(waits[2])
    for n in range(2):
        at = slice(384 * n, 384 * n + 384)
        weight = pj_held[2 * n : 2 * n + 2].reshape(384, FF)
        result[at, :] = middle[at, :] + jnp.dot(weight, act[...], preferred_element_type=f32)


def middle_kernel(here, stream, gains, *refs):
    mixed, pair, pj, pair_next = refs[0], refs[1:9], refs[9:11], refs[11:19]
    middle, before, result, sends = refs[19:23]
    ao_held, fc_held, pj_held, next_held, act, sems = refs[23:]
    waits = [
        fetch_ao(here, pair, ao_held, sems.at[0]),
        fetch_fc(here, pair, fc_held, sems.at[1]),
        fetch_pj(here, pj, pj_held, sems.at[2]),
        fetch_ao(here, pair_next, next_held, sems.at[3]),
    ]
    for copies in waits:
        begin(copies)
    after_attention(here, stream, mixed, gains, 0, ao_held, fc_held, pj_held, waits, act, before, middle, result)
    finish(waits[3])
    send_qkv(here, result[...], gains, 1, next_held, act, sends)


def middle_part(here, stream, gains, mixed, pair, pj, pair_next, waits):
    def kernel(*refs):
        middle_kernel(*refs[:22], *refs[22 + len(waits) :])

    return pl.pallas_call(
        kernel,
        out_shape=(shape(D, TOK, dtype=f32), shape(4, TOK, 768, dtype=f32), shape(D, TOK, dtype=f32), shape(4, 576, TOK)),
        in_specs=[SCALARS, *in_vmem(3), *anywhere(18 + len(waits))],
        out_specs=tuple(in_vmem(4)),
        scratch_shapes=[
            AO_HELD,
            FC_HELD,
            PJ_HELD,
            AO_HELD,
            pltpu.VMEM((FF, TOK), bf16),
            pltpu.SemaphoreType.DMA((4, 8)),
        ],
        compiler_params=params(56),
        name="middle_part",
    )(here, stream, gains, mixed, *pair, *pj, *pair_next, *waits)


def back_feed(here, grad, before, middle, gains, layer, ao_held, fc_held, pj_held, waits, act, spread, grad_middle, sends):
    rows = grad[...].T.astype(bf16)
    finish(waits[2])

    for n in range(4):
        cols = slice(768 * n, 768 * n + 768)
        grad_act = jnp.dot(rows, pj_held[:, :, :, :, cols].reshape(D, 768), preferred_element_type=f32)
        act[cols, :] = (gate_slope(before[n]) * grad_act).T.astype(bf16)
    finish(waits[1])
    for n in range(2):
        low = jnp.dot(fc_held[0, 2 * n : 2 * n + 2].reshape(384, 1536), act[:1536, :], preferred_element_type=f32)
        high = jnp.dot(fc_held[1, 2 * n : 2 * n + 2].reshape(384, 1536), act[1536:, :], preferred_element_type=f32)
        grad_middle[384 * n : 384 * n + 384, :] = low + high
    total = grad[...] + norm_back(middle[...], column(gains, layer, 1, 0), grad_middle[...])
    grad_middle[...] = total
    rounded = total.astype(bf16)
    for j in range(8):
        spread[128 * j : 128 * j + 32, :] = jnp.zeros((32, TOK), bf16)
        spread[128 * j + 32 : 128 * j + 128, :] = rounded[96 * j : 96 * j + 96, :]
    finish(waits[0])

    weight = jnp.concatenate([ao_held[:, :, :, 384 * j + 256 : 384 * j + 384].reshape(D, 128) for j in range(8)], axis=1)
    whole = jnp.dot(weight, spread[...], preferred_element_type=f32).astype(bf16)
    for y in range(4):

        @pl.when(here[Y] == y)
        def _():
            for k in range(4):
                row = 192 * ((y + k) % 4)
                sends[k][...] = whole[row : row + 192, :]


def last_kernel(here, stream, gains, *refs):
    mixed, grad_in, pair, pj = refs[0], refs[1], refs[2:10], refs[10:12]
    final, grad_middle, *sends = refs[12:18]
    ao_held, fc_held, pj_held, act, spread, before, middle, result, sems = refs[18:]
    waits = [
        fetch_ao(here, pair, ao_held, sems.at[0]),
        fetch_fc(here, pair, fc_held, sems.at[1]),
        fetch_pj_one(here, pj, pj_held, sems.at[2]),
    ]
    for copies in waits:
        begin(copies)
    after_attention(here, stream, mixed, gains, 1, ao_held, fc_held, pj_held, waits, act, before, middle, result)
    final[...] = result[...].T
    result[...] = flipped(grad_in[...])
    back_feed(here, result, before, middle, gains, 1, ao_held, fc_held, pj_held, [[], [], []], act, spread, grad_middle, sends)


def last_part(here, stream, gains, mixed, grad_in, pair, pj):
    return pl.pallas_call(
        last_kernel,
        out_shape=(shape(TOK, D, dtype=f32), shape(D, TOK, dtype=f32), *[shape(192, TOK)] * 4),
        in_specs=[SCALARS, *in_vmem(4), *anywhere(10)],
        out_specs=tuple(in_vmem(6)),
        scratch_shapes=[
            AO_HELD,
            FC_HELD,
            PJ_HELD,
            pltpu.VMEM((FF, TOK), bf16),
            pltpu.VMEM((1024, TOK), bf16),
            pltpu.VMEM((4, TOK, 768), f32),
            pltpu.VMEM((D, TOK), f32),
            pltpu.VMEM((D, TOK), f32),
            pltpu.SemaphoreType.DMA((3, 8)),
        ],
        compiler_params=params(40),
        name="last_part",
    )(here, stream, gains, mixed, grad_in, *pair, *pj)


def back_qkv(here, blocks, held, wait, wide, stream, gains, layer, grad_middle, result):
    for j in range(8):
        wide[384 * j + 288 : 384 * j + 384, :] = jnp.zeros((96, TOK), bf16)
    for y in range(4):

        @pl.when(here[Y] == y)
        def _():
            for k in range(4):
                for row, at in rows_of_place((y + k) % 4):
                    wide[row : row + 96, :] = blocks[k][at : at + 96, :]

    finish(wait)

    for n in range(2):
        weight = held[2 * n : 2 * n + 2].reshape(384, 3072)
        result[384 * n : 384 * n + 384, :] = jnp.dot(weight, wide[...], preferred_element_type=f32)
    result[...] = grad_middle[...] + norm_back(stream[...], column(gains, layer, 0, 0), result[...])


def turn_kernel(here, stream, gains, grad_above, before, middle, *refs):
    blocks, pair_above, pair, pj = refs[0:4], refs[4:12], refs[12:20], refs[20:22]
    grad_middle, *sends = refs[22:27]
    above_held, ao_held, fc_held, pj_held, act, spread, grad, sems = refs[27:]
    waits = [
        fetch_ao(here, pair_above, above_held, sems.at[0]),
        fetch_pj(here, pj, pj_held, sems.at[3]),
        fetch_fc(here, pair, fc_held, sems.at[2]),
        fetch_ao(here, pair, ao_held, sems.at[1]),
    ]
    for copies in waits:
        begin(copies)
    back_qkv(here, blocks, above_held, waits[0], act, stream, gains, 1, grad_above, grad)
    back_feed(here, grad, before, middle, gains, 0, ao_held, fc_held, pj_held, [waits[3], waits[2], waits[1]], act, spread, grad_middle, sends)


def turn_part(here, stream, gains, grad_above, before, middle, blocks, pair_above, pair, pj, waits):
    def kernel(*refs):
        turn_kernel(*refs[:28], *refs[28 + len(waits) :])

    return pl.pallas_call(
        kernel,
        out_shape=(shape(D, TOK, dtype=f32), *[shape(192, TOK)] * 4),
        in_specs=[SCALARS, *in_vmem(9), *anywhere(18 + len(waits))],
        out_specs=tuple(in_vmem(5)),
        scratch_shapes=[
            AO_HELD,
            AO_HELD,
            FC_HELD,
            PJ_HELD,
            pltpu.VMEM((FF, TOK), bf16),
            pltpu.VMEM((1024, TOK), bf16),
            pltpu.VMEM((D, TOK), f32),
            pltpu.SemaphoreType.DMA((4, 8)),
        ],
        compiler_params=params(44),
        name="turn_part",
    )(here, stream, gains, grad_above, before, middle, *blocks, *pair_above, *pair, *pj, *waits)


def end_kernel(here, stream, gains, grad_middle, *refs):
    blocks, ao, out, (held, wide, grad, sems) = refs[0:4], refs[4:12], refs[12], refs[13:]
    wait = fetch_ao(here, ao, held, sems)
    begin(wait)
    back_qkv(here, blocks, held, wait, wide, stream, gains, 0, grad_middle, grad)
    out[...] = grad[...].T


def end_part(here, stream, gains, grad_middle, blocks, ao, waits):
    def kernel(*refs):
        end_kernel(*refs[:16], *refs[16 + len(waits) :])

    return pl.pallas_call(
        kernel,
        out_shape=shape(TOK, D, dtype=f32),
        in_specs=[SCALARS, *in_vmem(7), *anywhere(8 + len(waits))],
        out_specs=pl.BlockSpec(memory_space=pltpu.VMEM),
        scratch_shapes=[AO_HELD, pltpu.VMEM((FF, TOK), bf16), pltpu.VMEM((D, TOK), f32), pltpu.SemaphoreType.DMA((8,))],
        compiler_params=params(56),
        name="end_part",
    )(here, stream, gains, grad_middle, *blocks, *ao, *waits)


HALF = 256
every = slice(None)
EVERY_PIECE = [slice(TOK * n, TOK * n + TOK) for n in range(8)] + [slice(LENGTH, LENGTH + PAD)]
SEEN = ((0, 1, 4, 5, 8), (0, 1, 2, 3, 4, 5, 6, 7, 8))


def hide(here, spans, hidden):
    inside = lax.broadcasted_iota(jnp.int32, (TOK, HALF), 0)
    for part in range(2):
        cols = slice(part * HALF, part * HALF + HALF)
        low, high = spans[0:1, cols], spans[1:2, cols]
        for n in SEEN[part][:-1]:
            start = TOK * (2 * (n % 4) + (here[CORE] if n < 4 else 1 - here[CORE]))
            seen = (inside >= low - start) & (inside <= high - start)
            hidden[EVERY_PIECE[n], cols] = jnp.where(seen, 0.0, big_negative)
    real = lax.broadcasted_iota(jnp.int32, (PAD, 2 * HALF), 0) < PREFIX
    hidden[LENGTH:, :] = jnp.where(real, 0.0, big_negative)


def head_rows(held, n, t, h):
    return held[n // 4][n % 4, 192 * t + 64 * h : 192 * t + 64 * h + 64, :]


def keys_and_values(held, table, h):
    tall = []
    for n in range(8):
        both = jnp.concatenate([head_rows(held, n, 1, h), head_rows(held, n, 2, h)], axis=0)
        tall.append(both.astype(f32).T.astype(bf16))
    return [*tall, table[h]]


def turned_table(table):
    return [table[h].astype(f32).T.astype(bf16) for h in range(GROUP)]


def side_by_side(held, pieces, t, h):
    return jnp.concatenate([head_rows(held, n, t, h) for n in pieces], axis=1)


def stacked_rows(ref, pieces, cols):
    return jnp.concatenate([ref[EVERY_PIECE[n], cols] for n in pieces], axis=0)


def attend_kernel(here, spans, *refs):
    held, table, out, logs = refs[0:2], refs[2], refs[3], refs[4]
    hidden, scores, probs = refs[5:]
    table_t = turned_table(table)
    hide(here, spans, hidden)
    for h in range(GROUP):
        tall = keys_and_values(held, table, h)
        for part in range(2):
            cols = slice(part * HALF, part * HALF + HALF)
            pieces = SEEN[part]
            query = side_by_side(held, (2 * part, 2 * part + 1), 0, h) * bf16(0.125)
            right = jnp.concatenate([query, jnp.zeros_like(query)], axis=0)
            top = jnp.full((8, HALF), big_negative, f32)
            for n in pieces:
                block = jnp.dot(tall[n], right, preferred_element_type=f32) + hidden[EVERY_PIECE[n], cols]
                scores[EVERY_PIECE[n], :] = block
                top = jnp.maximum(top, jnp.max(block.reshape(-1, 8, HALF), axis=0))
            top = jnp.max(top, axis=0, keepdims=True)
            total = jnp.zeros((8, HALF), f32)
            for n in pieces:
                block = jnp.exp(scores[EVERY_PIECE[n], :] - top)
                scores[EVERY_PIECE[n], :] = block
                total = total + jnp.sum(block.reshape(-1, 8, HALF), axis=0)
            total = jnp.sum(total, axis=0, keepdims=True)
            share = 1.0 / total
            for n in pieces:
                probs[EVERY_PIECE[n], :] = (scores[EVERY_PIECE[n], :] * share).astype(bf16)
            result = jnp.dot(
                side_by_side(held, pieces[:-1], 2, h), stacked_rows(probs, pieces[:-1], every), preferred_element_type=f32
            )
            result = result + jnp.dot(table_t[h][64:, :], probs[LENGTH:, :], preferred_element_type=f32)
            for n in range(2):
                out[2 * part + n, 64 * h : 64 * h + 64, :] = result[:, TOK * n : TOK * n + TOK].astype(bf16)
            logs[h : h + 1, cols] = top + jnp.log(total)


def attend(here, spans, own, other, tables, layer, waits=()):
    def kernel(*refs):
        attend_kernel(*refs[:4], refs[4].at[layer], *refs[5 + len(waits) :])

    return pl.pallas_call(
        kernel,
        out_shape=(shape(4, 192, TOK), shape(8, 512, dtype=f32)),
        in_specs=[SCALARS, *in_vmem(4), *anywhere(len(waits))],
        out_specs=tuple(in_vmem(2)),
        scratch_shapes=[
            pltpu.VMEM((LENGTH + PAD, 2 * HALF), f32),
            pltpu.VMEM((LENGTH + PAD, HALF), f32),
            pltpu.VMEM((LENGTH + PAD, HALF), bf16),
        ],
        compiler_params=params(20),
        name="attend",
    )(here, spans, own, other, tables, *waits)


def attend_back_kernel(here, spans, logs, *refs):
    held, blocks, table = refs[0:2], refs[2:6], refs[6]
    grad_query, mine, others, grad_table = refs[7:11]
    hidden, probs, slopes, packed, sums, grads = refs[11:]
    table_t = turned_table(table)
    for y in range(4):

        @pl.when(here[Y] == y)
        def _():
            for k in range(4):
                grads[(y + k) % 4] = blocks[k][...]

    hide(here, spans, hidden)
    for h in range(GROUP):
        tall = keys_and_values(held, table, h)
        for part in (1, 0):
            cols = slice(part * HALF, part * HALF + HALF)
            pieces = SEEN[part]
            query = side_by_side(held, (2 * part, 2 * part + 1), 0, h) * bf16(0.125)
            grad = jnp.concatenate([grads[2 * part + n, 64 * h : 64 * h + 64, :] for n in range(2)], axis=1)
            nothing = jnp.zeros_like(query)
            right = jnp.concatenate(
                [jnp.concatenate([query, nothing], axis=1), jnp.concatenate([nothing, grad], axis=1)], axis=0
            )
            right_t = right.astype(f32).T.astype(bf16)
            log_total = logs[h : h + 1, cols]
            inner = jnp.zeros((8, HALF), f32)
            for n in pieces:
                piece = EVERY_PIECE[n]
                both = jnp.dot(tall[n], right, preferred_element_type=f32)
                prob = jnp.exp(both[:, :HALF] + hidden[piece, cols] - log_total)
                slope = both[:, HALF:]
                probs[piece, :] = prob
                slopes[piece, :] = slope
                packed[piece, HALF:] = prob.astype(bf16)
                inner = inner + jnp.sum((prob * slope).reshape(-1, 8, HALF), axis=0)
            inner = jnp.sum(inner, axis=0, keepdims=True)
            for n in pieces:
                piece = EVERY_PIECE[n]
                packed[piece, :HALF] = (probs[piece, :] * (slopes[piece, :] - inner)).astype(bf16)
            result = jnp.dot(
                side_by_side(held, pieces[:-1], 1, h),
                stacked_rows(packed, pieces[:-1], slice(0, HALF)),
                preferred_element_type=f32,
            )
            result = result + jnp.dot(table_t[h][:64, :], packed[LENGTH:, :HALF], preferred_element_type=f32)
            grad_query[64 * h : 64 * h + 64, cols] = (result * 0.125).astype(bf16)
            for n in pieces:
                new = jnp.dot(packed[EVERY_PIECE[n], :], right_t, preferred_element_type=f32)
                sums[EVERY_PIECE[n], :] = new if part == 1 else sums[EVERY_PIECE[n], :] + new
        for n in range(4):
            mine[h, :, TOK * n : TOK * n + TOK] = sums[EVERY_PIECE[n], :].T
            others[h, :, TOK * n : TOK * n + TOK] = sums[EVERY_PIECE[4 + n], :].T.astype(bf16)
        grad_table[PREFIX * h : PREFIX * h + PREFIX, :] = sums[LENGTH : LENGTH + PREFIX, :]
    grad_table[GROUP * PREFIX :, :] = jnp.zeros((ROWS - GROUP * PREFIX, 128), f32)


def attend_back(here, spans, logs, own, other, grads, tables, layer):
    def kernel(*refs):
        attend_back_kernel(*refs[:9], refs[9].at[layer], *refs[10:])

    return pl.pallas_call(
        kernel,
        out_shape=(
            shape(192, 512),
            shape(GROUP, 128, 512, dtype=f32),
            shape(GROUP, 128, 512),
            shape(ROWS, 128, dtype=f32),
        ),
        in_specs=[SCALARS, *in_vmem(9)],
        out_specs=tuple(in_vmem(4)),
        scratch_shapes=[
            pltpu.VMEM((LENGTH + PAD, 2 * HALF), f32),
            pltpu.VMEM((LENGTH + PAD, HALF), f32),
            pltpu.VMEM((LENGTH + PAD, HALF), f32),
            pltpu.VMEM((LENGTH + PAD, 2 * HALF), bf16),
            pltpu.VMEM((LENGTH + PAD, 128), f32),
            pltpu.VMEM((4, 192, TOK), bf16),
        ],
        compiler_params=params(24),
        name="attend_back",
    )(here, spans, logs, own, other, *grads, tables)


def pack_back_kernel(here, grad_query, mine, got, *refs):
    outs = refs[-4:]
    for y in range(4):

        @pl.when(here[Y] == y)
        def _():
            for k in range(4):
                start = TOK * ((y + k) % 4)
                cols = slice(start, start + TOK)
                outs[k][0:192, :] = grad_query[:, cols]
                for h in range(GROUP):
                    both = (mine[h, :, cols] + got[h, :, cols].astype(f32)).astype(bf16)
                    outs[k][192 + 64 * h : 256 + 64 * h, :] = both[:64, :]
                    outs[k][384 + 64 * h : 448 + 64 * h, :] = both[64:, :]


def pack_back(here, grad_query, mine, got, waits):
    def kernel(*refs):
        pack_back_kernel(*refs[:4], *refs[-4:])

    return pl.pallas_call(
        kernel,
        out_shape=tuple([shape(576, TOK)] * 4),
        in_specs=[SCALARS, *in_vmem(3), *anywhere(len(waits))],
        out_specs=tuple(in_vmem(4)),
        compiler_params=params(16),
        name="pack_back",
    )(here, grad_query, mine, got, *waits)


def spread_kernel(*refs):
    tables, spread = refs[: 2 * LAYERS], refs[-1]
    whole = jnp.concatenate([tables[2 * n][...] + tables[2 * n + 1][...] for n in range(LAYERS)], axis=0).astype(bf16)
    for n in range(64):
        spread[n] = whole


def spread_tables(tables):
    return pl.pallas_call(
        spread_kernel,
        out_shape=shape(64, LAYERS * ROWS, 128),
        in_specs=in_vmem(2 * LAYERS),
        out_specs=pl.BlockSpec(memory_space=pltpu.VMEM),
        compiler_params=params(8),
        name="spread_tables",
    )(*tables)


def split(value):
    high = value.astype(bf16)
    return high, (value - high.astype(f32)).astype(bf16)


def products(left, right, dims):
    total = None
    for a, b in ((1, 0), (0, 1), (0, 0)):
        term = lax.dot_general(left[a], right[b], (dims, ((), ())), preferred_element_type=f32)
        total = term if total is None else total + term
    return total


PLAIN, TURNED = ((1,), (0,)), ((1,), (1,))


def prepare_kernel(
    here, layout_own, layout_other, table, matrix_in, bias_in, matrix_out, bias_out, gain, offset, tables, hidden, spans, gains, flat
):
    flat[:PREFIX, :D] = table[...]
    flat[PREFIX:, :D] = jnp.zeros((PAD - PREFIX, D), f32)
    inner = products(split(flat[:, :D]), split(matrix_in[...]), PLAIN) + bias_in[...]
    real = lax.broadcasted_iota(jnp.int32, (PAD, 512), 0) < PREFIX
    hidden[...] = jnp.where(real, jnp.tanh(inner), 0.0)
    parts = split(hidden[...])
    for n in range(6):
        cols = slice(512 * n, 512 * n + 512)
        flat[:, cols] = products(parts, split(matrix_out[:, cols]), PLAIN) + bias_out[:, cols]
    real = lax.broadcasted_iota(jnp.int32, (PAD, 2 * HD), 0) < PREFIX
    for y in range(SIDE):

        @pl.when(here[Y] == y)
        def _():
            for layer in range(LAYERS):
                for h in range(GROUP):
                    at = layer * 2 * D + (GROUP * y + h) * HD
                    both = jnp.concatenate([flat[:, at : at + HD], flat[:, at + D : at + D + HD]], axis=1)
                    tables[layer, h] = jnp.where(real, both, 0.0).astype(bf16)

    lane = lax.broadcasted_iota(jnp.int32, (8, 4 * TOK), 1)
    places = lane + TOK * (lax.div(lane, TOK) + here[CORE])
    own = here[4] == here[CORE]
    end = jnp.int32(0)
    starts = jnp.zeros((8, 4 * TOK), jnp.int32)
    for n in range(8):
        end = end + jnp.where(own, layout_own[n], layout_other[n])
        starts = jnp.where(places >= end, end, starts)
    living = LENGTH - jnp.where(own, layout_own[8], layout_other[8])
    starts = jnp.where(places < living, starts, 4 * LENGTH)
    spans[0:1, :] = starts[0:1, :]
    spans[1:2, :] = places[0:1, :]
    rows = [ref[layer, which : which + 1, :] for layer in range(LAYERS) for which in range(2) for ref in (gain, offset)]
    gains[...] = jnp.concatenate(rows, axis=0).T


def prepare(here, layout_own, layout_other, table, matrix_in, bias_in, matrix_out, bias_out, gain, offset):
    return pl.pallas_call(
        prepare_kernel,
        out_shape=(
            shape(LAYERS, GROUP, PAD, 2 * HD),
            shape(PAD, 512, dtype=f32),
            shape(2, 4 * TOK, dtype=jnp.int32),
            shape(D, 8, dtype=f32),
        ),
        in_specs=[SCALARS] * 3 + in_vmem(7),
        out_specs=tuple(in_vmem(4)),
        scratch_shapes=[pltpu.VMEM((PAD, 2 * LAYERS * D), f32)],
        compiler_params=params(20),
        name="prepare",
    )(here, layout_own, layout_other, table, matrix_in, bias_in[None], matrix_out, bias_out[None], gain, offset)


def chain_kernel(hidden, hidden_t, table_t, matrix_in, matrix_out, parts, g_table, g_in, g_in_bias, g_out, g_out_bias, *scratch):
    grads, new_out, sems = scratch
    chunks = [slice(512 * n, 512 * n + 512) for n in range(6)]
    writes = [pltpu.make_async_copy(new_out.at[:, c], g_out.at[:, c], sems.at[n]) for n, c in enumerate(chunks)]
    grads[...] = jnp.zeros_like(grads)
    for y in range(SIDE):
        total = jnp.zeros((LAYERS * ROWS, 128), f32)
        for z in range(4):
            for xl in range(2):
                for xh in range(2):
                    total = total + parts[((z * 2 + xl) * 4 + y) * 2 + xh].astype(f32)
        for layer in range(LAYERS):
            for h in range(GROUP):
                first_row = ROWS * layer + PREFIX * h
                rows = total[first_row : first_row + PREFIX, :]
                at = layer * 2 * D + (GROUP * y + h) * HD
                grads[:PREFIX, at : at + HD] = rows[:, :HD]
                grads[:PREFIX, at + D : at + D + HD] = rows[:, HD:]
    g_out_bias[...] = jnp.sum(grads[...], axis=0, keepdims=True)
    hidden_parts = split(hidden_t[...])
    some = [split(grads[:, cols]) for cols in chunks]
    for n, cols in enumerate(chunks):
        new_out[:, cols] = products(hidden_parts, some[n], PLAIN)
        writes[n].start()
    slope = jnp.zeros((PAD, 512), f32)
    for n, cols in enumerate(chunks):
        slope = slope + products(some[n], split(matrix_out[:, cols]), TURNED)
    slope = slope * (1.0 - hidden[...] * hidden[...])
    g_in_bias[...] = jnp.sum(slope, axis=0, keepdims=True)
    parts_of_slope = split(slope)
    g_in[...] = products(split(table_t[...]), parts_of_slope, PLAIN)
    g_table[...] = products(parts_of_slope, split(matrix_in[...]), TURNED)[:PREFIX, :]
    finish(writes)


def chain(hidden, table, matrix_in, matrix_out, parts):
    g_table, g_in, g_in_bias, g_out, g_out_bias = pl.pallas_call(
        chain_kernel,
        out_shape=(
            shape(PREFIX, D, dtype=f32),
            shape(D, 512, dtype=f32),
            shape(1, 512, dtype=f32),
            shape(512, 2 * LAYERS * D, dtype=f32),
            shape(1, 2 * LAYERS * D, dtype=f32),
        ),
        in_specs=in_vmem(6),
        out_specs=(*in_vmem(3), *anywhere(1), *in_vmem(1)),
        scratch_shapes=[
            pltpu.VMEM((PAD, 2 * LAYERS * D), f32),
            pltpu.VMEM((512, 2 * LAYERS * D), f32),
            pltpu.SemaphoreType.DMA((6,)),
        ],
        compiler_params=params(32),
        name="chain",
    )(hidden, hidden.T, table.T, matrix_in, matrix_out, parts)
    return g_table, g_in, g_in_bias[0], g_out, g_out_bias[0]


def start_weights(here, attn_weight, out_weight, fc_weight, proj_weight, waits):
    core = here[CORE]
    turned = jnp.swapaxes(proj_weight, 1, 2)
    mine = lax.dynamic_slice_in_dim(turned, 48 * core, 48, axis=1)
    theirs = lax.dynamic_slice_in_dim(turned, 48 * (1 - core), 48, axis=1)
    ao = jnp.concatenate([attn_weight, out_weight], axis=2)
    kept, given = jnp.where(core == 0, ao, fc_weight), jnp.where(core == 0, fc_weight, ao)
    got = move(given, core_pairs())
    pair = jnp.where(core == 0, jnp.stack([kept, got]), jnp.stack([got, kept]))
    got = move(theirs, core_pairs())
    pj = jnp.where(core == 0, jnp.concatenate([mine, got], axis=2), jnp.concatenate([got, mine], axis=2))
    pj = around(pj, Z)
    pair, *pj = assemble(
        here,
        None,
        [
            (around_two(pair, X, Y), shape(2, 4, 48, 768), put_pair_one),
            (pj, shape(48, 1536), put_proj_one(0)),
            (pj, shape(48, 1536), put_proj_one(1)),
        ],
        waits,
    )
    return around_two(pair, Y, Z), around(pj[0], X), around(pj[1], Y)


def both_cores(blocks):
    return [*blocks, *[move(b, core_pairs()) for b in blocks]]


PROJ_WHOLE = shape(2, 48, 3072)


def rest_of_pairs(here, pair, proj, waits):
    pair_whole = shape(4, 48, 3072)
    groups = [(pair, pair_whole, put_pair_two), (proj, PROJ_WHOLE, put_proj_two, True)]
    whole, whole_proj = assemble(here, 0, groups, waits)
    zero = around_two(whole, Z, X)
    near = [whole_proj, move(whole_proj, ring(Y, 1)), move(whole_proj, ring(Y, 3))]
    (whole,) = assemble(here, 1, [(pair, pair_whole, put_pair_two)], tuple(zero[1:]))
    return both_cores(zero), both_cores(around_two(whole, Z, X)), near


def far_of_proj(here, proj, near, waits):
    (whole,) = assemble(here, None, [(proj, PROJ_WHOLE, put_proj_two)], waits)
    own, ahead, behind = near
    return [own, ahead, move(whole, ring(Y, 2)), behind]


def put_on_y(here, k, block, result):
    result[wrap(here[Y] + k)] = block[...]


def put_on_x(here, k, block, result):
    result[wrap(here[X] + k)] = block[...]


def rest_of_proj_one(here, blocks, waits):
    (whole,) = assemble(here, None, [(blocks, shape(4, 48, 1536), put_on_y)], waits)
    return around(whole, X)


def proj_of_both(here, blocks, put, waits):
    (own,) = assemble(here, None, [(blocks, shape(4, *blocks[0].shape), put)], waits)
    return [own, move(own, core_pairs())]


def on_device(
    states_in,
    attn_weight,
    out_weight,
    fc_weight,
    proj_weight,
    norm_gain,
    norm_shift,
    prefix_table,
    reparam_in,
    reparam_in_bias,
    reparam_out,
    reparam_out_bias,
    doc_lengths,
    pad_counts,
    states_grad,
):
    z, xl, core, y, xh = (lax.axis_index(name) for name in AXES)
    here = jnp.stack([z, 2 * xh + xl, core, y, xh]).astype(jnp.int32)
    x = move(states_in[0], seat_pairs())
    grad_in = move(states_grad[0], seat_pairs())
    layout = jnp.concatenate([doc_lengths[0], pad_counts])
    pair, proj, proj_one = start_weights(here, attn_weight, out_weight, fc_weight, proj_weight, ())
    layout_other = move(layout, core_pairs())

    prepared = prepare(
        here,
        layout,
        layout_other,
        prefix_table,
        reparam_in,
        reparam_in_bias,
        reparam_out,
        reparam_out_bias,
        norm_gain,
        norm_shift,
    )
    tables, hidden, spans, gains = prepared
    pair_zero, pair_one, near = rest_of_pairs(here, pair, proj, (*prepared, x, grad_in, *proj_one[1:]))
    table = jnp.pad(prefix_table, ((0, PAD - PREFIX), (0, 0)))
    stream, sends = first(here, x, gains, pair_zero, (spans, tables))
    proj_zero = far_of_proj(here, proj, near, (sends,))
    arrived = [(*pair_one[1:4], *near[1:]), ()]
    streams = [stream]
    kept = []
    for layer in range(LAYERS):
        own = swap_on_ring(sends)
        other = move(own, core_pairs())
        if layer == 0:
            proj_one = rest_of_proj_one(here, proj_one, (own,))
        else:
            proj_one = proj_of_both(here, proj_one, put_on_x, (own,))
        mixed, logs = attend(here, spans, own, other, tables, layer, arrived[layer])
        if layer == 0:
            proj_zero = proj_of_both(here, proj_zero, put_on_y, (mixed,))
        mixed = swap_on_ring(mixed)
        kept.append((own, other, logs))
        if layer == 0:
            middle, before, stream, sends = middle_part(here, stream, gains, mixed, pair_zero, proj_zero, pair_one, ())
            streams.append(stream)
        else:
            final, grad_middle, *sends = last_part(here, stream, gains, mixed, grad_in, pair_one, proj_one)
    final = move(final, seat_pairs())

    tables_back = ()
    for layer in reversed(range(LAYERS)):
        own, other, logs = kept[layer]
        grads = to_places(sends)
        grad_query, mine, theirs, grad_table = attend_back(here, spans, logs, own, other, grads, tables, layer)
        tables_back = (grad_table, move(grad_table, core_pairs()), *tables_back)
        theirs = move(theirs, core_pairs())
        waits = () if layer else (spread_tables(tables_back),)
        back = to_places(pack_back(here, grad_query, mine, theirs, waits))
        if layer == 1:
            grad_middle, *sends = turn_part(
                here, streams[1], gains, grad_middle, before, middle, back, pair_one, pair_zero, proj_zero, (final,)
            )
        else:
            shared = lax.all_to_all(waits[0], ("z", "xl", "y", "xh"), 0, 0, tiled=True)
            prefix_grads = chain(hidden, table, reparam_in, reparam_out, shared)
            grad_states = end_part(here, streams[0], gains, grad_middle, back, pair_zero, (prefix_grads[0],))
    grad_states = move(grad_states, seat_pairs())

    return (final[None], grad_states[None], *prefix_grads)


def solution(mesh):
    grid = Mesh(mesh.devices.reshape(GRID), AXES)
    rows, cols = ("z", "xl", "core"), ("y", "xh")
    return jax.shard_map(
        on_device,
        mesh=grid,
        in_specs=(
            P(rows, cols, None),
            P(None, rows, cols),
            P(None, rows, cols),
            P(None, rows, cols),
            P(None, rows, cols),
            P(),
            P(),
            P(),
            P(),
            P(),
            P(),
            P(),
            P(rows, None),
            P(rows),
            P(rows, cols, None),
        ),
        out_specs=(P(rows, cols, None), P(rows, cols, None), P(), P(), P(), P(), P()),
        check_vma=False,
    )
```

```python
import jax
import jax.numpy as jnp
from jax import lax
from jax.experimental import pallas as pl
from jax.experimental.pallas import tpu as pltpu
from jax.sharding import Mesh
from jax.sharding import PartitionSpec as P

D = 768
H = 12
HD = 64
FF = 3072
LENGTH = 1024
PREFIX = 10
LAYERS = 2
TOK = 128
PAD = 16
GROUP = 3
ROWS = 32
SIDE = 4
AXES = ("z", "xl", "core", "y", "xh")
GRID = (4, 2, 2, 4, 2)

epsilon = 1e-05
highest = lax.Precision.HIGHEST
big_negative = -1e30
bf16 = jnp.bfloat16
f32 = jnp.float32


def index_of(z, x, core, y):
    return (((z * 2 + x % 2) * 2 + core) * 4 + y) * 2 + x // 2


def everywhere():
    return [(z, x, c, y) for z in range(4) for x in range(4) for c in range(2) for y in range(4)]


def ring(axis, ahead):
    pairs = []
    for spot in everywhere():
        source = list(spot)
        source[axis] = (source[axis] + ahead) % 4
        pairs.append((index_of(*source), index_of(*spot)))
    return pairs


def two_rings(axis_zero, axis_one, ahead):
    pairs = []
    for spot in everywhere():
        source = list(spot)
        axis = axis_one if spot[CORE] else axis_zero
        source[axis] = (source[axis] + ahead) % 4
        pairs.append((index_of(*source), index_of(*spot)))
    return pairs


def core_pairs():
    return [(index_of(z, x, 1 - c, y), index_of(z, x, c, y)) for z, x, c, y in everywhere()]


def seat_pairs():
    return [(index_of(z, c * 2 + x % 2, x // 2, y), index_of(z, x, c, y)) for z, x, c, y in everywhere()]


Z, X, CORE, Y = 0, 1, 2, 3


def move(value, pairs):
    return lax.ppermute(value, AXES, pairs)


def around(value, axis):
    return [value] + [move(value, ring(axis, k)) for k in (1, 2, 3)]


def around_two(value, axis_zero, axis_one):
    return [value] + [move(value, two_rings(axis_zero, axis_one, k)) for k in (1, 2, 3)]


def to_places(blocks):
    got = [None, *[move(blocks[k], ring(Y, -k)) for k in (1, 2, 3)]]
    return [blocks[0], got[3], got[2], got[1]]


def swap_on_ring(blocks):
    return lax.all_to_all(blocks, "y", 0, 0, tiled=True)


def wrap(value):
    return lax.rem(value, SIDE)


def params(limit):
    return pltpu.CompilerParams(vmem_limit_bytes=limit * 2**20)


def anywhere(count):
    return [pl.BlockSpec(memory_space=pl.ANY)] * count


def in_vmem(count):
    return [pl.BlockSpec(memory_space=pltpu.VMEM)] * count


SCALARS = pl.BlockSpec(memory_space=pltpu.SMEM)


def shape(*dims, dtype=bf16):
    return jax.ShapeDtypeStruct(dims, dtype)


def lanes(start, size):
    return pl.ds(pl.multiple_of(start, 128), size)


def block_of(layer, dims):
    if layer is None:
        return pl.BlockSpec(dims, lambda i: (0,) * len(dims))
    return pl.BlockSpec((None, *dims[1:]), lambda i: (layer,) + (0,) * (len(dims) - 1))


def assemble(here, layer, groups, waits=()):
    count = len(groups)

    def kernel(here, *refs):
        for n, (_, _, put, *_) in enumerate(groups):
            for k in range(4):
                put(here, k, refs[4 * n + k], refs[n - count])

    blocks = [b for group in groups for b in group[0]]
    outs = [group[1] for group in groups]
    specs = [block_of(None if len(group) > 3 else layer, b.shape) for group in groups for b in group[0]]
    return pl.pallas_call(
        kernel,
        grid=(1,),
        out_shape=outs,
        in_specs=[SCALARS, *specs, *anywhere(len(waits))],
        out_specs=[block_of(None, out.shape) for out in outs],
        compiler_params=params(16),
        name="assemble",
    )(here, *blocks, *waits)


def pick(here, zero, one):
    return jnp.where(here[CORE] == 0, zero, one)


def put_pair_one(here, k, block, result):
    place = wrap(pick(here, here[X], here[Y]) + k)
    low, high = lax.rem(place, 2), lax.div(place, 2)
    for c in range(2):
        row, col = pick(here, 2 * low + c, 2 * c + high), pick(here, high, low)
        result[:, row, :, lanes(384 * col, 384)] = block[c]


def put_pair_two(here, k, block, result):
    place = wrap(pick(here, here[Y], here[Z]) + k)
    for i in range(4):
        result[pick(here, i, place), :, lanes(768 * pick(here, place, i), 768)] = block[i]


def put_proj_one(layer):
    def put(here, k, block, result):
        result[:, lanes(384 * wrap(here[Z] + k), 384)] = block[layer]

    return put


def put_proj_two(here, k, block, result):
    place = wrap(here[X] + k)
    result[lax.div(place, 2), :, lanes(1536 * lax.rem(place, 2), 1536)] = block[...]


AO_HELD = pltpu.VMEM((4, 4, 48, 3072), bf16)
FC_HELD = pltpu.VMEM((2, 4, 2, 2, 48, 1536), bf16)
PJ_HELD = pltpu.VMEM((4, 2, 2, 48, 3072), bf16)


class Chosen:
    def __init__(self, here, zero, one, target, sem):
        self.here = here
        self.copies = [pltpu.make_async_copy(source, target, sem) for source in (zero, one)]

    def start(self):
        for core in range(2):
            pl.when(self.here[CORE] == core)(self.copies[core].start)

    def wait(self):
        self.copies[0].wait()


def fetch_ao(here, refs, held, sems):
    return [Chosen(here, refs[k], refs[4 + k], held.at[wrap(here[Z] + k)], sems.at[k]) for k in range(4)]


def fetch_fc(here, refs, held, sems):
    copies = []
    for k in range(4):
        there = wrap(here[X] + k)
        for c in range(2):
            target = held.at[lax.div(there, 2), :, lax.rem(there, 2), c]
            cols = slice(1536 * c, 1536 * c + 1536)
            copies.append(Chosen(here, refs[4 + k].at[:, :, cols], refs[k].at[:, :, cols], target, sems.at[2 * k + c]))
    return copies


def fetch_pj(here, refs, held, sems):
    cores = (here[CORE], 1 - here[CORE])
    return [pltpu.make_async_copy(refs[n], held.at[:, :, core], sems.at[n]) for n, core in enumerate(cores)]


def fetch_pj_one(here, refs, held, sems):
    copies = []
    for n, core in enumerate((here[CORE], 1 - here[CORE])):
        for x in range(4):
            cols = slice(1536 * (x % 2), 1536 * (x % 2) + 1536)
            copies.append(pltpu.make_async_copy(refs[n].at[x], held.at[:, x // 2, core, :, cols], sems.at[4 * n + x]))
    return copies


def begin(copies):
    for one in copies:
        one.start()


def finish(copies):
    for one in copies:
        one.wait()


def flipped(value):
    return value.astype(f32).T


def norm_stats(stream):
    centre = jnp.mean(stream, axis=0, keepdims=True)
    centred = stream - centre
    spread = jnp.mean(centred * centred, axis=0, keepdims=True)
    return centred, lax.rsqrt(spread + epsilon)


def norm(stream, gain, shift):
    centred, rate = norm_stats(stream)
    return centred * rate * gain + shift


def norm_back(stream, gain, grad):
    centred, rate = norm_stats(stream)
    unit = centred * rate
    scaled = grad * gain
    inner = jnp.mean(scaled * unit, axis=0, keepdims=True)
    return rate * (scaled - jnp.mean(scaled, axis=0, keepdims=True) - unit * inner)


root = 0.7978845608028654


def gate(u):
    return 0.5 * u * (1.0 + jnp.tanh(root * (u + 0.044715 * (u * u * u))))


def gate_slope(u):
    squared = u * u
    t = jnp.tanh(root * (u + 0.044715 * (squared * u)))
    return 0.5 * (1.0 + t) + (0.5 * root) * u * (1.0 - t * t) * (1.0 + (3.0 * 0.044715) * squared)


def column(gains, layer, which, part):
    at = layer * 4 + which * 2 + part
    return gains[:, at : at + 1]


def rows_of_place(place):
    pieces = []
    for t in range(3):
        for u in range(2):
            piece = 8 * t + 2 * place + u
            pieces.append((384 * (piece // 3) + 96 * (piece % 3), t * 192 + u * 96))
    return pieces


def send_qkv(here, stream, gains, layer, held, wide, sends):
    normed = norm(stream, column(gains, layer, 0, 0), column(gains, layer, 0, 1)).T.astype(bf16)
    for j in range(4):
        cols = slice(768 * j, 768 * j + 768)
        packed = jnp.dot(normed, held[:, :, :, cols].reshape(D, 768), preferred_element_type=f32)
        wide[cols, :] = packed.T.astype(bf16)
    for place in range(4):
        for row, at in rows_of_place(place):
            sends[place, at : at + 96, :] = wide[row : row + 96, :]


def first_kernel(here, x_ref, gains, *refs):
    ao, (stream, sends), (held, wide, sems) = refs[0:8], refs[8:10], refs[10:]
    copies = fetch_ao(here, ao, held, sems)
    begin(copies)
    stream[...] = flipped(x_ref[...])
    finish(copies)
    send_qkv(here, stream[...], gains, 0, held, wide, sends)


def first(here, x, gains, ao, waits):
    def kernel(*refs):
        first_kernel(*refs[:11], *refs[11 + len(waits) :])

    return pl.pallas_call(
        kernel,
        out_shape=(shape(D, TOK, dtype=f32), shape(4, 576, TOK)),
        in_specs=[SCALARS, *in_vmem(2), *anywhere(8 + len(waits))],
        out_specs=tuple(in_vmem(2)),
        scratch_shapes=[AO_HELD, pltpu.VMEM((FF, TOK), bf16), pltpu.SemaphoreType.DMA((8,))],
        compiler_params=params(24),
        name="first",
    )(here, x, gains, *ao, *waits)


def after_attention(here, stream, mixed, gains, layer, ao_held, fc_held, pj_held, waits, act, before, middle, result):
    rows = flipped(mixed[...].reshape(D, TOK)).astype(bf16)
    finish(waits[0])

    weight = jnp.concatenate([ao_held[:, :, :, 384 * j + 256 : 384 * j + 384].reshape(D, 128) for j in range(8)], axis=1)
    part = jnp.dot(rows, weight, preferred_element_type=f32).T
    for j in range(8):
        at = slice(96 * j, 96 * j + 96)
        middle[at, :] = stream[at, :] + part[128 * j + 32 : 128 * j + 128, :]
    normed = norm(middle[...], column(gains, layer, 1, 0), column(gains, layer, 1, 1)).T.astype(bf16)
    finish(waits[1])

    for n in range(4):
        low = 768 * (n % 2)
        weight = fc_held[n // 2, :, :, :, :, low : low + 768].reshape(D, 768)
        inputs = jnp.dot(normed, weight, preferred_element_type=f32)
        before[n] = inputs
        act[768 * n : 768 * n + 768, :] = gate(inputs).T.astype(bf16)
    finish(waits[2])
    for n in range(2):
        at = slice(384 * n, 384 * n + 384)
        weight = pj_held[2 * n : 2 * n + 2].reshape(384, FF)
        result[at, :] = middle[at, :] + jnp.dot(weight, act[...], preferred_element_type=f32)


def middle_kernel(here, stream, gains, *refs):
    mixed, pair, pj, pair_next = refs[0], refs[1:9], refs[9:11], refs[11:19]
    middle, before, result, sends = refs[19:23]
    ao_held, fc_held, pj_held, next_held, act, sems = refs[23:]
    waits = [
        fetch_ao(here, pair, ao_held, sems.at[0]),
        fetch_fc(here, pair, fc_held, sems.at[1]),
        fetch_pj(here, pj, pj_held, sems.at[2]),
        fetch_ao(here, pair_next, next_held, sems.at[3]),
    ]
    for copies in waits:
        begin(copies)
    after_attention(here, stream, mixed, gains, 0, ao_held, fc_held, pj_held, waits, act, before, middle, result)
    finish(waits[3])
    send_qkv(here, result[...], gains, 1, next_held, act, sends)


def middle_part(here, stream, gains, mixed, pair, pj, pair_next, waits):
    def kernel(*refs):
        middle_kernel(*refs[:22], *refs[22 + len(waits) :])

    return pl.pallas_call(
        kernel,
        out_shape=(shape(D, TOK, dtype=f32), shape(4, TOK, 768, dtype=f32), shape(D, TOK, dtype=f32), shape(4, 576, TOK)),
        in_specs=[SCALARS, *in_vmem(3), *anywhere(18 + len(waits))],
        out_specs=tuple(in_vmem(4)),
        scratch_shapes=[
            AO_HELD,
            FC_HELD,
            PJ_HELD,
            AO_HELD,
            pltpu.VMEM((FF, TOK), bf16),
            pltpu.SemaphoreType.DMA((4, 8)),
        ],
        compiler_params=params(56),
        name="middle_part",
    )(here, stream, gains, mixed, *pair, *pj, *pair_next, *waits)


def back_feed(here, grad, before, middle, gains, layer, ao_held, fc_held, pj_held, waits, act, spread, grad_middle, sends):
    rows = grad[...].T.astype(bf16)
    finish(waits[2])

    for n in range(4):
        cols = slice(768 * n, 768 * n + 768)
        grad_act = jnp.dot(rows, pj_held[:, :, :, :, cols].reshape(D, 768), preferred_element_type=f32)
        act[cols, :] = (gate_slope(before[n]) * grad_act).T.astype(bf16)
    finish(waits[1])
    for n in range(2):
        low = jnp.dot(fc_held[0, 2 * n : 2 * n + 2].reshape(384, 1536), act[:1536, :], preferred_element_type=f32)
        high = jnp.dot(fc_held[1, 2 * n : 2 * n + 2].reshape(384, 1536), act[1536:, :], preferred_element_type=f32)
        grad_middle[384 * n : 384 * n + 384, :] = low + high
    total = grad[...] + norm_back(middle[...], column(gains, layer, 1, 0), grad_middle[...])
    grad_middle[...] = total
    rounded = total.astype(bf16)
    for j in range(8):
        spread[128 * j : 128 * j + 32, :] = jnp.zeros((32, TOK), bf16)
        spread[128 * j + 32 : 128 * j + 128, :] = rounded[96 * j : 96 * j + 96, :]
    finish(waits[0])

    weight = jnp.concatenate([ao_held[:, :, :, 384 * j + 256 : 384 * j + 384].reshape(D, 128) for j in range(8)], axis=1)
    whole = jnp.dot(weight, spread[...], preferred_element_type=f32).astype(bf16)
    for y in range(4):

        @pl.when(here[Y] == y)
        def _():
            for k in range(4):
                row = 192 * ((y + k) % 4)
                sends[k][...] = whole[row : row + 192, :]


def last_kernel(here, stream, gains, *refs):
    mixed, grad_in, pair, pj = refs[0], refs[1], refs[2:10], refs[10:12]
    final, grad_middle, *sends = refs[12:18]
    ao_held, fc_held, pj_held, act, spread, before, middle, result, sems = refs[18:]
    waits = [
        fetch_ao(here, pair, ao_held, sems.at[0]),
        fetch_fc(here, pair, fc_held, sems.at[1]),
        fetch_pj_one(here, pj, pj_held, sems.at[2]),
    ]
    for copies in waits:
        begin(copies)
    after_attention(here, stream, mixed, gains, 1, ao_held, fc_held, pj_held, waits, act, before, middle, result)
    final[...] = result[...].T
    result[...] = flipped(grad_in[...])
    back_feed(here, result, before, middle, gains, 1, ao_held, fc_held, pj_held, [[], [], []], act, spread, grad_middle, sends)


def last_part(here, stream, gains, mixed, grad_in, pair, pj):
    return pl.pallas_call(
        last_kernel,
        out_shape=(shape(TOK, D, dtype=f32), shape(D, TOK, dtype=f32), *[shape(192, TOK)] * 4),
        in_specs=[SCALARS, *in_vmem(4), *anywhere(10)],
        out_specs=tuple(in_vmem(6)),
        scratch_shapes=[
            AO_HELD,
            FC_HELD,
            PJ_HELD,
            pltpu.VMEM((FF, TOK), bf16),
            pltpu.VMEM((1024, TOK), bf16),
            pltpu.VMEM((4, TOK, 768), f32),
            pltpu.VMEM((D, TOK), f32),
            pltpu.VMEM((D, TOK), f32),
            pltpu.SemaphoreType.DMA((3, 8)),
        ],
        compiler_params=params(40),
        name="last_part",
    )(here, stream, gains, mixed, grad_in, *pair, *pj)


def back_qkv(here, blocks, held, wait, wide, stream, gains, layer, grad_middle, result):
    for j in range(8):
        wide[384 * j + 288 : 384 * j + 384, :] = jnp.zeros((96, TOK), bf16)
    for y in range(4):

        @pl.when(here[Y] == y)
        def _():
            for k in range(4):
                for row, at in rows_of_place((y + k) % 4):
                    wide[row : row + 96, :] = blocks[k][at : at + 96, :]

    finish(wait)

    for n in range(2):
        weight = held[2 * n : 2 * n + 2].reshape(384, 3072)
        result[384 * n : 384 * n + 384, :] = jnp.dot(weight, wide[...], preferred_element_type=f32)
    result[...] = grad_middle[...] + norm_back(stream[...], column(gains, layer, 0, 0), result[...])


def turn_kernel(here, stream, gains, grad_above, before, middle, *refs):
    blocks, pair_above, pair, pj = refs[0:4], refs[4:12], refs[12:20], refs[20:22]
    grad_middle, *sends = refs[22:27]
    above_held, ao_held, fc_held, pj_held, act, spread, grad, sems = refs[27:]
    waits = [
        fetch_ao(here, pair_above, above_held, sems.at[0]),
        fetch_pj(here, pj, pj_held, sems.at[3]),
        fetch_fc(here, pair, fc_held, sems.at[2]),
        fetch_ao(here, pair, ao_held, sems.at[1]),
    ]
    for copies in waits:
        begin(copies)
    back_qkv(here, blocks, above_held, waits[0], act, stream, gains, 1, grad_above, grad)
    back_feed(here, grad, before, middle, gains, 0, ao_held, fc_held, pj_held, [waits[3], waits[2], waits[1]], act, spread, grad_middle, sends)


def turn_part(here, stream, gains, grad_above, before, middle, blocks, pair_above, pair, pj, waits):
    def kernel(*refs):
        turn_kernel(*refs[:28], *refs[28 + len(waits) :])

    return pl.pallas_call(
        kernel,
        out_shape=(shape(D, TOK, dtype=f32), *[shape(192, TOK)] * 4),
        in_specs=[SCALARS, *in_vmem(9), *anywhere(18 + len(waits))],
        out_specs=tuple(in_vmem(5)),
        scratch_shapes=[
            AO_HELD,
            AO_HELD,
            FC_HELD,
            PJ_HELD,
            pltpu.VMEM((FF, TOK), bf16),
            pltpu.VMEM((1024, TOK), bf16),
            pltpu.VMEM((D, TOK), f32),
            pltpu.SemaphoreType.DMA((4, 8)),
        ],
        compiler_params=params(44),
        name="turn_part",
    )(here, stream, gains, grad_above, before, middle, *blocks, *pair_above, *pair, *pj, *waits)


def end_kernel(here, stream, gains, grad_middle, *refs):
    blocks, ao, out, (held, wide, grad, sems) = refs[0:4], refs[4:12], refs[12], refs[13:]
    wait = fetch_ao(here, ao, held, sems)
    begin(wait)
    back_qkv(here, blocks, held, wait, wide, stream, gains, 0, grad_middle, grad)
    out[...] = grad[...].T


def end_part(here, stream, gains, grad_middle, blocks, ao, waits):
    def kernel(*refs):
        end_kernel(*refs[:16], *refs[16 + len(waits) :])

    return pl.pallas_call(
        kernel,
        out_shape=shape(TOK, D, dtype=f32),
        in_specs=[SCALARS, *in_vmem(7), *anywhere(8 + len(waits))],
        out_specs=pl.BlockSpec(memory_space=pltpu.VMEM),
        scratch_shapes=[AO_HELD, pltpu.VMEM((FF, TOK), bf16), pltpu.VMEM((D, TOK), f32), pltpu.SemaphoreType.DMA((8,))],
        compiler_params=params(56),
        name="end_part",
    )(here, stream, gains, grad_middle, *blocks, *ao, *waits)


HALF = 256
every = slice(None)
EVERY_PIECE = [slice(TOK * n, TOK * n + TOK) for n in range(8)] + [slice(LENGTH, LENGTH + PAD)]
SEEN = ((0, 1, 4, 5, 8), (0, 1, 2, 3, 4, 5, 6, 7, 8))


def hide(here, spans, hidden):
    inside = lax.broadcasted_iota(jnp.int32, (TOK, HALF), 0)
    for part in range(2):
        cols = slice(part * HALF, part * HALF + HALF)
        low, high = spans[0:1, cols], spans[1:2, cols]
        for n in SEEN[part][:-1]:
            start = TOK * (2 * (n % 4) + (here[CORE] if n < 4 else 1 - here[CORE]))
            seen = (inside >= low - start) & (inside <= high - start)
            hidden[EVERY_PIECE[n], cols] = jnp.where(seen, 0.0, big_negative)
    real = lax.broadcasted_iota(jnp.int32, (PAD, 2 * HALF), 0) < PREFIX
    hidden[LENGTH:, :] = jnp.where(real, 0.0, big_negative)


def head_rows(held, n, t, h):
    return held[n // 4][n % 4, 192 * t + 64 * h : 192 * t + 64 * h + 64, :]


def keys_and_values(held, table, h):
    tall = []
    for n in range(8):
        both = jnp.concatenate([head_rows(held, n, 1, h), head_rows(held, n, 2, h)], axis=0)
        tall.append(both.astype(f32).T.astype(bf16))
    return [*tall, table[h]]


def turned_table(table):
    return [table[h].astype(f32).T.astype(bf16) for h in range(GROUP)]


def side_by_side(held, pieces, t, h):
    return jnp.concatenate([head_rows(held, n, t, h) for n in pieces], axis=1)


def stacked_rows(ref, pieces, cols):
    return jnp.concatenate([ref[EVERY_PIECE[n], cols] for n in pieces], axis=0)


def attend_kernel(here, spans, *refs):
    held, table, out, logs = refs[0:2], refs[2], refs[3], refs[4]
    hidden, scores, probs = refs[5:]
    table_t = turned_table(table)
    hide(here, spans, hidden)
    for h in range(GROUP):
        tall = keys_and_values(held, table, h)
        for part in range(2):
            cols = slice(part * HALF, part * HALF + HALF)
            pieces = SEEN[part]
            query = side_by_side(held, (2 * part, 2 * part + 1), 0, h) * bf16(0.125)
            right = jnp.concatenate([query, jnp.zeros_like(query)], axis=0)
            top = jnp.full((8, HALF), big_negative, f32)
            for n in pieces:
                block = jnp.dot(tall[n], right, preferred_element_type=f32) + hidden[EVERY_PIECE[n], cols]
                scores[EVERY_PIECE[n], :] = block
                top = jnp.maximum(top, jnp.max(block.reshape(-1, 8, HALF), axis=0))
            top = jnp.max(top, axis=0, keepdims=True)
            total = jnp.zeros((8, HALF), f32)
            for n in pieces:
                block = jnp.exp(scores[EVERY_PIECE[n], :] - top)
                scores[EVERY_PIECE[n], :] = block
                total = total + jnp.sum(block.reshape(-1, 8, HALF), axis=0)
            total = jnp.sum(total, axis=0, keepdims=True)
            share = 1.0 / total
            for n in pieces:
                probs[EVERY_PIECE[n], :] = (scores[EVERY_PIECE[n], :] * share).astype(bf16)
            result = jnp.dot(
                side_by_side(held, pieces[:-1], 2, h), stacked_rows(probs, pieces[:-1], every), preferred_element_type=f32
            )
            result = result + jnp.dot(table_t[h][64:, :], probs[LENGTH:, :], preferred_element_type=f32)
            for n in range(2):
                out[2 * part + n, 64 * h : 64 * h + 64, :] = result[:, TOK * n : TOK * n + TOK].astype(bf16)
            logs[h : h + 1, cols] = top + jnp.log(total)


def attend(here, spans, own, other, tables, layer, waits=()):
    def kernel(*refs):
        attend_kernel(*refs[:4], refs[4].at[layer], *refs[5 + len(waits) :])

    return pl.pallas_call(
        kernel,
        out_shape=(shape(4, 192, TOK), shape(8, 512, dtype=f32)),
        in_specs=[SCALARS, *in_vmem(4), *anywhere(len(waits))],
        out_specs=tuple(in_vmem(2)),
        scratch_shapes=[
            pltpu.VMEM((LENGTH + PAD, 2 * HALF), f32),
            pltpu.VMEM((LENGTH + PAD, HALF), f32),
            pltpu.VMEM((LENGTH + PAD, HALF), bf16),
        ],
        compiler_params=params(20),
        name="attend",
    )(here, spans, own, other, tables, *waits)


def attend_back_kernel(here, spans, logs, *refs):
    held, blocks, table = refs[0:2], refs[2:6], refs[6]
    grad_query, mine, others, grad_table = refs[7:11]
    hidden, probs, slopes, packed, sums, grads = refs[11:]
    table_t = turned_table(table)
    for y in range(4):

        @pl.when(here[Y] == y)
        def _():
            for k in range(4):
                grads[(y + k) % 4] = blocks[k][...]

    hide(here, spans, hidden)
    for h in range(GROUP):
        tall = keys_and_values(held, table, h)
        for part in (1, 0):
            cols = slice(part * HALF, part * HALF + HALF)
            pieces = SEEN[part]
            query = side_by_side(held, (2 * part, 2 * part + 1), 0, h) * bf16(0.125)
            grad = jnp.concatenate([grads[2 * part + n, 64 * h : 64 * h + 64, :] for n in range(2)], axis=1)
            nothing = jnp.zeros_like(query)
            right = jnp.concatenate(
                [jnp.concatenate([query, nothing], axis=1), jnp.concatenate([nothing, grad], axis=1)], axis=0
            )
            right_t = right.astype(f32).T.astype(bf16)
            log_total = logs[h : h + 1, cols]
            inner = jnp.zeros((8, HALF), f32)
            for n in pieces:
                piece = EVERY_PIECE[n]
                both = jnp.dot(tall[n], right, preferred_element_type=f32)
                prob = jnp.exp(both[:, :HALF] + hidden[piece, cols] - log_total)
                slope = both[:, HALF:]
                probs[piece, :] = prob
                slopes[piece, :] = slope
                packed[piece, HALF:] = prob.astype(bf16)
                inner = inner + jnp.sum((prob * slope).reshape(-1, 8, HALF), axis=0)
            inner = jnp.sum(inner, axis=0, keepdims=True)
            for n in pieces:
                piece = EVERY_PIECE[n]
                packed[piece, :HALF] = (probs[piece, :] * (slopes[piece, :] - inner)).astype(bf16)
            result = jnp.dot(
                side_by_side(held, pieces[:-1], 1, h),
                stacked_rows(packed, pieces[:-1], slice(0, HALF)),
                preferred_element_type=f32,
            )
            result = result + jnp.dot(table_t[h][:64, :], packed[LENGTH:, :HALF], preferred_element_type=f32)
            grad_query[64 * h : 64 * h + 64, cols] = (result * 0.125).astype(bf16)
            for n in pieces:
                new = jnp.dot(packed[EVERY_PIECE[n], :], right_t, preferred_element_type=f32)
                sums[EVERY_PIECE[n], :] = new if part == 1 else sums[EVERY_PIECE[n], :] + new
        for n in range(4):
            mine[h, :, TOK * n : TOK * n + TOK] = sums[EVERY_PIECE[n], :].T
            others[h, :, TOK * n : TOK * n + TOK] = sums[EVERY_PIECE[4 + n], :].T.astype(bf16)
        grad_table[PREFIX * h : PREFIX * h + PREFIX, :] = sums[LENGTH : LENGTH + PREFIX, :]
    grad_table[GROUP * PREFIX :, :] = jnp.zeros((ROWS - GROUP * PREFIX, 128), f32)


def attend_back(here, spans, logs, own, other, grads, tables, layer):
    def kernel(*refs):
        attend_back_kernel(*refs[:9], refs[9].at[layer], *refs[10:])

    return pl.pallas_call(
        kernel,
        out_shape=(
            shape(192, 512),
            shape(GROUP, 128, 512, dtype=f32),
            shape(GROUP, 128, 512),
            shape(ROWS, 128, dtype=f32),
        ),
        in_specs=[SCALARS, *in_vmem(9)],
        out_specs=tuple(in_vmem(4)),
        scratch_shapes=[
            pltpu.VMEM((LENGTH + PAD, 2 * HALF), f32),
            pltpu.VMEM((LENGTH + PAD, HALF), f32),
            pltpu.VMEM((LENGTH + PAD, HALF), f32),
            pltpu.VMEM((LENGTH + PAD, 2 * HALF), bf16),
            pltpu.VMEM((LENGTH + PAD, 128), f32),
            pltpu.VMEM((4, 192, TOK), bf16),
        ],
        compiler_params=params(24),
        name="attend_back",
    )(here, spans, logs, own, other, *grads, tables)


def pack_back_kernel(here, grad_query, mine, got, *refs):
    outs = refs[-4:]
    for y in range(4):

        @pl.when(here[Y] == y)
        def _():
            for k in range(4):
                start = TOK * ((y + k) % 4)
                cols = slice(start, start + TOK)
                outs[k][0:192, :] = grad_query[:, cols]
                for h in range(GROUP):
                    both = (mine[h, :, cols] + got[h, :, cols].astype(f32)).astype(bf16)
                    outs[k][192 + 64 * h : 256 + 64 * h, :] = both[:64, :]
                    outs[k][384 + 64 * h : 448 + 64 * h, :] = both[64:, :]


def pack_back(here, grad_query, mine, got, waits):
    def kernel(*refs):
        pack_back_kernel(*refs[:4], *refs[-4:])

    return pl.pallas_call(
        kernel,
        out_shape=tuple([shape(576, TOK)] * 4),
        in_specs=[SCALARS, *in_vmem(3), *anywhere(len(waits))],
        out_specs=tuple(in_vmem(4)),
        compiler_params=params(16),
        name="pack_back",
    )(here, grad_query, mine, got, *waits)


def spread_kernel(*refs):
    tables, spread = refs[: 2 * LAYERS], refs[-1]
    whole = jnp.concatenate([tables[2 * n][...] + tables[2 * n + 1][...] for n in range(LAYERS)], axis=0).astype(bf16)
    for n in range(64):
        spread[n] = whole


def spread_tables(tables):
    return pl.pallas_call(
        spread_kernel,
        out_shape=shape(64, LAYERS * ROWS, 128),
        in_specs=in_vmem(2 * LAYERS),
        out_specs=pl.BlockSpec(memory_space=pltpu.VMEM),
        compiler_params=params(8),
        name="spread_tables",
    )(*tables)


def split(value):
    high = value.astype(bf16)
    return high, (value - high.astype(f32)).astype(bf16)


def products(left, right, dims):
    total = None
    for a, b in ((1, 0), (0, 1), (0, 0)):
        term = lax.dot_general(left[a], right[b], (dims, ((), ())), preferred_element_type=f32)
        total = term if total is None else total + term
    return total


PLAIN, TURNED = ((1,), (0,)), ((1,), (1,))


def prepare_kernel(
    here, layout_own, layout_other, table, matrix_in, bias_in, matrix_out, bias_out, gain, offset, tables, hidden, spans, gains, flat
):
    flat[:PREFIX, :D] = table[...]
    flat[PREFIX:, :D] = jnp.zeros((PAD - PREFIX, D), f32)
    inner = products(split(flat[:, :D]), split(matrix_in[...]), PLAIN) + bias_in[...]
    real = lax.broadcasted_iota(jnp.int32, (PAD, 512), 0) < PREFIX
    hidden[...] = jnp.where(real, jnp.tanh(inner), 0.0)
    parts = split(hidden[...])
    for n in range(6):
        cols = slice(512 * n, 512 * n + 512)
        flat[:, cols] = products(parts, split(matrix_out[:, cols]), PLAIN) + bias_out[:, cols]
    real = lax.broadcasted_iota(jnp.int32, (PAD, 2 * HD), 0) < PREFIX
    for y in range(SIDE):

        @pl.when(here[Y] == y)
        def _():
            for layer in range(LAYERS):
                for h in range(GROUP):
                    at = layer * 2 * D + (GROUP * y + h) * HD
                    both = jnp.concatenate([flat[:, at : at + HD], flat[:, at + D : at + D + HD]], axis=1)
                    tables[layer, h] = jnp.where(real, both, 0.0).astype(bf16)

    lane = lax.broadcasted_iota(jnp.int32, (8, 4 * TOK), 1)
    places = lane + TOK * (lax.div(lane, TOK) + here[CORE])
    own = here[4] == here[CORE]
    end = jnp.int32(0)
    starts = jnp.zeros((8, 4 * TOK), jnp.int32)
    for n in range(8):
        end = end + jnp.where(own, layout_own[n], layout_other[n])
        starts = jnp.where(places >= end, end, starts)
    living = LENGTH - jnp.where(own, layout_own[8], layout_other[8])
    starts = jnp.where(places < living, starts, 4 * LENGTH)
    spans[0:1, :] = starts[0:1, :]
    spans[1:2, :] = places[0:1, :]
    rows = [ref[layer, which : which + 1, :] for layer in range(LAYERS) for which in range(2) for ref in (gain, offset)]
    gains[...] = jnp.concatenate(rows, axis=0).T


def prepare(here, layout_own, layout_other, table, matrix_in, bias_in, matrix_out, bias_out, gain, offset):
    return pl.pallas_call(
        prepare_kernel,
        out_shape=(
            shape(LAYERS, GROUP, PAD, 2 * HD),
            shape(PAD, 512, dtype=f32),
            shape(2, 4 * TOK, dtype=jnp.int32),
            shape(D, 8, dtype=f32),
        ),
        in_specs=[SCALARS] * 3 + in_vmem(7),
        out_specs=tuple(in_vmem(4)),
        scratch_shapes=[pltpu.VMEM((PAD, 2 * LAYERS * D), f32)],
        compiler_params=params(20),
        name="prepare",
    )(here, layout_own, layout_other, table, matrix_in, bias_in[None], matrix_out, bias_out[None], gain, offset)


def chain_kernel(hidden, hidden_t, table_t, matrix_in, matrix_out, parts, g_table, g_in, g_in_bias, g_out, g_out_bias, *scratch):
    grads, new_out, sems = scratch
    chunks = [slice(512 * n, 512 * n + 512) for n in range(6)]
    writes = [pltpu.make_async_copy(new_out.at[:, c], g_out.at[:, c], sems.at[n]) for n, c in enumerate(chunks)]
    grads[...] = jnp.zeros_like(grads)
    for y in range(SIDE):
        total = jnp.zeros((LAYERS * ROWS, 128), f32)
        for z in range(4):
            for xl in range(2):
                for xh in range(2):
                    total = total + parts[((z * 2 + xl) * 4 + y) * 2 + xh].astype(f32)
        for layer in range(LAYERS):
            for h in range(GROUP):
                first_row = ROWS * layer + PREFIX * h
                rows = total[first_row : first_row + PREFIX, :]
                at = layer * 2 * D + (GROUP * y + h) * HD
                grads[:PREFIX, at : at + HD] = rows[:, :HD]
                grads[:PREFIX, at + D : at + D + HD] = rows[:, HD:]
    g_out_bias[...] = jnp.sum(grads[...], axis=0, keepdims=True)
    hidden_parts = split(hidden_t[...])
    some = [split(grads[:, cols]) for cols in chunks]
    for n, cols in enumerate(chunks):
        new_out[:, cols] = products(hidden_parts, some[n], PLAIN)
        writes[n].start()
    slope = jnp.zeros((PAD, 512), f32)
    for n, cols in enumerate(chunks):
        slope = slope + products(some[n], split(matrix_out[:, cols]), TURNED)
    slope = slope * (1.0 - hidden[...] * hidden[...])
    g_in_bias[...] = jnp.sum(slope, axis=0, keepdims=True)
    parts_of_slope = split(slope)
    g_in[...] = products(split(table_t[...]), parts_of_slope, PLAIN)
    g_table[...] = products(parts_of_slope, split(matrix_in[...]), TURNED)[:PREFIX, :]
    finish(writes)


def chain(hidden, table, matrix_in, matrix_out, parts):
    g_table, g_in, g_in_bias, g_out, g_out_bias = pl.pallas_call(
        chain_kernel,
        out_shape=(
            shape(PREFIX, D, dtype=f32),
            shape(D, 512, dtype=f32),
            shape(1, 512, dtype=f32),
            shape(512, 2 * LAYERS * D, dtype=f32),
            shape(1, 2 * LAYERS * D, dtype=f32),
        ),
        in_specs=in_vmem(6),
        out_specs=(*in_vmem(3), *anywhere(1), *in_vmem(1)),
        scratch_shapes=[
            pltpu.VMEM((PAD, 2 * LAYERS * D), f32),
            pltpu.VMEM((512, 2 * LAYERS * D), f32),
            pltpu.SemaphoreType.DMA((6,)),
        ],
        compiler_params=params(32),
        name="chain",
    )(hidden, hidden.T, table.T, matrix_in, matrix_out, parts)
    return g_table, g_in, g_in_bias[0], g_out, g_out_bias[0]


def start_weights(here, attn_weight, out_weight, fc_weight, proj_weight, waits):
    core = here[CORE]
    turned = jnp.swapaxes(proj_weight, 1, 2)
    mine = lax.dynamic_slice_in_dim(turned, 48 * core, 48, axis=1)
    theirs = lax.dynamic_slice_in_dim(turned, 48 * (1 - core), 48, axis=1)
    ao = jnp.concatenate([attn_weight, out_weight], axis=2)
    kept, given = jnp.where(core == 0, ao, fc_weight), jnp.where(core == 0, fc_weight, ao)
    got = move(given, core_pairs())
    pair = jnp.where(core == 0, jnp.stack([kept, got]), jnp.stack([got, kept]))
    got = move(theirs, core_pairs())
    pj = jnp.where(core == 0, jnp.concatenate([mine, got], axis=2), jnp.concatenate([got, mine], axis=2))
    pj = around(pj, Z)
    pair, *pj = assemble(
        here,
        None,
        [
            (around_two(pair, X, Y), shape(2, 4, 48, 768), put_pair_one),
            (pj, shape(48, 1536), put_proj_one(0)),
            (pj, shape(48, 1536), put_proj_one(1)),
        ],
        waits,
    )
    return around_two(pair, Y, Z), around(pj[0], X), around(pj[1], Y)


def both_cores(blocks):
    return [*blocks, *[move(b, core_pairs()) for b in blocks]]


PROJ_WHOLE = shape(2, 48, 3072)


def rest_of_pairs(here, pair, proj, waits):
    pair_whole = shape(4, 48, 3072)
    groups = [(pair, pair_whole, put_pair_two), (proj, PROJ_WHOLE, put_proj_two, True)]
    whole, whole_proj = assemble(here, 0, groups, waits)
    zero = around_two(whole, Z, X)
    near = [whole_proj, move(whole_proj, ring(Y, 1)), move(whole_proj, ring(Y, 3))]
    (whole,) = assemble(here, 1, [(pair, pair_whole, put_pair_two)], tuple(zero[1:]))
    return both_cores(zero), both_cores(around_two(whole, Z, X)), near


def far_of_proj(here, proj, near, waits):
    (whole,) = assemble(here, None, [(proj, PROJ_WHOLE, put_proj_two)], waits)
    own, ahead, behind = near
    return [own, ahead, move(whole, ring(Y, 2)), behind]


def put_on_y(here, k, block, result):
    result[wrap(here[Y] + k)] = block[...]


def put_on_x(here, k, block, result):
    result[wrap(here[X] + k)] = block[...]


def rest_of_proj_one(here, blocks, waits):
    (whole,) = assemble(here, None, [(blocks, shape(4, 48, 1536), put_on_y)], waits)
    return around(whole, X)


def proj_of_both(here, blocks, put, waits):
    (own,) = assemble(here, None, [(blocks, shape(4, *blocks[0].shape), put)], waits)
    return [own, move(own, core_pairs())]


def on_device(
    states_in,
    attn_weight,
    out_weight,
    fc_weight,
    proj_weight,
    norm_gain,
    norm_shift,
    prefix_table,
    reparam_in,
    reparam_in_bias,
    reparam_out,
    reparam_out_bias,
    doc_lengths,
    pad_counts,
    states_grad,
):
    z, xl, core, y, xh = (lax.axis_index(name) for name in AXES)
    here = jnp.stack([z, 2 * xh + xl, core, y, xh]).astype(jnp.int32)
    x = move(states_in[0], seat_pairs())
    grad_in = move(states_grad[0], seat_pairs())
    layout = jnp.concatenate([doc_lengths[0], pad_counts])
    pair, proj, proj_one = start_weights(here, attn_weight, out_weight, fc_weight, proj_weight, ())
    layout_other = move(layout, core_pairs())

    prepared = prepare(
        here,
        layout,
        layout_other,
        prefix_table,
        reparam_in,
        reparam_in_bias,
        reparam_out,
        reparam_out_bias,
        norm_gain,
        norm_shift,
    )
    tables, hidden, spans, gains = prepared
    pair_zero, pair_one, near = rest_of_pairs(here, pair, proj, (x, grad_in, *proj_one[1:]))
    table = jnp.pad(prefix_table, ((0, PAD - PREFIX), (0, 0)))
    stream, sends = first(here, x, gains, pair_zero, (spans, tables))
    proj_zero = far_of_proj(here, proj, near, (sends,))
    arrived = [(*pair_one[1:4], *near[1:]), ()]
    streams = [stream]
    kept = []
    for layer in range(LAYERS):
        own = swap_on_ring(sends)
        other = move(own, core_pairs())
        if layer == 0:
            proj_one = rest_of_proj_one(here, proj_one, (own,))
        else:
            proj_one = proj_of_both(here, proj_one, put_on_x, (own,))
        mixed, logs = attend(here, spans, own, other, tables, layer, arrived[layer])
        if layer == 0:
            proj_zero = proj_of_both(here, proj_zero, put_on_y, (mixed,))
        mixed = swap_on_ring(mixed)
        kept.append((own, other, logs))
        if layer == 0:
            middle, before, stream, sends = middle_part(here, stream, gains, mixed, pair_zero, proj_zero, pair_one, ())
            streams.append(stream)
        else:
            final, grad_middle, *sends = last_part(here, stream, gains, mixed, grad_in, pair_one, proj_one)
    final = move(final, seat_pairs())

    tables_back = ()
    for layer in reversed(range(LAYERS)):
        own, other, logs = kept[layer]
        grads = to_places(sends)
        grad_query, mine, theirs, grad_table = attend_back(here, spans, logs, own, other, grads, tables, layer)
        tables_back = (grad_table, move(grad_table, core_pairs()), *tables_back)
        theirs = move(theirs, core_pairs())
        waits = () if layer else (spread_tables(tables_back),)
        back = to_places(pack_back(here, grad_query, mine, theirs, waits))
        if layer == 1:
            grad_middle, *sends = turn_part(
                here, streams[1], gains, grad_middle, before, middle, back, pair_one, pair_zero, proj_zero, (final,)
            )
        else:
            shared = lax.all_to_all(waits[0], ("z", "xl", "y", "xh"), 0, 0, tiled=True)
            prefix_grads = chain(hidden, table, reparam_in, reparam_out, shared)
            grad_states = end_part(here, streams[0], gains, grad_middle, back, pair_zero, (prefix_grads[0],))
    grad_states = move(grad_states, seat_pairs())

    return (final[None], grad_states[None], *prefix_grads)


def solution(mesh):
    grid = Mesh(mesh.devices.reshape(GRID), AXES)
    rows, cols = ("z", "xl", "core"), ("y", "xh")
    return jax.shard_map(
        on_device,
        mesh=grid,
        in_specs=(
            P(rows, cols, None),
            P(None, rows, cols),
            P(None, rows, cols),
            P(None, rows, cols),
            P(None, rows, cols),
            P(),
            P(),
            P(),
            P(),
            P(),
            P(),
            P(),
            P(rows, None),
            P(rows),
            P(rows, cols, None),
        ),
        out_specs=(P(rows, cols, None), P(rows, cols, None), P(), P(), P(), P(), P()),
        check_vma=False,
    )
```
